32 devices in a mesh: dp: 8 (over z, y), mp: 4 (over x, core).
Axes of the slice: x: 2, y: 2, z: 4, core: 2. Of those that a mesh axis runs over, the one named last changes fastest.
Arguments:
- frames: bfloat16 [5888, 768], P(('dp', 'mp')), may hold values from -6 to 6
- span_mask: int32 [5888], P(('dp', 'mp')), may hold values from 0 to 1, as said below
- mask_vector: bfloat16 [768], replicated, may hold values from -6 to 6
- w_query: bfloat16 [2, 768, 768], P(None, None, 'mp'), may hold values from -0.21875 to 0.21875
- b_query: bfloat16 [2, 768], P(None, 'mp'), may hold values from -3 to 3
- w_key: bfloat16 [2, 768, 768], P(None, None, 'mp'), may hold values from -0.21875 to 0.21875
- w_value: bfloat16 [2, 768, 768], P(None, None, 'mp'), may hold values from -0.21875 to 0.21875
- b_value: bfloat16 [2, 768], P(None, 'mp'), may hold values from -3 to 3
- w_out: bfloat16 [2, 768, 768], P(None, 'mp'), may hold values from -0.75 to 0.75
- b_out: bfloat16 [2, 768], replicated, may hold values from -2 to 2
- attn_gain: bfloat16 [2, 768], replicated, may hold values from 0.099609375 to 1.8984375
- attn_bias: bfloat16 [2, 768], replicated, may hold values from -2 to 2
- w_up: bfloat16 [2, 768, 3072], P(None, None, 'mp'), may hold values from -0.21875 to 0.21875
- b_up: bfloat16 [2, 3072], P(None, 'mp'), may hold values from -3 to 3
- w_down: bfloat16 [2, 3072, 768], P(None, 'mp'), may hold values from -0.109375 to 0.109375
- b_down: bfloat16 [2, 768], replicated, may hold values from -2 to 2
- ffn_gain: bfloat16 [2, 768], replicated, may hold values from 0.099609375 to 1.8984375
- ffn_bias: bfloat16 [2, 768], replicated, may hold values from -2 to 2
- out_grad: bfloat16 [5888, 768], P(('dp', 'mp'))
Outputs:
- hidden_out: bfloat16 [5888, 768], P(('dp', 'mp'))
- frames_grad: float32 [5888, 768], P(('dp', 'mp'))
- mask_vector_grad: float32 [768], replicated
- w_query_grad: float32 [2, 768, 768], P(None, None, 'mp')
- b_query_grad: float32 [2, 768], P(None, 'mp')
- w_key_grad: float32 [2, 768, 768], P(None, None, 'mp')
- w_value_grad: float32 [2, 768, 768], P(None, None, 'mp')
- b_value_grad: float32 [2, 768], P(None, 'mp')
- w_out_grad: float32 [2, 768, 768], P(None, 'mp')
- b_out_grad: float32 [2, 768], replicated
- attn_gain_grad: float32 [2, 768], replicated
- attn_bias_grad: float32 [2, 768], replicated
- w_up_grad: float32 [2, 768, 3072], P(None, None, 'mp')
- b_up_grad: float32 [2, 3072], P(None, 'mp')
- w_down_grad: float32 [2, 3072, 768], P(None, 'mp')
- b_down_grad: float32 [2, 768], replicated
- ffn_gain_grad: float32 [2, 768], replicated
- ffn_bias_grad: float32 [2, 768], replicated
The draws below stay inside these ranges and needn't reach their ends.
Inputs may be any that keep to these rules, and one draw needn't show every extreme that they name: `span_mask`: in each clip of 368 frames, masked frames come in aligned spans of 8, and 30 to 60 percent of the frames are masked.
All inputs are finite; a program needn't handle non-finite values.
Results may differ from the reference program's by a relative error of at most 0.017.
Values may be sent and summed in bfloat16 or wider, within the bound.
No kernel may reach another device: no remote copies, remote signals or barrier semaphores. Data moves between devices by JAX's collectives and lax.ppermute only.
A program may use at most 128 MiB of HBM per device.

```python
import math
import jax
import jax.numpy as jnp
from jax import lax

D = 768
HEADS = 12
HEAD_DIM = 64
FF = 3072
CLIP = 368
LAYERS = 2
CLIPS = 16
TOKENS = 5888


def draw_span_mask(key, part):
    key = jax.random.fold_in(key, 11)
    pieces = CLIP // 8
    count_key, order_key = jax.random.split(key)
    counts = jax.random.randint(count_key, (CLIPS, 1), pieces * 3 // 10 + 1, pieces * 6 // 10 + 1)
    orders = jax.vmap(lambda single: jax.random.permutation(single, pieces))(jax.random.split(order_key, CLIPS))
    marked = (orders < counts).astype(jnp.int32)
    return jnp.repeat(marked, 8, axis=1).reshape(TOKENS)


def draw_out_grad(key, part):
    key = jax.random.fold_in(key, 12)
    pick_key, value_key = jax.random.split(key)
    heavy_count = max(CLIPS // 16, 1)
    ranks = jax.random.permutation(pick_key, CLIPS)
    clip_scale = jnp.where(ranks < heavy_count, 6.0, 1.0).astype(jnp.float32)
    values = jnp.clip(jax.random.normal(value_key, (CLIPS, CLIP, D), jnp.float32), -6.0, 6.0)
    values = values * clip_scale[:, None, None]
    return values.reshape(TOKENS, D).astype(jnp.bfloat16)


def shard_levels(rng, shape, cuts, least, top_value):
    def one(axis_at, parts):
        draws = jax.random.uniform(jax.random.fold_in(jax.random.fold_in(rng, 6), axis_at), (parts,), jnp.float32, least / len(cuts), top_value / len(cuts))
        return jnp.repeat(jnp.exp(draws), shape[axis_at] // parts).reshape((-1,) + (1,) * (len(shape) - axis_at - 1))

    factor_of = one(*cuts[0])
    for cut in cuts[1:]:
        factor_of = factor_of * one(*cut)
    return factor_of


def scatter_about(own_key, shape, scale, bound, cuts=(), held_as=jnp.bfloat16):
    array = scale * jax.random.normal(own_key, shape, jnp.float32)
    if cuts:
        array = array * shard_levels(own_key, shape, cuts, -0.22, 0.18)
    return jnp.clip(array, -bound, bound).astype(held_as)


def setup_inputs(seed: int = 0) -> dict:
    streams_of = jax.random.split(jax.random.key(seed), 20)
    return {
        "frames": scatter_about(streams_of[0], (TOKENS, D), 1.0, 6.0, ((0, 32),)),
        "span_mask": draw_span_mask(jax.random.fold_in(streams_of[19], 71), 0),
        "mask_vector": scatter_about(streams_of[2], (D,), 1.0, 6.0),
        "w_query": scatter_about(streams_of[3], (LAYERS, D, D), D ** -0.5, 0.21875, ((2, 4),)),
        "b_query": scatter_about(streams_of[4], (LAYERS, D), 0.5, 3.0, ((1, 4),)),
        "w_key": scatter_about(streams_of[5], (LAYERS, D, D), D ** -0.5, 0.21875, ((2, 4),)),
        "w_value": scatter_about(streams_of[6], (LAYERS, D, D), D ** -0.5, 0.21875, ((2, 4),)),
        "b_value": scatter_about(streams_of[7], (LAYERS, D), 0.5, 3.0, ((1, 4),)),
        "w_out": scatter_about(streams_of[8], (LAYERS, D, D), (max(D * 32 // CLIP, 1)) ** -0.5, 0.75, ((1, 4),)),
        "b_out": scatter_about(streams_of[9], (LAYERS, D), 0.3, 2.0),
        "attn_gain": jnp.clip(1.0 + 0.18 * jax.random.normal(streams_of[10], (LAYERS, D), jnp.float32), 0.099609375, 1.8984375).astype(jnp.bfloat16),
        "attn_bias": scatter_about(streams_of[11], (LAYERS, D), 0.3, 2.0),
        "w_up": scatter_about(streams_of[12], (LAYERS, D, FF), D ** -0.5, 0.21875, ((2, 4),)),
        "b_up": scatter_about(streams_of[13], (LAYERS, FF), 0.5, 3.0, ((1, 4),)),
        "w_down": scatter_about(streams_of[14], (LAYERS, FF, D), FF ** -0.5, 0.109375, ((1, 4),)),
        "b_down": scatter_about(streams_of[15], (LAYERS, D), 0.3, 2.0),
        "ffn_gain": jnp.clip(1.0 + 0.18 * jax.random.normal(streams_of[16], (LAYERS, D), jnp.float32), 0.099609375, 1.8984375).astype(jnp.bfloat16),
        "ffn_bias": scatter_about(streams_of[17], (LAYERS, D), 0.3, 2.0),
        "out_grad": draw_out_grad(jax.random.fold_in(streams_of[19], 71), 0),
    }


@jax.custom_vjp
def low(v):
    return lax.optimization_barrier(v.astype(jnp.bfloat16)).astype(jnp.float32)

@jax.custom_vjp
def low_back(v):
    return v

def low_keep(v):
    return (low(v), None)

def low_pass(kept, grad):
    return (grad,)

def back_keep(v):
    return (v, None)

def back_low(kept, grad):
    return (low(grad),)
low.defvjp(low_keep, low_pass)
low_back.defvjp(back_keep, back_low)

def matmul(left_mat, right_mat):
    return jnp.dot(left_mat, right_mat, precision=lax.Precision.HIGHEST, preferred_element_type=jnp.float32)

def gelu_exact(values):
    return 0.5 * values * (1.0 + jax.scipy.special.erf(values * 0.7071067811865476))

def layer_norm(resid, gain_vec, bias_vec):
    row_mean = lax.optimization_barrier(jnp.mean(resid, axis=-1, keepdims=True))
    centered = resid - row_mean
    row_var = lax.optimization_barrier(jnp.mean(centered * centered, axis=-1, keepdims=True))
    return centered * lax.rsqrt(row_var + 1e-05) * gain_vec + bias_vec

def ref_layer(stream, params, layer_index):
    w_query, b_query, w_key, w_value, b_value, w_out, b_out, attn_gain, attn_bias, w_up, b_up, w_down, b_down, ffn_gain, ffn_bias = params
    split_shape = (-1, CLIP, HEADS, HEAD_DIM)
    score_scale = HEAD_DIM ** (-0.5)
    attn_input = low(stream)
    queries = low(low_back(matmul(attn_input, w_query[layer_index]) + b_query[layer_index])).reshape(split_shape)
    key_rows = low(low_back(matmul(attn_input, w_key[layer_index]))).reshape(split_shape)
    value_rows = low(low_back(matmul(attn_input, w_value[layer_index]) + b_value[layer_index])).reshape(split_shape)
    scores = low_back(jnp.einsum('bqhe,bkhe->bhqk', queries, key_rows, precision=lax.Precision.HIGHEST) * score_scale)
    row_max = lax.optimization_barrier(jnp.max(scores, axis=-1, keepdims=True))
    exp_scores = jnp.exp(scores - row_max)
    probs = low(exp_scores / lax.optimization_barrier(jnp.sum(exp_scores, axis=-1, keepdims=True)))
    context = jnp.einsum('bhqk,bkhe->bqhe', probs, value_rows, precision=lax.Precision.HIGHEST).reshape(stream.shape)
    context = low(low_back(context))
    attn_branch = low_back(matmul(context, w_out[layer_index]) + b_out[layer_index])
    normed = layer_norm(stream + attn_branch, attn_gain[layer_index], attn_bias[layer_index])
    ffn_input = low(normed)
    pre_act = low_back(matmul(ffn_input, w_up[layer_index]) + b_up[layer_index])
    hidden = low(gelu_exact(pre_act))
    ffn_branch = low_back(matmul(hidden, w_down[layer_index]) + b_down[layer_index])
    return layer_norm(normed + ffn_branch, ffn_gain[layer_index], ffn_bias[layer_index])

def forward(params, frames, marks):
    stream = frames * (1.0 - marks) + marks * params[0]
    for layer_index in range(LAYERS):
        stream = ref_layer(stream, params[1:], layer_index)
    return stream

def reference(frames, span_mask, mask_vector, w_query, b_query, w_key, w_value, b_value, w_out, b_out, attn_gain, attn_bias, w_up, b_up, w_down, b_down, ffn_gain, ffn_bias, out_grad):
    params = tuple((weight.astype(jnp.float32) for weight in (mask_vector, w_query, b_query, w_key, w_value, b_value, w_out, b_out, attn_gain, attn_bias, w_up, b_up, w_down, b_down, ffn_gain, ffn_bias)))
    group_clips = math.gcd(CLIPS, 8)
    group_rows = group_clips * CLIP
    group_count = TOKENS // group_rows
    all_frames = frames.astype(jnp.float32).reshape(group_count, group_rows, D)
    all_marks = span_mask.astype(jnp.float32).reshape(group_count, group_rows, 1)
    all_cots = out_grad.astype(jnp.float32).reshape(group_count, group_rows, D)

    def group_step(grad_total, group_data):
        group_frames, group_mask, group_cot = group_data
        result, pullback = jax.vjp(lambda weights, inputs: forward(weights, inputs, group_mask), params, group_frames)
        param_grads, frame_grads = pullback(group_cot * group_mask)
        grad_total = jax.tree.map(jnp.add, grad_total, param_grads)
        return (grad_total, (result.astype(jnp.bfloat16), frame_grads))
    zero_grads = jax.tree.map(jnp.zeros_like, params)
    grad_total, (results, frame_grads) = lax.scan(group_step, zero_grads, (all_frames, all_marks, all_cots))
    return (results.reshape(TOKENS, D), frame_grads.reshape(TOKENS, D), grad_total[0], grad_total[1], grad_total[2], grad_total[3], grad_total[4], grad_total[5], grad_total[6], grad_total[7], grad_total[8], grad_total[9], grad_total[10], grad_total[11], grad_total[12], grad_total[13], grad_total[14], grad_total[15])
```

```python
import functools
import jax
import jax.numpy as jnp
from jax import lax
from jax.experimental import pallas as pl
from jax.experimental.pallas import tpu as pltpu
from jax.sharding import PartitionSpec as P

HEAD_DIM = 64
CLIP = 368
BF = jnp.bfloat16
F32 = jnp.float32
SPAN = 2 * 10**10
LONG = 10**12
VMEM_LIMIT = 48 * 1024 * 1024


def nn(a, b):
    return lax.dot_general(a, b, (((1,), (0,)), ((), ())), preferred_element_type=F32)


def nt(a, b):
    return lax.dot_general(a, b, (((1,), (1,)), ((), ())), preferred_element_type=F32)


def tn(a, b):
    return lax.dot_general(a, b, (((0,), (0,)), ((), ())), preferred_element_type=F32)


def whole(shape):
    zeros = (0,) * len(shape)
    return pl.BlockSpec(tuple(shape), lambda i: zeros)


def at_layer(shape, layer):
    rest = (0,) * (len(shape) - 1)
    return pl.BlockSpec((1,) + tuple(shape[1:]), lambda i: (layer,) + rest)


class Order:
    def __init__(self):
        self.last = None
        self.span = SPAN

    def call(self, body, count, args, **given):
        given["in_specs"] = list(given["in_specs"])
        if self.last is not None:
            given["in_specs"].append(pl.BlockSpec(memory_space=pl.ANY))
            args = [*args, self.last]

        def kernel(*refs):
            body(*refs[:count], *refs[len(args) :])

        out = pl.pallas_call(kernel, grid=(1,), **given)(*args)
        self.last = out[0]
        return out


ORDER = Order()


def call(kernel, ins, outs, scratch=(), flops=0, name=None):
    specs = [
        pl.BlockSpec(memory_space=pltpu.SMEM)
        if l == "smem"
        else whole(a.shape)
        if l is None
        else at_layer(a.shape, l)
        for a, l in ins
    ]
    nbytes = sum(
        (a.size // a.shape[0] if isinstance(l, int) else a.size) * a.dtype.itemsize for a, l in ins
    ) + sum(o.size * o.dtype.itemsize for o in outs)
    return ORDER.call(
        kernel,
        len(ins),
        [a for a, _ in ins],
        in_specs=specs,
        out_specs=[whole(o.shape) for o in outs],
        out_shape=outs,
        scratch_shapes=list(scratch),
        compiler_params=pltpu.CompilerParams(vmem_limit_bytes=VMEM_LIMIT),
        cost_estimate=pl.CostEstimate(
            flops=max(flops, ORDER.span), bytes_accessed=nbytes, transcendentals=0
        ),
        name=name,
    )


def sds(shape, dtype):
    return jax.ShapeDtypeStruct(shape, dtype)


def split_out(value, scratch, oa, ob, who):
    half = oa.shape[0]
    scratch[...] = value
    at = pl.multiple_of(who[0] * half, 8)
    oa[...] = scratch[pl.ds(at, half), :].astype(BF)
    ob[...] = scratch[pl.ds(half - at, half), :].astype(BF)


def head_mask(width, head):
    cols = lax.broadcasted_iota(jnp.int32, (1, width), 1)
    return (cols // HEAD_DIM == head).astype(F32)


def soft(k, q, head):
    mask = (head_mask(q.shape[1], head) * HEAD_DIM ** (-0.5)).astype(BF)
    s = nt(k, q * mask)
    e = jnp.exp(s - jnp.max(s, axis=0, keepdims=True))
    return e * (1.0 / jnp.sum(e, axis=0, keepdims=True))


def attn_fwd_kernel(
    who, x_in, wq, wk, wv, wo, bq, bv, pa, pb, qo, ko, vo, kto, cto, scr, *, layer
):
    x = x_in[...]
    q = (nt(x, wq[0]) + bq[layer : layer + 1, :].astype(F32)).astype(BF)
    k = nt(x, wk[0]).astype(BF)
    kto[...] = nt(wk[0], x).astype(BF)
    v32 = nt(x, wv[0]) + bv[layer : layer + 1, :].astype(F32)
    v = v32.astype(BF)
    vt = v32.T.astype(BF)
    qo[...] = q
    ko[...] = k
    vo[...] = v
    parts = []
    for h in range(q.shape[1] // HEAD_DIM):
        pt = soft(k, q, h).astype(BF)
        parts.append(nn(vt[h * HEAD_DIM : (h + 1) * HEAD_DIM], pt))
    ct = jnp.concatenate(parts, axis=0).astype(BF)
    cto[...] = ct
    split_out(tn(ct, wo[0]), scr, pa, pb, who)


def attn_fwd(who, layer, x, wq, wk, wv, wo, bq, bv):
    rows, d = x.shape
    hd = wq.shape[1]
    outs = [
        sds((rows // 2, d), BF),
        sds((rows // 2, d), BF),
        sds((rows, hd), BF),
        sds((rows, hd), BF),
        sds((rows, hd), BF),
        sds((hd, rows), BF),
        sds((hd, rows), BF),
    ]
    return call(
        functools.partial(attn_fwd_kernel, layer=layer),
        [(who, "smem"), (x, None)]
        + [(w, layer) for w in (wq, wk, wv, wo)]
        + [(bq, None), (bv, None)],
        outs,
        [pltpu.VMEM((rows, d), F32)],
        flops=2 * rows * hd * (5 * d + 2 * rows),
        name="attn_fwd",
    )


def attn_bwd_kernel(
    who, b_in, q, k, v, kt, wq, wk, wv, wo, marks, pa, pb, dqt, dk, dv, sbq, sbv, smask, scr
):
    b = b_in[...]
    cg = nt(b, wo[0]).astype(BF)
    qv, kv, vv, ktv = q[...], k[...], v[...], kt[...]
    width = qv.shape[1]
    scale = HEAD_DIM ** (-0.5)
    dqs = []
    dk32 = jnp.zeros(qv.shape, F32)
    dv32 = jnp.zeros(qv.shape, F32)
    for h in range(width // HEAD_DIM):
        mask = head_mask(width, h)
        p = soft(kv, qv, h)
        dp = nt(vv, cg * mask.astype(BF))
        dsum = jnp.sum(p * dp, axis=0, keepdims=True)
        ds = (p * (dp - dsum)).astype(BF)
        dqs.append(nn(ktv[h * HEAD_DIM : (h + 1) * HEAD_DIM], ds))
        dk32 = dk32 + nn(ds, qv) * (mask * scale)
        dv32 = dv32 + nn(p.astype(BF), cg) * mask
    dqtv = (jnp.concatenate(dqs, axis=0) * scale).astype(BF)
    dkv = dk32.astype(BF)
    dvv = dv32.astype(BF)
    dqt[...] = dqtv
    dk[...] = dkv
    dv[...] = dvv
    sbq[...] = jnp.sum(dqtv.astype(F32).T, axis=0, keepdims=True)
    sbv[...] = jnp.sum(dvv.astype(F32), axis=0, keepdims=True)
    total = tn(dqtv, wq[0]) + nn(dkv, wk[0]) + nn(dvv, wv[0])
    smask[...] = jnp.sum(total * marks[:, :1].astype(F32), axis=0, keepdims=True)
    split_out(total, scr, pa, pb, who)


def attn_bwd(who, layer, b, q, k, v, kt, marks, wq, wk, wv, wo):
    rows, d = b.shape
    hd = wq.shape[1]
    outs = [
        sds((rows // 2, d), BF),
        sds((rows // 2, d), BF),
        sds((hd, rows), BF),
        sds((rows, hd), BF),
        sds((rows, hd), BF),
        sds((1, hd), F32),
        sds((1, hd), F32),
        sds((1, d), F32),
    ]
    return call(
        attn_bwd_kernel,
        [(who, "smem"), (b, None), (q, None), (k, None), (v, None), (kt, None)]
        + [(w, layer) for w in (wq, wk, wv, wo)]
        + [(marks, None)],
        outs,
        [pltpu.VMEM((rows, d), F32)],
        flops=2 * rows * hd * (4 * d + 5 * rows),
        name="attn_bwd",
    )


def ffn_fwd_kernel(who, y_in, wu, wd, bu, pa, pb, hid, slo, scr, *, layer):
    pre = nn(y_in[...], wu[0]) + bu[layer : layer + 1, :].astype(F32)
    phi = 0.5 * (1.0 + lax.erf(pre * 0.7071067811865476))
    hidden = (pre * phi).astype(BF)
    hid[...] = hidden
    slo[...] = (phi + pre * jnp.exp(-0.5 * pre * pre) * 0.3989422804014327).astype(BF)
    split_out(nn(hidden, wd[0]), scr, pa, pb, who)


def ffn_fwd(who, layer, y, wu, wd, bu):
    rows, d = y.shape
    ff = wu.shape[2]
    outs = [
        sds((rows // 2, d), BF),
        sds((rows // 2, d), BF),
        sds((rows, ff), BF),
        sds((rows, ff), BF),
    ]
    return call(
        functools.partial(ffn_fwd_kernel, layer=layer),
        [(who, "smem"), (y, None), (wu, layer), (wd, layer), (bu, None)],
        outs,
        [pltpu.VMEM((rows, d), F32)],
        flops=4 * rows * d * ff,
        name="ffn_fwd",
    )


def ffn_bwd_kernel(who, d_in, slo, wu, wd, pa, pb, act_o, sbu, scr):
    act = (nt(d_in[...], wd[0]) * slo[...].astype(F32)).astype(BF)
    act_o[...] = act
    sbu[...] = jnp.sum(act.astype(F32), axis=0, keepdims=True)
    split_out(nt(act, wu[0]), scr, pa, pb, who)


def ffn_bwd(who, layer, d_in, slo, wu, wd):
    rows, d = d_in.shape
    ff = wu.shape[2]
    outs = [
        sds((rows // 2, d), BF),
        sds((rows // 2, d), BF),
        sds((rows, ff), BF),
        sds((1, ff), F32),
    ]
    return call(
        ffn_bwd_kernel,
        [(who, "smem"), (d_in, None), (slo, None), (wu, layer), (wd, layer)],
        outs,
        [pltpu.VMEM((rows, d), F32)],
        flops=4 * rows * d * ff,
        name="ffn_bwd",
    )


def put_halves(bits, pick, scr, send, keep):
    half = keep.shape[0]
    bit = bits[pick]
    keep[...] = scr[pl.ds(pl.multiple_of(bit * half, 16), half), :]
    send[...] = scr[pl.ds(pl.multiple_of((1 - bit) * half, 16), half), :]


def pair_wgrad_kernel(bits, al, ar, bl, br, send, keep, scr, *, pick):
    scr[...] = (tn(al[...], bl[...]) + tn(ar[...], br[...])).astype(BF)
    put_halves(bits, pick, scr, send, keep)


def pair_wgrad(bits, pick, a, b, name):
    rows, m = a[0].shape
    n = b[0].shape[1]
    return call(
        functools.partial(pair_wgrad_kernel, pick=pick),
        [(bits, "smem")] + [(v, None) for v in (*a, *b)],
        [sds((m // 2, n), BF)] * 2,
        [pltpu.VMEM((m, n), BF)],
        flops=4 * rows * m * n,
        name=name,
    )


SMALL = 16


def attn_wgrad_kernel(
    bits, xl, xr, dqtl, dqtr, dkl, dkr, dvl, dvr, ctl, ctr, bl, br,
    sql, sqr, svl, svr, sul, sur, sma, smb, own_a, own_f, send, keep, scr, *, pick, masked
):
    hd = scr.shape[0] // 4 - SMALL
    step = hd + SMALL
    scr[:hd] = (nn(dqtl[...], xl[...]) + nn(dqtr[...], xr[...])).astype(BF)
    scr[step : step + hd] = (tn(dkl[...], xl[...]) + tn(dkr[...], xr[...])).astype(BF)
    scr[2 * step : 2 * step + hd] = (tn(dvl[...], xl[...]) + tn(dvr[...], xr[...])).astype(BF)
    scr[3 * step : 3 * step + hd] = (nn(ctl[...], bl[...]) + nn(ctr[...], br[...])).astype(BF)
    zeros = jnp.zeros((SMALL, scr.shape[1]), F32)
    for i in range(1, 4):
        scr[i * step + hd : (i + 1) * step] = zeros.astype(BF)
    heads = [sql[...] + sqr[...], svl[...] + svr[...], zeros[:1, : scr.shape[1] - 2 * hd]]
    mask_row = own_a[3:4] + sma[...] + smb[...] if masked else zeros[:1]
    rows = [
        jnp.concatenate(heads, axis=1),
        sul[...] + sur[...],
        own_a[:3],
        own_f[:3],
        mask_row,
        zeros[: SMALL - 9],
    ]
    scr[hd:step] = jnp.concatenate(rows, axis=0).astype(BF)
    put_halves(bits, pick, scr, send, keep)


def attn_wgrad(bits, pick, masked, hd, *values):
    rows, dim = values[0].shape
    size = 2 * (hd + SMALL)
    return call(
        functools.partial(attn_wgrad_kernel, pick=pick, masked=masked),
        [(bits, "smem")] + [(v, None) for v in values],
        [sds((size, dim), BF)] * 2,
        [pltpu.VMEM((2 * size, dim), BF)],
        flops=16 * rows * dim * hd,
        name="attn_wgrad",
    )


def halve_kernel(bits, have, got, send, keep, *, pick):
    half = keep.shape[0]
    bit = bits[pick]
    mine = pl.ds(pl.multiple_of(bit * half, 16), half)
    other = pl.ds(pl.multiple_of((1 - bit) * half, 16), half)
    keep[...] = (have[mine, :].astype(F32) + got[mine, :].astype(F32)).astype(BF)
    send[...] = (have[other, :].astype(F32) + got[other, :].astype(F32)).astype(BF)


def halve(bits, pick, have, got):
    rows, dim = have.shape
    return call(
        functools.partial(halve_kernel, pick=pick),
        [(bits, "smem"), (have, None), (got, None)],
        [sds((rows // 2, dim), BF)] * 2,
        name="halve",
    )


def add_kernel(a, b, o):
    o[...] = (a[...].astype(F32) + b[...].astype(F32)).astype(BF)


def add(a, b):
    return call(add_kernel, [(a, None), (b, None)], [sds(a.shape, BF)], name="add")[0]


def stacked_call(kernel, bits, parts, outs, small, layer, layers, old, name):
    dim = parts[0].shape[1]
    old = [] if old is None else list(old)
    shapes = [sds((layers, rows, dim), F32) for rows in outs]
    specs = [pl.BlockSpec((1, rows, dim), lambda i: (layer, 0, 0)) for rows in outs]
    if small is not None:
        shapes.append(sds(small, F32))
        specs.append(whole(small))
    n = 1 + len(parts)

    def body(*refs):
        kernel(*refs[:n], *refs[n + len(old) :])

    return ORDER.call(
        body,
        n + len(old),
        [bits, *parts, *old],
        in_specs=[pl.BlockSpec(memory_space=pltpu.SMEM)]
        + [whole(q.shape) for q in parts]
        + [pl.BlockSpec(memory_space=pl.ANY)] * len(old),
        out_specs=specs,
        out_shape=shapes,
        input_output_aliases={n + i: i for i in range(len(old))},
        compiler_params=pltpu.CompilerParams(vmem_limit_bytes=VMEM_LIMIT),
        cost_estimate=pl.CostEstimate(flops=ORDER.span, bytes_accessed=1, transcendentals=0),
        name=name,
    )


def when_at(first, second, fn):
    for spot in range(4):

        @pl.when(2 * first + second == spot)
        def _(spot=spot):
            fn(spot)


def place_attn_kernel(bits, *refs, picks):
    parts, outs, small = refs[:4], refs[4:8], refs[8]
    hd = outs[0].shape[1]
    for i, ref in enumerate(parts):
        first = bits[picks[0]] if i < 2 else 1 - bits[picks[0]]
        second = bits[picks[1]] if i % 2 == 0 else 1 - bits[picks[1]]

        def put(spot, ref=ref):
            outs[spot][0] = ref[:hd, :].astype(F32)
            if spot == 0:
                small[...] = ref[hd:, :].astype(F32)

        when_at(first, second, put)


def place_attn(bits, picks, parts, layer, layers, old):
    rows, dim = parts[0].shape
    return stacked_call(
        functools.partial(place_attn_kernel, picks=picks),
        bits,
        parts,
        [rows - SMALL] * 4,
        (SMALL, dim),
        layer,
        layers,
        old,
        "place_attn",
    )


def place_ffn_kernel(bits, mine, by_low, by_high, down_far, up_far, down, up):
    size = down_far.shape[0]
    low, high = bits[0], bits[1]
    parts = [
        (low, high, mine, mine),
        (1 - low, high, by_low, by_low),
        (low, 1 - high, by_high, by_high),
        (1 - low, 1 - high, down_far, up_far),
    ]
    for l, h, ref_down, ref_up in parts:

        def put_down(spot, ref=ref_down):
            down[0, spot * size : (spot + 1) * size, :] = ref[:size, :].astype(F32)

        def put_up(spot, ref=ref_up):
            up[0, spot * size : (spot + 1) * size, :] = ref[ref.shape[0] - size :, :].astype(F32)

        when_at(l, h, put_down)
        when_at(h, l, put_up)


def place_ffn(bits, parts, layer, layers, old):
    rows = 4 * parts[3].shape[0]
    return stacked_call(
        place_ffn_kernel, bits, parts, [rows] * 2, None, layer, layers, old, "place_ffn"
    )


def halve_two_kernel(bits, kd, gd, ku, gu, send_d, send_u, keep):
    size = send_d.shape[0]
    for have, got, send, pick, at in ((kd, gd, send_d, 1, 0), (ku, gu, send_u, 0, size)):
        bit = bits[pick]
        mine = pl.ds(pl.multiple_of(bit * size, 16), size)
        other = pl.ds(pl.multiple_of((1 - bit) * size, 16), size)
        keep[at : at + size, :] = (have[mine, :].astype(F32) + got[mine, :].astype(F32)).astype(BF)
        send[...] = (have[other, :].astype(F32) + got[other, :].astype(F32)).astype(BF)


def halve_two(bits, kd, gd, ku, gu):
    rows, dim = kd.shape
    return call(
        halve_two_kernel,
        [(bits, "smem"), (kd, None), (gd, None), (ku, None), (gu, None)],
        [sds((rows // 2, dim), BF), sds((rows // 2, dim), BF), sds((rows, dim), BF)],
        name="halve_two",
    )


def add_two_kernel(have, gd, gu, out):
    size = gd.shape[0]
    out[:size, :] = (have[:size, :].astype(F32) + gd[...].astype(F32)).astype(BF)
    out[size:, :] = (have[size:, :].astype(F32) + gu[...].astype(F32)).astype(BF)


def add_two(have, gd, gu):
    return call(
        add_two_kernel, [(have, None), (gd, None), (gu, None)], [sds(have.shape, BF)], name="add_two"
    )[0]


def cut_two_kernel(by_high, by_low, od, ou):
    size = od.shape[0]
    od[...] = by_high[:size, :]
    ou[...] = by_low[size:, :]


def cut_two(by_high, by_low):
    rows, dim = by_high.shape
    return call(
        cut_two_kernel,
        [(by_high, None), (by_low, None)],
        [sds((rows // 2, dim), BF)] * 2,
        name="cut_two",
    )


def swap_bit(v, size, pick):
    return lax.ppermute(v, "dp", [(i, i ^ (1 << pick)) for i in range(size)])


def copy_kernel(have, out):
    out[...] = have[...]


def gate(v):
    return call(copy_kernel, [(v, None)], [sds(v.shape, v.dtype)], name="gate")[0]


class DpSum:
    def __init__(self, bits, size, picks):
        self.bits, self.size, self.picks = bits, size, picks
        self.rest = [p for p in range(size.bit_length() - 1) if p not in picks]

    def swap(self, v, pick):
        return swap_bit(v, self.size, pick)

    def start(self, fn, *values):
        send, self.keep = fn(self.bits, self.picks[0], *values)
        self.got = self.swap(send, self.picks[0])

    def halve(self):
        send, self.keep = halve(self.bits, self.picks[1], self.keep, self.got)
        self.got = self.swap(send, self.picks[1])

    def cross(self):
        self.keep = add(self.keep, self.got)
        if self.rest:
            self.got = self.swap(self.keep, self.rest[0])

    def total(self):
        for i in range(len(self.rest)):
            self.keep = add(self.keep, self.got)
            if i + 1 < len(self.rest):
                self.got = self.swap(self.keep, self.rest[i + 1])

    def hold(self):
        self.keep = gate(self.keep)

    def spread(self):
        self.near = self.swap(self.keep, self.picks[1])
        self.far = self.swap(self.keep, self.picks[0])

    def last(self):
        self.end = self.swap(self.near, self.picks[0])

    def parts(self):
        return self.keep, self.near, self.far, self.end


class FfnSum:
    def __init__(self, bits, size):
        self.bits, self.size = bits, size
        self.rest = range(2, size.bit_length() - 1)

    def swap(self, v, pick):
        return swap_bit(v, self.size, pick)

    def start(self, down, up):
        send, self.kd = pair_wgrad(self.bits, 0, down[:2], down[2:], "down_wgrad")
        self.gd = self.swap(send, 0)
        send, self.ku = pair_wgrad(self.bits, 1, up[:2], up[2:], "up_wgrad")
        self.gu = self.swap(send, 1)

    def halve(self):
        send_d, send_u, self.keep = halve_two(self.bits, self.kd, self.gd, self.ku, self.gu)
        self.gd = self.swap(send_d, 1)
        self.gu = self.swap(send_u, 0)

    def cross(self):
        self.keep = add_two(self.keep, self.gd, self.gu)
        if self.rest:
            self.got = self.swap(self.keep, self.rest[0])

    def total(self):
        for i in range(len(self.rest)):
            self.keep = add(self.keep, self.got)
            if i + 1 < len(self.rest):
                self.got = self.swap(self.keep, self.rest[i + 1])

    def hold(self):
        self.keep = gate(self.keep)

    def high(self):
        self.by_high = self.swap(self.keep, 1)

    def low(self):
        self.by_low = self.swap(self.keep, 0)

    def last(self):
        od, ou = cut_two(self.by_high, self.by_low)
        self.down_far = self.swap(od, 0)
        self.up_far = self.swap(ou, 1)

    def parts(self):
        return self.keep, self.by_low, self.by_high, self.down_far, self.up_far


def three(who, mine, pair, far):
    half = mine.shape[0]
    near = jnp.where(who[0] == 0, pair[half:, :].astype(F32), pair[:half, :].astype(F32))
    return mine[...].astype(F32) + near + far[...].astype(F32)


def norm_fwd_kernel(who, p0, p1, p2, res, bias, gain, shift, out, unit, inv, low, *, layer):
    row = slice(layer, layer + 1)
    r = res[...] + three(who, p0, p1, p2) + bias[row, :].astype(F32)
    mean = jnp.mean(r, axis=-1, keepdims=True)
    c = r - mean
    i = lax.rsqrt(jnp.mean(c * c, axis=-1, keepdims=True) + 1e-05)
    u = c * i
    o = u * gain[row, :].astype(F32) + shift[row, :].astype(F32)
    out[...] = o
    unit[...] = u
    inv[...] = i
    low[...] = o.astype(BF)


def norm_fwd(who, layer, parts, res, bias, gain, shift):
    rows, d = res.shape
    return call(
        functools.partial(norm_fwd_kernel, layer=layer),
        [(who, "smem")] + [(v, None) for v in (*parts, res, bias, gain, shift)],
        [sds((rows, d), F32), sds((rows, d), F32), sds((rows, 1), F32), sds((rows, d), BF)],
        name="norm_fwd",
    )


def norm_bwd_core(up, unit, inv, gain, marks, resid, low, sums, layer):
    u = unit[...]
    e = up * gain[layer : layer + 1, :].astype(F32)
    r = inv[...] * (
        e - jnp.mean(e, axis=-1, keepdims=True) - u * jnp.mean(e * u, axis=-1, keepdims=True)
    )
    resid[...] = r
    lo = r.astype(BF)
    low[...] = lo
    sums[0:1, :] = jnp.sum(up * u, axis=0, keepdims=True)
    sums[1:2, :] = jnp.sum(up, axis=0, keepdims=True)
    sums[2:3, :] = jnp.sum(lo.astype(F32), axis=0, keepdims=True)
    sums[3:4, :] = jnp.sum(r * marks[...], axis=0, keepdims=True)


def norm_bwd_first_kernel(og, unit, inv, gain, marks, resid, low, sums, *, layer):
    up = og[...].astype(F32) * marks[...]
    norm_bwd_core(up, unit, inv, gain, marks, resid, low, sums, layer)


def norm_bwd_kernel(who, p0, p1, p2, res, unit, inv, gain, marks, resid, low, sums, *, layer):
    up = res[...] + three(who, p0, p1, p2)
    norm_bwd_core(up, unit, inv, gain, marks, resid, low, sums, layer)


def norm_bwd(who, layer, ins, unit, inv, gain, marks):
    rows, d = unit.shape
    first = len(ins) == 1
    return call(
        functools.partial(norm_bwd_first_kernel if first else norm_bwd_kernel, layer=layer),
        ([] if first else [(who, "smem")])
        + [(v, None) for v in (*ins, unit, inv, gain, marks)],
        [sds((rows, d), F32), sds((rows, d), BF), sds((4, d), F32)],
        name="norm_bwd",
    )


def last_kernel(who, p0, p1, p2, res, marks, out):
    out[...] = (res[...] + three(who, p0, p1, p2)) * (1.0 - marks[...])


def last_rows(who, parts, res, marks):
    return call(
        last_kernel,
        [(who, "smem")] + [(v, None) for v in (*parts, res, marks)],
        [sds(res.shape, F32)],
        name="last_rows",
    )[0]


FFN, ATTN = range(2)
ATTN_PICKS = (0, 1)
PLAN = {
    ("attn_near", False): [(0, FFN, "halve")],
    ("attn_far", False): [(0, ATTN, "start"), (0, FFN, "cross")],
    ("ffn_near", True): [(1, ATTN, "halve")],
    ("ffn_far", True): [(0, FFN, "start"), (1, ATTN, "cross"), (1, FFN, "total"), (1, FFN, "high")],
    ("attn_near", True): [(0, FFN, "halve"), (1, ATTN, "total"), (1, FFN, "hold"), (1, FFN, "low")],
    ("attn_far", True): [(0, FFN, "cross"), (0, ATTN, "start"), (1, FFN, "last")],
}
PLAN["ffn_far", False] = [(0, FFN, "start")]
TAIL = [
    (0, ATTN, "halve"),
    (1, FFN, "place"),
    (1, ATTN, "hold"),
    (1, ATTN, "spread"),
    (0, FFN, "total"),
    (0, FFN, "high"),
    (0, FFN, "low"),
    (0, ATTN, "cross"),
    (1, ATTN, "last"),
    (0, FFN, "last"),
    (0, ATTN, "total"),
    (0, ATTN, "spread"),
    (1, ATTN, "place"),
    (0, ATTN, "last"),
    (0, FFN, "place"),
    (0, ATTN, "place"),
]
CHIP = [(0, 2), (2, 0), (1, 3), (3, 1)]


def chip(v):
    return lax.ppermute(v, "mp", CHIP)


def both_cores(v):
    return lax.all_gather(v, "mp", axis=0, tiled=True, axis_index_groups=[[0, 1], [2, 3]])


def join_kernel(who, mine, pair, out):
    half = mine.shape[0]
    theirs = jnp.where(who[0] == 0, pair[half:, :].astype(F32), pair[:half, :].astype(F32))
    out[...] = (mine[...].astype(F32) + theirs).astype(BF)


def gather_sum(who, local, remote):
    joined = call(
        join_kernel,
        [(who, "smem"), (remote[0], None), (both_cores(remote[1]), None)],
        [sds(remote[0].shape, BF)],
        name="join",
    )[0]
    return local[0], both_cores(local[1]), chip(joined)


def per_device(
    frames,
    span_mask,
    mask_vector,
    w_query,
    b_query,
    w_key,
    w_value,
    b_value,
    w_out,
    b_out,
    attn_gain,
    attn_bias,
    w_up,
    b_up,
    w_down,
    b_down,
    ffn_gain,
    ffn_bias,
    out_grad,
):
    layers = w_query.shape[0]
    dim = frames.shape[1]
    size = lax.axis_size("dp")
    place_in_dp = lax.axis_index("dp")
    who = (lax.axis_index("mp") & 1).astype(jnp.int32)[None]
    bits = jnp.stack([(place_in_dp >> k) & 1 for k in range(size.bit_length() - 1)]).astype(jnp.int32)
    wq = jnp.swapaxes(w_query, 1, 2)
    wk = jnp.swapaxes(w_key, 1, 2)
    wv = jnp.swapaxes(w_value, 1, 2)
    marks = span_mask.astype(F32)[:, None]
    stream = frames.astype(F32) * (1.0 - marks) + marks * mask_vector.astype(F32)
    low = stream.astype(BF)
    ORDER.last, ORDER.span = None, SPAN
    records = []

    def both(fn, v, extra, jobs=None):
        far = chip(v)
        near = both_cores(gate(v))
        first = fn(near, *extra[0])
        if jobs:
            jobs()
        far = both_cores(far)
        return (near, far), [first, fn(far, *extra[1])]

    mark_rows = jnp.broadcast_to(marks.astype(BF), (marks.shape[0], 128))
    mark_near = both_cores(mark_rows)
    mark_sides = (mark_near, chip(mark_near))

    none = ((), ())
    for l in range(layers):
        xs, att = both(
            lambda v: attn_fwd(who, l, v, wq, wk, wv, w_out, b_query, b_value), low, none
        )
        parts = gather_sum(who, att[0][:2], att[1][:2])
        normed, unit_a, inv_a, low_a = norm_fwd(who, l, parts, stream, b_out, attn_gain, attn_bias)
        ys, ffn = both(lambda v: ffn_fwd(who, l, v, w_up, w_down, b_up), low_a, none)
        parts = gather_sum(who, ffn[0][:2], ffn[1][:2])
        stream, unit_f, inv_f, low = norm_fwd(who, l, parts, normed, b_down, ffn_gain, ffn_bias)
        records.append((xs, att, ys, ffn, unit_a, inv_a, unit_f, inv_f))
    hidden_out = low
    sums = [None] * layers
    ins = (out_grad,)
    for l in reversed(range(layers)):
        xs, att, ys, ffn, unit_a, inv_a, unit_f, inv_f = records[l]
        sums[l] = (FfnSum(bits, size), DpSum(bits, size, ATTN_PICKS))
        inputs = [None, None]

        def window(name):
            for ahead, which, step in PLAN.get((name, l == 0), ()):
                if l + ahead < layers:
                    group = sums[l + ahead][which]
                    if step == "start":
                        group.start(*inputs[which])
                    else:
                        getattr(group, step)()

        resid_f, low_f, sums_f = norm_bwd(who, l, ins, unit_f, inv_f, ffn_gain, marks)
        ds, back = both(
            lambda v, c: ffn_bwd(who, l, v, c, w_up, w_down),
            low_f,
            [(f[3],) for f in ffn],
            lambda: window("ffn_near"),
        )
        parts = gather_sum(who, back[0][:2], back[1][:2])
        inputs[FFN] = ((ffn[0][2], ffn[1][2], *ds), (*ys, back[0][2], back[1][2]))
        window("ffn_far")
        s_up = (back[0][3], back[1][3])
        resid_a, low_a, sums_a = norm_bwd(who, l, (*parts, resid_f), unit_a, inv_a, attn_gain, marks)
        bs, back = both(
            lambda v, *c: attn_bwd(who, l, v, *c, wq, wk, wv, w_out),
            low_a,
            [(*a[2:6], m) for a, m in zip(att, mark_sides)],
            lambda: window("attn_near"),
        )
        parts = gather_sum(who, back[0][:2], back[1][:2])
        values = [*xs]
        for i in (2, 3, 4):
            values += [b[i] for b in back]
        values += [a[6] for a in att]
        values += bs
        for i in (5, 6):
            values += [b[i] for b in back]
        values += s_up
        values += [b[7] for b in back]
        inputs[ATTN] = (
            lambda bi, p, *v: attn_wgrad(bi, p, l == 0, wq.shape[1], *v),
            *values,
            sums_a,
            sums_f,
        )
        ORDER.span = 2 * SPAN if l == 0 else SPAN
        window("attn_far")
        ins = (*parts, resid_a)
    frames_grad = last_rows(who, ins[:3], ins[3], marks)
    g_att = g_ffn = None
    smalls = [None] * layers
    for ahead, which, step in TAIL:
        if ahead >= layers:
            continue
        group = sums[ahead][which]
        if step != "place":
            getattr(group, step)()
        elif which == FFN:
            g_ffn = place_ffn(bits, group.parts(), ahead, layers, g_ffn)
        else:
            *g_att, smalls[ahead] = place_attn(
                bits, ATTN_PICKS, group.parts(), ahead, layers, g_att
            )
    g_down, g_up = g_ffn
    common = jnp.concatenate([v[2:10] for v in smalls], axis=0)
    common = common.reshape(-1, 8, dim)
    pair = both_cores(common.reshape(-1, dim)).reshape(2, -1, dim)
    common = pair[0] + pair[1]
    common = (common + chip(common)).reshape(layers, 8, dim)
    hd = wq.shape[1]
    heads = jnp.stack([v[0] for v in smalls])

    def swapped(i):
        return jnp.swapaxes(g_att[i], 1, 2)

    return (
        hidden_out,
        frames_grad,
        common[0, 6],
        swapped(0),
        heads[:, :hd],
        swapped(1),
        swapped(2),
        heads[:, hd : 2 * hd],
        g_att[3],
        common[:, 2],
        common[:, 0],
        common[:, 1],
        g_up,
        jnp.stack([v[1] for v in smalls]),
        g_down,
        common[:, 5],
        common[:, 3],
        common[:, 4],
    )


def solution(mesh):
    rows = P(("dp", "mp"), None)
    cols = P(None, None, "mp")
    units = P(None, "mp", None)
    vec = P(None, "mp")
    return jax.shard_map(
        per_device,
        mesh=mesh,
        in_specs=(
            rows, P(("dp", "mp")), P(), cols, vec, cols, cols, vec, units, P(), P(), P(),
            cols, vec, units, P(), P(), P(), rows,
        ),
        out_specs=(
            rows, rows, P(), cols, vec, cols, cols, vec, units, P(), P(), P(),
            cols, vec, units, P(), P(), P(),
        ),
        check_vma=False,
    )
```

```python
import functools
import math
import jax
import jax.numpy as jnp
from jax import lax
from jax.experimental import pallas as pl
from jax.experimental.pallas import tpu as pltpu
from jax.sharding import PartitionSpec as P

HEAD_DIM = 64
CLIP = 368
BF = jnp.bfloat16
F32 = jnp.float32
SPAN = 8 * 10**9
LONG = 10**12
VMEM_LIMIT = 48 * 1024 * 1024


def nn(a, b):
    return lax.dot_general(a, b, (((1,), (0,)), ((), ())), preferred_element_type=F32)


def nt(a, b):
    return lax.dot_general(a, b, (((1,), (1,)), ((), ())), preferred_element_type=F32)


def tn(a, b):
    return lax.dot_general(a, b, (((0,), (0,)), ((), ())), preferred_element_type=F32)


def whole(shape):
    zeros = (0,) * len(shape)
    return pl.BlockSpec(tuple(shape), lambda i: zeros)


def at_layer(shape, layer):
    rest = (0,) * (len(shape) - 1)
    return pl.BlockSpec((1,) + tuple(shape[1:]), lambda i: (layer,) + rest)


def sds(shape, dtype):
    return jax.ShapeDtypeStruct(shape, dtype)


def kept(shape, dtype):
    return pltpu.HBM(shape, dtype)


class Order:
    def __init__(self):
        self.last = None
        self.span = SPAN
        self.small = True

    def call(self, body, count, args, mark=0, **given):
        given["in_specs"] = list(given["in_specs"])
        if self.last is not None:
            given["in_specs"].append(pl.BlockSpec(memory_space=pl.ANY))
            args = [*args, self.last]

        def kernel(*refs):
            body(*refs[:count], *refs[len(args) :])

        out = pl.pallas_call(kernel, grid=(1,), **given)(*args)
        if mark is not None:
            self.last = out[mark]
        return out


ORDER = Order()


def call(kernel, ins, outs, scratch=(), flops=0, name=None, mark=0):
    specs = [
        pl.BlockSpec(memory_space=pltpu.SMEM)
        if l == "smem"
        else whole(a.shape)
        if l is None
        else at_layer(a.shape, l)
        for a, l in ins
    ]
    nbytes = sum(
        (a.size // a.shape[0] if isinstance(l, int) else a.size) * a.dtype.itemsize for a, l in ins
    ) + sum(math.prod(o.shape) * o.dtype.itemsize for o in outs)
    return ORDER.call(
        kernel,
        len(ins),
        [a for a, _ in ins],
        mark=mark,
        in_specs=specs,
        out_specs=[whole(o.shape) for o in outs],
        out_shape=outs,
        scratch_shapes=list(scratch),
        compiler_params=pltpu.CompilerParams(vmem_limit_bytes=VMEM_LIMIT),
        cost_estimate=pl.CostEstimate(
            flops=max(flops, ORDER.span), bytes_accessed=nbytes, transcendentals=0
        ),
        name=name,
    )


def join(a_ref, b_ref, scratch, joined):
    half = a_ref.shape[0]
    scratch[:half] = a_ref[...].astype(F32)
    scratch[half:] = b_ref[...].astype(F32)
    value = scratch[...].astype(BF)
    joined[...] = value
    return value


def arrange(who, pair, scratch, arranged):
    half = pair.shape[0] // 2
    scratch[...] = pair[...].astype(F32)
    at = pl.multiple_of(who[0] * half, 8)
    both = [scratch[pl.ds(at, half), :], scratch[pl.ds(half - at, half), :]]
    value = jnp.concatenate(both, axis=0).astype(BF)
    arranged[...] = value
    return value


def split_out(value, scratch, oa, ob):
    half = oa.shape[0]
    scratch[...] = value
    oa[...] = scratch[:half].astype(BF)
    ob[...] = scratch[half:].astype(BF)


def head_mask(width, head):
    cols = lax.broadcasted_iota(jnp.int32, (1, width), 1)
    return (cols // HEAD_DIM == head).astype(F32)


def soft(k, q, head):
    mask = (head_mask(q.shape[1], head) * HEAD_DIM ** (-0.5)).astype(BF)
    s = nt(k, q * mask)
    e = jnp.exp(s - jnp.max(s, axis=0, keepdims=True))
    return e * (1.0 / jnp.sum(e, axis=0, keepdims=True))


def attn_fwd_kernel(
    xa, xb, wq, wk, wv, wo, bq, bv, pa, pb, xc, qo, ko, vo, kto, cto, scr, *, layer
):
    x = join(xa, xb, scr, xc)
    q = (nt(x, wq[0]) + bq[layer : layer + 1, :].astype(F32)).astype(BF)
    k = nt(x, wk[0]).astype(BF)
    kto[...] = nt(wk[0], x).astype(BF)
    v32 = nt(x, wv[0]) + bv[layer : layer + 1, :].astype(F32)
    v = v32.astype(BF)
    vt = v32.T.astype(BF)
    qo[...] = q
    ko[...] = k
    vo[...] = v
    parts = []
    for h in range(q.shape[1] // HEAD_DIM):
        pt = soft(k, q, h).astype(BF)
        parts.append(nn(vt[h * HEAD_DIM : (h + 1) * HEAD_DIM], pt))
    ct = jnp.concatenate(parts, axis=0).astype(BF)
    cto[...] = ct
    split_out(tn(ct, wo[0]), scr, pa, pb)


def attn_fwd(layer, xa, xb, wq, wk, wv, wo, bq, bv):
    rows, d = 2 * xa.shape[0], xa.shape[1]
    hd = wq.shape[1]
    outs = [
        sds((rows // 2, d), BF),
        sds((rows // 2, d), BF),
        sds((rows, d), BF),
        sds((rows, hd), BF),
        sds((rows, hd), BF),
        sds((rows, hd), BF),
        sds((hd, rows), BF),
        sds((hd, rows), BF),
    ]
    return call(
        functools.partial(attn_fwd_kernel, layer=layer),
        [(xa, None), (xb, None)]
        + [(w, layer) for w in (wq, wk, wv, wo)]
        + [(bq, None), (bv, None)],
        outs,
        [pltpu.VMEM((rows, d), F32)],
        flops=2 * rows * hd * (5 * d + 2 * rows),
        name="attn_fwd",
    )


def attn_bwd_kernel(
    who, b_in, q, k, v, kt, wq, wk, wv, wo, marks, pa, pb, bc, dqt, dk, dv, sbq, sbv, smask, scr
):
    b = arrange(who, b_in, scr, bc)
    cg = nt(b, wo[0]).astype(BF)
    qv, kv, vv, ktv = q[...], k[...], v[...], kt[...]
    width = qv.shape[1]
    scale = HEAD_DIM ** (-0.5)
    dqs = []
    dk32 = jnp.zeros(qv.shape, F32)
    dv32 = jnp.zeros(qv.shape, F32)
    for h in range(width // HEAD_DIM):
        mask = head_mask(width, h)
        p = soft(kv, qv, h)
        dp = nt(vv, cg * mask.astype(BF))
        dsum = jnp.sum(p * dp, axis=0, keepdims=True)
        ds = (p * (dp - dsum)).astype(BF)
        dqs.append(nn(ktv[h * HEAD_DIM : (h + 1) * HEAD_DIM], ds))
        dk32 = dk32 + nn(ds, qv) * (mask * scale)
        dv32 = dv32 + nn(p.astype(BF), cg) * mask
    dqtv = (jnp.concatenate(dqs, axis=0) * scale).astype(BF)
    dkv = dk32.astype(BF)
    dvv = dv32.astype(BF)
    dqt[...] = dqtv
    dk[...] = dkv
    dv[...] = dvv
    sbq[...] = jnp.sum(dqtv.astype(F32).T, axis=0, keepdims=True)
    sbv[...] = jnp.sum(dvv.astype(F32), axis=0, keepdims=True)
    total = tn(dqtv, wq[0]) + nn(dkv, wk[0]) + nn(dvv, wv[0])
    smask[...] = jnp.sum(total * marks[:, :1].astype(F32), axis=0, keepdims=True)
    split_out(total, scr, pa, pb)


def attn_bwd(who, layer, b, q, k, v, kt, marks, wq, wk, wv, wo):
    rows, d = b.shape
    hd = wq.shape[1]
    outs = [
        sds((rows // 2, d), BF),
        sds((rows // 2, d), BF),
        sds((rows, d), BF),
        sds((hd, rows), BF),
        sds((rows, hd), BF),
        sds((rows, hd), BF),
        sds((1, hd), F32),
        sds((1, hd), F32),
        sds((1, d), F32),
    ]
    return call(
        attn_bwd_kernel,
        [(who, "smem"), (b, None), (q, None), (k, None), (v, None), (kt, None)]
        + [(w, layer) for w in (wq, wk, wv, wo)]
        + [(marks, None)],
        outs,
        [pltpu.VMEM((rows, d), F32)],
        flops=2 * rows * hd * (4 * d + 5 * rows),
        name="attn_bwd",
    )


def ffn_fwd_kernel(ya, yb, wu, wd, bu, pa, pb, yc, hid, slo, scr, *, layer):
    pre = nn(join(ya, yb, scr, yc), wu[0]) + bu[layer : layer + 1, :].astype(F32)
    phi = 0.5 * (1.0 + lax.erf(pre * 0.7071067811865476))
    hidden = (pre * phi).astype(BF)
    hid[...] = hidden
    slo[...] = (phi + pre * jnp.exp(-0.5 * pre * pre) * 0.3989422804014327).astype(BF)
    split_out(nn(hidden, wd[0]), scr, pa, pb)


def ffn_fwd(layer, ya, yb, wu, wd, bu):
    rows, d = 2 * ya.shape[0], ya.shape[1]
    ff = wu.shape[2]
    outs = [
        sds((rows // 2, d), BF),
        sds((rows // 2, d), BF),
        sds((rows, d), BF),
        sds((rows, ff), BF),
        sds((rows, ff), BF),
    ]
    return call(
        functools.partial(ffn_fwd_kernel, layer=layer),
        [(ya, None), (yb, None), (wu, layer), (wd, layer), (bu, None)],
        outs,
        [pltpu.VMEM((rows, d), F32)],
        flops=4 * rows * d * ff,
        name="ffn_fwd",
    )


def ffn_bwd_kernel(who, d_in, slo, wu, wd, pa, pb, dc, act_o, sbu, scr):
    act = (nt(arrange(who, d_in, scr, dc), wd[0]) * slo[...].astype(F32)).astype(BF)
    act_o[...] = act
    sbu[...] = jnp.sum(act.astype(F32), axis=0, keepdims=True)
    split_out(nt(act, wu[0]), scr, pa, pb)


def ffn_bwd(who, layer, d_in, slo, wu, wd):
    rows, d = d_in.shape
    ff = wu.shape[2]
    outs = [
        sds((rows // 2, d), BF),
        sds((rows // 2, d), BF),
        sds((rows, d), BF),
        sds((rows, ff), BF),
        sds((1, ff), F32),
    ]
    return call(
        ffn_bwd_kernel,
        [(who, "smem"), (d_in, None), (slo, None), (wu, layer), (wd, layer)],
        outs,
        [pltpu.VMEM((rows, d), F32)],
        flops=4 * rows * d * ff,
        name="ffn_bwd",
    )


def put_halves(bits, pick, scr, send, keep):
    half = keep.shape[0]
    bit = bits[pick]
    keep[...] = scr[pl.ds(pl.multiple_of(bit * half, 16), half), :]
    send[...] = scr[pl.ds(pl.multiple_of((1 - bit) * half, 16), half), :]


def pair_wgrad_kernel(bits, al, ar, bl, br, send, keep, scr, *, pick):
    scr[...] = (tn(al[...], bl[...]) + tn(ar[...], br[...])).astype(BF)
    put_halves(bits, pick, scr, send, keep)


def pair_wgrad(bits, pick, a, b, name):
    rows, m = a[0].shape
    n = b[0].shape[1]
    return call(
        functools.partial(pair_wgrad_kernel, pick=pick),
        [(bits, "smem")] + [(v, None) for v in (*a, *b)],
        [sds((m // 2, n), BF)] * 2,
        [pltpu.VMEM((m, n), BF)],
        flops=4 * rows * m * n,
        name=name,
    )


def attn_wgrad_kernel(
    bits, xl, xr, dqtl, dqtr, dkl, dkr, dvl, dvr, ctl, ctr, bl, br, send, keep, scr, *, pick
):
    hd = scr.shape[0] // 4
    scr[:hd] = (nn(dqtl[...], xl[...]) + nn(dqtr[...], xr[...])).astype(BF)
    scr[hd : 2 * hd] = (tn(dkl[...], xl[...]) + tn(dkr[...], xr[...])).astype(BF)
    scr[2 * hd : 3 * hd] = (tn(dvl[...], xl[...]) + tn(dvr[...], xr[...])).astype(BF)
    scr[3 * hd :] = (nn(ctl[...], bl[...]) + nn(ctr[...], br[...])).astype(BF)
    put_halves(bits, pick, scr, send, keep)


def attn_wgrad(bits, pick, hd, *values):
    rows, dim = values[0].shape
    return call(
        functools.partial(attn_wgrad_kernel, pick=pick),
        [(bits, "smem")] + [(v, None) for v in values],
        [sds((2 * hd, dim), BF)] * 2,
        [pltpu.VMEM((4 * hd, dim), BF)],
        flops=16 * rows * dim * hd,
        name="attn_wgrad",
    )


def attn_wgrad_two_kernel(
    bits, xl, xr, dqtl, dqtr, dkl, dkr, dvl, dvr, ctl, ctr, bl, br, sd, kd, su, ku, sc_d, sc_u
):
    hd = sc_d.shape[0] // 2
    sc_d[:hd] = (nn(dqtl[...], xl[...]) + nn(dqtr[...], xr[...])).astype(BF)
    sc_d[hd:] = (tn(dkl[...], xl[...]) + tn(dkr[...], xr[...])).astype(BF)
    put_halves(bits, 0, sc_d, sd, kd)
    sc_u[:hd] = (tn(dvl[...], xl[...]) + tn(dvr[...], xr[...])).astype(BF)
    sc_u[hd:] = (nn(ctl[...], bl[...]) + nn(ctr[...], br[...])).astype(BF)
    put_halves(bits, 1, sc_u, su, ku)


def attn_wgrad_two(bits, hd, *values):
    rows, dim = values[0].shape
    return call(
        attn_wgrad_two_kernel,
        [(bits, "smem")] + [(v, None) for v in values],
        [sds((hd, dim), BF)] * 4,
        [pltpu.VMEM((2 * hd, dim), BF)] * 2,
        flops=16 * rows * dim * hd,
        name="attn_wgrad",
    )


def place_two_kernel(bits, mine, by_low, by_high, down_far, up_far, *outs):
    size = down_far.shape[0]
    low, high = bits[0], bits[1]
    parts = [
        (low, high, mine, mine),
        (1 - low, high, by_low, by_low),
        (low, 1 - high, by_high, by_high),
        (1 - low, 1 - high, down_far, up_far),
    ]
    for l, h, ref_down, ref_up in parts:

        def put_down(spot, ref=ref_down):
            at = (spot % 2) * size
            outs[spot // 2][0, at : at + size, :] = ref[:size, :].astype(F32)

        def put_up(spot, ref=ref_up):
            at = (spot % 2) * size
            outs[2 + spot // 2][0, at : at + size, :] = ref[ref.shape[0] - size :, :].astype(F32)

        when_at(l, h, put_down)
        when_at(h, l, put_up)


def small_kernel(*refs, layers, hd):
    out = refs[-1]
    width = out.shape[1]
    zeros = jnp.zeros((8, width), F32)
    rows = []
    for l in range(layers):
        sql, sqr, svl, svr, sul, sur, own_a, own_f, sma, smb = refs[10 * l : 10 * l + 10]
        heads = [sql[...] + sqr[...], svl[...] + svr[...], zeros[:1, : width - 2 * hd]]
        mask_row = own_a[3:4] + sma[...] + smb[...] if l == 0 else zeros[:1]
        rows += [own_a[:3], own_f[:3], mask_row, zeros[:1]]
        rows += [jnp.concatenate(heads, axis=1), sul[...] + sur[...], zeros[:6]]
    out[...] = jnp.concatenate(rows, axis=0)


def small_rows(values, hd):
    layers = len(values)
    dim = values[0][6].shape[1]
    return call(
        functools.partial(small_kernel, layers=layers, hd=hd),
        [(v, None) for vs in values for v in vs],
        [sds((16 * layers, dim), F32)],
        name="small_rows",
    )[0]


def small_mp_kernel(have, got, out):
    for l in range(have.shape[0] // 16):
        out[16 * l : 16 * l + 8, :] = have[16 * l : 16 * l + 8, :] + got[16 * l : 16 * l + 8, :]
        out[16 * l + 8 : 16 * l + 16, :] = have[16 * l + 8 : 16 * l + 16, :]


def small_dp_kernel(have, got, out):
    out[...] = have[...] + got[...]


def small_add(have, got, over_mp):
    return call(
        small_mp_kernel if over_mp else small_dp_kernel,
        [(have, None), (got, None)],
        [sds(have.shape, F32)],
        name="small_add",
    )[0]


def halve_kernel(bits, have, got, send, keep, *, pick):
    half = keep.shape[0]
    bit = bits[pick]
    mine = pl.ds(pl.multiple_of(bit * half, 16), half)
    other = pl.ds(pl.multiple_of((1 - bit) * half, 16), half)
    keep[...] = (have[mine, :].astype(F32) + got[mine, :].astype(F32)).astype(BF)
    send[...] = (have[other, :].astype(F32) + got[other, :].astype(F32)).astype(BF)


def halve(bits, pick, have, got):
    rows, dim = have.shape
    return call(
        functools.partial(halve_kernel, pick=pick),
        [(bits, "smem"), (have, None), (got, None)],
        [sds((rows // 2, dim), BF)] * 2,
        name="halve",
    )


def add_kernel(a, b, o):
    o[...] = (a[...].astype(F32) + b[...].astype(F32)).astype(BF)


def add(a, b):
    return call(add_kernel, [(a, None), (b, None)], [sds(a.shape, BF)], name="add")[0]


def stacked_call(kernel, bits, parts, outs, layer, layers, old, name):
    dim = parts[0].shape[1]
    old = [] if old is None else list(old)
    shapes = [sds((layers, rows, dim), F32) for rows in outs]
    specs = [pl.BlockSpec((1, rows, dim), lambda i: (layer, 0, 0)) for rows in outs]
    n = 1 + len(parts)

    def body(*refs):
        kernel(*refs[:n], *refs[n + len(old) :])

    return ORDER.call(
        body,
        n + len(old),
        [bits, *parts, *old],
        mark=None,
        in_specs=[pl.BlockSpec(memory_space=pltpu.SMEM)]
        + [whole(q.shape) for q in parts]
        + [pl.BlockSpec(memory_space=pl.ANY)] * len(old),
        out_specs=specs,
        out_shape=shapes,
        input_output_aliases={n + i: i for i in range(len(old))},
        compiler_params=pltpu.CompilerParams(vmem_limit_bytes=VMEM_LIMIT),
        cost_estimate=pl.CostEstimate(flops=ORDER.span, bytes_accessed=1, transcendentals=0),
        name=name,
    )


def when_at(first, second, fn):
    for spot in range(4):

        @pl.when(2 * first + second == spot)
        def _(spot=spot):
            fn(spot)


def place_attn_kernel(bits, *refs, picks):
    parts, outs = refs[:4], refs[4:]
    for i, ref in enumerate(parts):
        first = bits[picks[0]] if i < 2 else 1 - bits[picks[0]]
        second = bits[picks[1]] if i % 2 == 0 else 1 - bits[picks[1]]

        def put(spot, ref=ref):
            outs[spot][0] = ref[...].astype(F32)

        when_at(first, second, put)


def place_attn(bits, picks, parts, layer, layers, old):
    return stacked_call(
        functools.partial(place_attn_kernel, picks=picks),
        bits,
        parts,
        [parts[0].shape[0]] * 4,
        layer,
        layers,
        old,
        "place_attn",
    )


def place_ffn_kernel(bits, mine, by_low, by_high, down_far, up_far, down, up):
    size = down_far.shape[0]
    low, high = bits[0], bits[1]
    parts = [
        (low, high, mine, mine),
        (1 - low, high, by_low, by_low),
        (low, 1 - high, by_high, by_high),
        (1 - low, 1 - high, down_far, up_far),
    ]
    for l, h, ref_down, ref_up in parts:

        def put_down(spot, ref=ref_down):
            down[0, spot * size : (spot + 1) * size, :] = ref[:size, :].astype(F32)

        def put_up(spot, ref=ref_up):
            up[0, spot * size : (spot + 1) * size, :] = ref[ref.shape[0] - size :, :].astype(F32)

        when_at(l, h, put_down)
        when_at(h, l, put_up)


def place_ffn(bits, parts, layer, layers, old):
    rows = 4 * parts[3].shape[0]
    return stacked_call(
        place_ffn_kernel, bits, parts, [rows] * 2, layer, layers, old, "place_ffn"
    )


def halve_two_kernel(bits, kd, gd, ku, gu, send_d, send_u, keep):
    size = send_d.shape[0]
    for have, got, send, pick, at in ((kd, gd, send_d, 1, 0), (ku, gu, send_u, 0, size)):
        bit = bits[pick]
        mine = pl.ds(pl.multiple_of(bit * size, 16), size)
        other = pl.ds(pl.multiple_of((1 - bit) * size, 16), size)
        keep[at : at + size, :] = (have[mine, :].astype(F32) + got[mine, :].astype(F32)).astype(BF)
        send[...] = (have[other, :].astype(F32) + got[other, :].astype(F32)).astype(BF)


def halve_two(bits, kd, gd, ku, gu):
    rows, dim = kd.shape
    return call(
        halve_two_kernel,
        [(bits, "smem"), (kd, None), (gd, None), (ku, None), (gu, None)],
        [sds((rows // 2, dim), BF), sds((rows // 2, dim), BF), sds((rows, dim), BF)],
        name="halve_two",
    )


def add_two_kernel(have, gd, gu, out):
    size = gd.shape[0]
    out[:size, :] = (have[:size, :].astype(F32) + gd[...].astype(F32)).astype(BF)
    out[size:, :] = (have[size:, :].astype(F32) + gu[...].astype(F32)).astype(BF)


def add_two(have, gd, gu):
    return call(
        add_two_kernel, [(have, None), (gd, None), (gu, None)], [sds(have.shape, BF)], name="add_two"
    )[0]


def cut_two_kernel(by_high, by_low, od, ou):
    size = od.shape[0]
    od[...] = by_high[:size, :]
    ou[...] = by_low[size:, :]


def cut_two(by_high, by_low):
    rows, dim = by_high.shape
    return call(
        cut_two_kernel,
        [(by_high, None), (by_low, None)],
        [sds((rows // 2, dim), BF)] * 2,
        name="cut_two",
    )


def swap_bit(v, size, pick):
    return lax.ppermute(v, "dp", [(i, i ^ (1 << pick)) for i in range(size)])


def copy_kernel(have, out):
    out[...] = have[...]


def gate(v):
    return call(copy_kernel, [(v, None)], [sds(v.shape, v.dtype)], name="gate")[0]


def merge_kernel(ffn, have, got, out):
    size = ffn.shape[0]
    out[:size, :] = ffn[...]
    out[size:, :] = (have[...].astype(F32) + got[...].astype(F32)).astype(BF)


def cut_merged_kernel(by_high, by_low, od, ou):
    size = ou.shape[0]
    od[:size, :] = by_high[:size, :]
    od[size:, :] = by_high[2 * size :, :]
    ou[...] = by_low[size : 2 * size, :]


def place_merged_kernel(bits, mine, by_low, by_high, down_far, up_far, down, up, *heads):
    size = up_far.shape[0]
    low, high = bits[0], bits[1]
    parts = [
        (low, high, mine, mine, mine, 2),
        (1 - low, high, by_low, by_low, by_low, 2),
        (low, 1 - high, by_high, by_high, by_high, 2),
        (1 - low, 1 - high, down_far, up_far, down_far, 1),
    ]
    for l, h, ref_down, ref_up, ref_head, at in parts:

        def put_down(spot, ref=ref_down, head=ref_head, at=at):
            down[0, spot * size : (spot + 1) * size, :] = ref[:size, :].astype(F32)
            heads[spot][0] = head[at * size : (at + 1) * size, :].astype(F32)

        def put_up(spot, ref=ref_up, at=at):
            up[0, spot * size : (spot + 1) * size, :] = ref[
                (at - 1) * size : at * size, :
            ].astype(F32)

        when_at(l, h, put_down)
        when_at(h, l, put_up)


class Merged:
    def __init__(self, ffn, attn):
        self.ffn, self.attn = ffn, attn

    def merge(self):
        ffn, attn = self.ffn, self.attn
        for i in range(len(attn.rest) - 1):
            attn.keep = add(attn.keep, attn.got)
            attn.got = attn.swap(attn.keep, attn.rest[i + 1])
        have, got = attn.keep, attn.got
        rows = ffn.keep.shape[0] + have.shape[0]
        self.keep = call(
            merge_kernel,
            [(ffn.keep, None), (have, None), (got, None)],
            [sds((rows, have.shape[1]), BF)],
            name="merge",
        )[0]
        self.by_high = ffn.swap(self.keep, 1)
        self.by_low = ffn.swap(self.keep, 0)

    def cut(self):
        rows, dim = self.keep.shape
        od, ou = call(
            cut_merged_kernel,
            [(self.by_high, None), (self.by_low, None)],
            [sds((2 * rows // 3, dim), BF), sds((rows // 3, dim), BF)],
            name="cut_merged",
        )
        self.down_far = self.ffn.swap(od, 0)
        self.up_far = self.ffn.swap(ou, 1)

    def place(self, bits, layer, layers):
        size = self.up_far.shape[0]
        parts = self.keep, self.by_low, self.by_high, self.down_far, self.up_far
        outs = [4 * size] * 2 + [size] * 4
        got = stacked_call(
            place_merged_kernel, bits, parts, outs, layer, layers, None, "place_merged"
        )
        return got[:2], got[2:]


class DpSum:
    def __init__(self, bits, size, picks):
        self.bits, self.size, self.picks = bits, size, picks
        self.rest = [p for p in range(size.bit_length() - 1) if p not in picks]

    def swap(self, v, pick):
        return swap_bit(v, self.size, pick)

    def start(self, fn, *values):
        send, self.keep = fn(self.bits, self.picks[0], *values)
        self.got = self.swap(send, self.picks[0])

    def halve(self):
        send, self.keep = halve(self.bits, self.picks[1], self.keep, self.got)
        self.got = self.swap(send, self.picks[1])

    def cross(self):
        self.keep = add(self.keep, self.got)
        if self.rest:
            self.got = self.swap(self.keep, self.rest[0])

    def total(self):
        for i in range(len(self.rest)):
            self.keep = add(self.keep, self.got)
            if i + 1 < len(self.rest):
                self.got = self.swap(self.keep, self.rest[i + 1])

    def hold(self):
        self.keep = gate(self.keep)

    def spread(self):
        self.near = self.swap(self.keep, self.picks[1])
        self.far = self.swap(self.keep, self.picks[0])

    def last(self):
        self.end = self.swap(self.near, self.picks[0])

    def parts(self):
        return self.keep, self.near, self.far, self.end


class FfnSum:
    def __init__(self, bits, size):
        self.bits, self.size = bits, size
        self.rest = range(2, size.bit_length() - 1)

    def swap(self, v, pick):
        return swap_bit(v, self.size, pick)

    def start(self, down, up):
        send, self.kd = pair_wgrad(self.bits, 0, down[:2], down[2:], "down_wgrad")
        self.gd = self.swap(send, 0)
        send, self.ku = pair_wgrad(self.bits, 1, up[:2], up[2:], "up_wgrad")
        self.gu = self.swap(send, 1)

    def halve(self):
        send_d, send_u, self.keep = halve_two(self.bits, self.kd, self.gd, self.ku, self.gu)
        self.gd = self.swap(send_d, 1)
        self.gu = self.swap(send_u, 0)

    def cross(self):
        self.keep = add_two(self.keep, self.gd, self.gu)
        if self.rest:
            self.got = self.swap(self.keep, self.rest[0])

    def total(self):
        for i in range(len(self.rest)):
            self.keep = add(self.keep, self.got)
            if i + 1 < len(self.rest):
                self.got = self.swap(self.keep, self.rest[i + 1])

    def hold(self):
        self.keep = gate(self.keep)

    def high(self):
        self.by_high = self.swap(self.keep, 1)

    def low(self):
        self.by_low = self.swap(self.keep, 0)

    def last(self):
        od, ou = cut_two(self.by_high, self.by_low)
        self.down_far = self.swap(od, 0)
        self.up_far = self.swap(ou, 1)

    def parts(self):
        return self.keep, self.by_low, self.by_high, self.down_far, self.up_far


class AttnSum(FfnSum):
    def start(self, fn, *values):
        sd, self.kd, su, self.ku = attn_wgrad_two(self.bits, values[0], *values[1:])
        self.gd = self.swap(sd, 0)
        self.gu = self.swap(su, 1)

    def place(self, layer, layers, old):
        parts = self.parts()
        rows = 2 * parts[3].shape[0]
        return stacked_call(
            place_two_kernel, self.bits, parts, [rows] * 4, layer, layers, old, "place_attn"
        )


def three(who, mine, pair, far):
    half = mine.shape[0]
    if pair.shape[0] == half:
        near = pair[...].astype(F32)
    else:
        near = jnp.where(who[0] == 0, pair[half:, :].astype(F32), pair[:half, :].astype(F32))
    return mine[...].astype(F32) + near + far[...].astype(F32)


def norm_fwd_kernel(near, far, res, bias, gain, shift, out, unit, inv, low, *, layer):
    row = slice(layer, layer + 1)
    r = res[...] + (near[...] + far[...].astype(F32)) + bias[row, :].astype(F32)
    mean = jnp.mean(r, axis=-1, keepdims=True)
    c = r - mean
    i = lax.rsqrt(jnp.mean(c * c, axis=-1, keepdims=True) + 1e-05)
    u = c * i
    o = u * gain[row, :].astype(F32) + shift[row, :].astype(F32)
    out[...] = o
    unit[...] = u
    inv[...] = i
    low[...] = o.astype(BF)


def norm_fwd(layer, parts, res, bias, gain, shift):
    rows, d = res.shape
    return call(
        functools.partial(norm_fwd_kernel, layer=layer),
        [(v, None) for v in (*parts, res, bias, gain, shift)],
        [sds((rows, d), F32), sds((rows, d), F32), sds((rows, 1), F32), sds((rows, d), BF)],
        name="norm_fwd",
        mark=3,
    )


def norm_bwd_core(up, unit, inv, gain, marks, resid, low, sums, layer):
    u = unit[...]
    e = up * gain[layer : layer + 1, :].astype(F32)
    r = inv[...] * (
        e - jnp.mean(e, axis=-1, keepdims=True) - u * jnp.mean(e * u, axis=-1, keepdims=True)
    )
    resid[...] = r
    lo = r.astype(BF)
    low[...] = lo
    sums[0:1, :] = jnp.sum(up * u, axis=0, keepdims=True)
    sums[1:2, :] = jnp.sum(up, axis=0, keepdims=True)
    sums[2:3, :] = jnp.sum(lo.astype(F32), axis=0, keepdims=True)
    sums[3:4, :] = jnp.sum(r * marks[...], axis=0, keepdims=True)


def norm_bwd_first_kernel(og, unit, inv, gain, marks, resid, low, sums, *, layer):
    up = og[...].astype(F32) * marks[...]
    norm_bwd_core(up, unit, inv, gain, marks, resid, low, sums, layer)


def norm_bwd_kernel(who, p0, p1, p2, res, unit, inv, gain, marks, resid, low, sums, *, layer):
    up = res[...] + three(who, p0, p1, p2)
    norm_bwd_core(up, unit, inv, gain, marks, resid, low, sums, layer)


def norm_bwd(who, layer, ins, unit, inv, gain, marks):
    rows, d = unit.shape
    first = len(ins) == 1
    return call(
        functools.partial(norm_bwd_first_kernel if first else norm_bwd_kernel, layer=layer),
        ([] if first else [(who, "smem")])
        + [(v, None) for v in (*ins, unit, inv, gain, marks)],
        [sds((rows, d), F32), sds((rows, d), BF), sds((4, d), F32)],
        name="norm_bwd",
        mark=1,
    )


def last_kernel(who, p0, p1, p2, res, marks, out):
    out[...] = (res[...] + three(who, p0, p1, p2)) * (1.0 - marks[...])


def last_rows(who, parts, res, marks):
    return call(
        last_kernel,
        [(who, "smem")] + [(v, None) for v in (*parts, res, marks)],
        [sds(res.shape, F32)],
        name="last_rows",
        mark=None,
    )[0]


FFN, ATTN, BOTH, SMALL = range(4)
ATTN_PICKS = (0, 1)
PLAN = {
    ("ffn_far", False): [(0, FFN, "start")],
    ("attn_near", False): [(0, FFN, "halve")],
    ("attn_far", False): [(0, ATTN, "start"), (0, FFN, "cross")],
    ("ffn_near", True): [(1, ATTN, "halve")],
    ("ffn_far", True): [(0, FFN, "start"), (1, ATTN, "cross"), (1, FFN, "total")],
    ("attn_near", True): [(0, FFN, "halve"), (1, BOTH, "merge")],
    ("attn_mid", True): [(0, FFN, "cross")],
    ("attn_far", True): [(0, ATTN, "start"), (1, BOTH, "cut")],
}
TAIL = [
    (0, ATTN, "halve"),
    (0, SMALL, ""),
    (1, BOTH, "place"),
    (0, ATTN, "cross"),
    (0, SMALL, ""),
    (0, FFN, "total"),
    (0, FFN, "high"),
    (0, FFN, "low"),
    (0, SMALL, ""),
    (0, ATTN, "total"),
    (0, ATTN, "high"),
    (0, ATTN, "low"),
    (0, FFN, "last"),
    (0, SMALL, ""),
    (0, ATTN, "last"),
    (0, FFN, "place"),
    (0, SMALL, ""),
    (0, ATTN, "place"),
]
CORE = [(0, 1), (1, 0), (2, 3), (3, 2)]
CHIP = [(0, 2), (2, 0), (1, 3), (3, 1)]


def core(v):
    return lax.ppermute(v, "mp", CORE)


def chip(v):
    return lax.ppermute(v, "mp", CHIP)


def both_cores(v):
    return lax.all_gather(v, "mp", axis=0, tiled=True, axis_index_groups=[[0, 1], [2, 3]])


def join_kernel(who, mine, pair, out):
    half = mine.shape[0]
    theirs = jnp.where(who[0] == 0, pair[half:, :].astype(F32), pair[:half, :].astype(F32))
    out[...] = (mine[...].astype(F32) + theirs).astype(BF)


def gather_sum(who, local, remote):
    joined = call(
        join_kernel,
        [(who, "smem"), (remote[0], None), (both_cores(remote[1]), None)],
        [sds(remote[0].shape, BF)],
        name="join",
    )[0]
    return local[0], both_cores(local[1]), chip(joined)


def prep_kernel(frames, span, vector, stream, low, marks, wide):
    m = jnp.broadcast_to(span[...].astype(F32), (8, span.shape[1])).T[:, :1]
    value = frames[...].astype(F32) * (1.0 - m) + m * vector[...].astype(F32)
    stream[...] = value
    low[...] = value.astype(BF)
    marks[...] = m
    wide[...] = jnp.broadcast_to(m, wide.shape).astype(BF)


def prep(frames, span, vector):
    rows = frames.shape[0]
    return call(
        prep_kernel,
        [(frames, None), (span, None), (vector, None)],
        [sds(frames.shape, F32), sds(frames.shape, BF), sds((rows, 1), F32), sds((rows, 128), BF)],
        name="prep",
        mark=1,
    )


def pair_kernel(a, b, out):
    both = [a[...].astype(F32), b[...].astype(F32)]
    out[...] = jnp.concatenate(both, axis=0).astype(out.dtype)


def pair_rows(a, b):
    shape = (2 * a.shape[0], a.shape[1])
    return call(pair_kernel, [(a, None), (b, None)], [sds(shape, a.dtype)], name="pair_rows")[0]


def plus_kernel(a, b, out):
    out[...] = (a[...].astype(F32) + b[...].astype(F32)).astype(out.dtype)


def plus(a, b, dtype):
    return call(plus_kernel, [(a, None), (b, None)], [sds(a.shape, dtype)], name="plus")[0]


def per_device(
    frames,
    span_mask,
    mask_vector,
    w_query,
    b_query,
    w_key,
    w_value,
    b_value,
    w_out,
    b_out,
    attn_gain,
    attn_bias,
    w_up,
    b_up,
    w_down,
    b_down,
    ffn_gain,
    ffn_bias,
    out_grad,
):
    layers = w_query.shape[0]
    dim = frames.shape[1]
    size = lax.axis_size("dp")
    place_in_dp = lax.axis_index("dp")
    who = (lax.axis_index("mp") & 1).astype(jnp.int32)[None]
    bits = jnp.stack([(place_in_dp >> k) & 1 for k in range(size.bit_length() - 1)]).astype(jnp.int32)
    wq = jnp.swapaxes(w_query, 1, 2)
    wk = jnp.swapaxes(w_key, 1, 2)
    wv = jnp.swapaxes(w_value, 1, 2)
    ORDER.last, ORDER.span, ORDER.small = None, 2 * 10**10, True
    stream, low, marks, mark_rows = prep(frames, span_mask[None], mask_vector[None])
    records = []

    def both(fn, v, extra, jobs=None, later=None, light=False):
        far = chip(v)
        near = both_cores(gate(v))
        first = fn(near, *extra[0])
        if jobs:
            jobs()
        far = both_cores(far)
        if later and light:
            ORDER.span = 0
        second = fn(far, *extra[1])
        ORDER.span = SPAN
        if later:
            later()
        return [first, second]

    def forward(fn, v, marked=None):
        far = chip(v)
        first = fn(v, core(v))
        if marked is not None:
            mark_sides.extend(pair_rows(v, core(v)) for v in (marked, chip(marked)))
        near_sum = plus(first[0], core(first[1]), F32)
        second = fn(far, core(far))
        far_sum = chip(plus(second[0], core(second[1]), BF))
        return (near_sum, far_sum), [first[2:], second[2:]]

    mark_sides = []
    for l in range(layers):
        parts, att = forward(
            lambda *v: attn_fwd(l, *v, wq, wk, wv, w_out, b_query, b_value),
            low,
            None if l else mark_rows,
        )
        normed, unit_a, inv_a, low_a = norm_fwd(l, parts, stream, b_out, attn_gain, attn_bias)
        parts, ffn = forward(lambda *v: ffn_fwd(l, *v, w_up, w_down, b_up), low_a)
        stream, unit_f, inv_f, low = norm_fwd(l, parts, normed, b_down, ffn_gain, ffn_bias)
        records.append((att, ffn, unit_a, inv_a, unit_f, inv_f))
    hidden_out = low
    ORDER.span, ORDER.small = SPAN, True
    sums = [None] * layers
    smalls = [None] * layers
    ins = (out_grad,)
    for l in reversed(range(layers)):
        att, ffn, unit_a, inv_a, unit_f, inv_f = records[l]
        sums[l] = [FfnSum(bits, size), DpSum(bits, size, ATTN_PICKS) if l else AttnSum(bits, size)]
        sums[l].append(Merged(*sums[l]))
        inputs = [None, None]

        def window(name):
            for ahead, which, step in PLAN.get((name, l == 0), ()):
                if l + ahead < layers:
                    group = sums[l + ahead][which]
                    if step == "start":
                        group.start(*inputs[which])
                    else:
                        getattr(group, step)()

        resid_f, low_f, sums_f = norm_bwd(who, l, ins, unit_f, inv_f, ffn_gain, marks)
        back = both(
            lambda v, c: ffn_bwd(who, l, v, c, w_up, w_down),
            low_f,
            [(f[2],) for f in ffn],
            lambda: window("ffn_near"),
            lambda: window("ffn_mid"),
        )
        parts = gather_sum(who, back[0][:2], back[1][:2])
        inputs[FFN] = (
            [f[1] for f in ffn] + [b[2] for b in back],
            [f[0] for f in ffn] + [b[3] for b in back],
        )
        window("ffn_far")
        s_up = [b[4] for b in back]
        resid_a, low_a, sums_a = norm_bwd(
            who, l, (*parts, resid_f), unit_a, inv_a, attn_gain, marks
        )
        back = both(
            lambda v, *c: attn_bwd(who, l, v, *c, wq, wk, wv, w_out),
            low_a,
            [(*a[1:5], m) for a, m in zip(att, mark_sides)],
            lambda: window("attn_near"),
            lambda: window("attn_mid"),
            l == 0,
        )
        parts = gather_sum(who, back[0][:2], back[1][:2])
        values = [a[0] for a in att]
        for i in (3, 4, 5):
            values += [b[i] for b in back]
        values += [a[5] for a in att]
        values += [b[2] for b in back]
        smalls[l] = [b[i] for i in (6, 7) for b in back] + s_up
        smalls[l] += [sums_a, sums_f] + [b[8] for b in back]
        inputs[ATTN] = (
            lambda bi, p, hd, *v: attn_wgrad(bi, p, hd, *v),
            wq.shape[1],
            *values,
        )
        ORDER.span = 2 * SPAN if l == 0 else SPAN
        window("attn_far")
        ins = (*parts, resid_a)
    frames_grad = last_rows(who, ins[:3], ins[3], marks)
    g_att = g_ffn = None
    small = small_rows(smalls, wq.shape[1])
    small_at = 0
    for ahead, which, step in TAIL:
        if ahead >= layers:
            continue
        if which == SMALL:
            if small_at < 2:
                small = small_add(small, (core, chip)[small_at](small), True)
            elif small_at < size.bit_length() + 1:
                small = small_add(small, swap_bit(small, size, small_at - 2), False)
            small_at += 1
            continue
        group = sums[ahead][which]
        if step != "place":
            getattr(group, step)()
        elif which == BOTH:
            g_ffn, g_att = group.place(bits, ahead, layers)
        elif which == FFN:
            g_ffn = place_ffn(bits, group.parts(), ahead, layers, g_ffn)
        elif ahead:
            g_att = place_attn(bits, ATTN_PICKS, group.parts(), ahead, layers, g_att)
        else:
            g_att = group.place(ahead, layers, g_att)
    while small_at < size.bit_length() + 1:
        small = small_add(small, swap_bit(small, size, small_at - 2), False)
        small_at += 1
    g_down, g_up = g_ffn
    small = small.reshape(layers, 16, dim)
    common = small[:, :8]
    heads = small[:, 8]
    hd = wq.shape[1]

    def swapped(i):
        return jnp.swapaxes(g_att[i], 1, 2)

    return (
        hidden_out,
        frames_grad,
        common[0, 6],
        swapped(0),
        heads[:, :hd],
        swapped(1),
        swapped(2),
        heads[:, hd : 2 * hd],
        g_att[3],
        common[:, 2],
        common[:, 0],
        common[:, 1],
        g_up,
        small[:, 9],
        g_down,
        common[:, 5],
        common[:, 3],
        common[:, 4],
    )


def solution(mesh):
    rows = P(("dp", "mp"), None)
    cols = P(None, None, "mp")
    units = P(None, "mp", None)
    vec = P(None, "mp")
    return jax.shard_map(
        per_device,
        mesh=mesh,
        in_specs=(
            rows, P(("dp", "mp")), P(), cols, vec, cols, cols, vec, units, P(), P(), P(),
            cols, vec, units, P(), P(), P(), rows,
        ),
        out_specs=(
            rows, rows, P(), cols, vec, cols, cols, vec, units, P(), P(), P(),
            cols, vec, units, P(), P(), P(),
        ),
        check_vma=False,
    )
```

```python
import functools
import math
import jax
import jax.numpy as jnp
from jax import lax
from jax.experimental import pallas as pl
from jax.experimental.pallas import tpu as pltpu
from jax.sharding import PartitionSpec as P

HEAD_DIM = 64
CLIP = 368
BF = jnp.bfloat16
F32 = jnp.float32
SPAN = 8 * 10**9
LONG = 10**12
VMEM_LIMIT = 32 * 1024 * 1024


def nn(a, b):
    return lax.dot_general(a, b, (((1,), (0,)), ((), ())), preferred_element_type=F32)


def nt(a, b):
    return lax.dot_general(a, b, (((1,), (1,)), ((), ())), preferred_element_type=F32)


def tn(a, b):
    return lax.dot_general(a, b, (((0,), (0,)), ((), ())), preferred_element_type=F32)


def whole(shape):
    zeros = (0,) * len(shape)
    return pl.BlockSpec(tuple(shape), lambda i: zeros)


def at_layer(shape, layer):
    rest = (0,) * (len(shape) - 1)
    return pl.BlockSpec((1,) + tuple(shape[1:]), lambda i: (layer,) + rest)


def sds(shape, dtype):
    return jax.ShapeDtypeStruct(shape, dtype)


def kept(shape, dtype):
    return pltpu.HBM(shape, dtype)


class Order:
    def __init__(self):
        self.last = None
        self.span = SPAN
        self.small = True

    def call(self, body, count, args, mark=0, **given):
        anywhere = pl.BlockSpec(memory_space=pl.ANY)
        given["in_specs"] = list(given["in_specs"])
        if self.last is not None:
            given["in_specs"].append(anywhere)
            args = [*args, self.last]
        extra = mark is None
        if extra:
            given["out_specs"] = [*given["out_specs"], anywhere]
            given["out_shape"] = [*given["out_shape"], sds((8, 128), F32)]
        n = len(given["out_shape"])

        def kernel(*refs):
            outs = refs[len(args) : len(args) + n - extra]
            body(*refs[:count], *outs, *refs[len(args) + n :])

        out = pl.pallas_call(kernel, grid=(1,), **given)(*args)
        self.last = out[-1 if extra else mark]
        return out[: n - extra]


ORDER = Order()


def call(kernel, ins, outs, scratch=(), flops=0, name=None, mark=0):
    specs = [
        pl.BlockSpec(memory_space=pltpu.SMEM)
        if l == "smem"
        else whole(a.shape)
        if l is None
        else at_layer(a.shape, l)
        for a, l in ins
    ]
    nbytes = sum(
        (a.size // a.shape[0] if isinstance(l, int) else a.size) * a.dtype.itemsize for a, l in ins
    ) + sum(math.prod(o.shape) * o.dtype.itemsize for o in outs)
    return ORDER.call(
        kernel,
        len(ins),
        [a for a, _ in ins],
        mark=mark,
        in_specs=specs,
        out_specs=[whole(o.shape) for o in outs],
        out_shape=outs,
        scratch_shapes=list(scratch),
        compiler_params=pltpu.CompilerParams(vmem_limit_bytes=VMEM_LIMIT),
        cost_estimate=pl.CostEstimate(
            flops=max(flops, ORDER.span), bytes_accessed=nbytes, transcendentals=0
        ),
        name=name,
    )


def join(a_ref, b_ref, scratch, joined):
    half = a_ref.shape[0]
    scratch[:half] = a_ref[...].astype(F32)
    scratch[half:] = b_ref[...].astype(F32)
    value = scratch[...].astype(BF)
    joined[...] = value
    return value


def arrange(who, pair, scratch, arranged):
    half = pair.shape[0] // 2
    scratch[...] = pair[...].astype(F32)
    at = pl.multiple_of(who[0] * half, 8)
    both = [scratch[pl.ds(at, half), :], scratch[pl.ds(half - at, half), :]]
    value = jnp.concatenate(both, axis=0).astype(BF)
    arranged[...] = value
    return value


def split_out(value, scratch, oa, ob):
    half = oa.shape[0]
    scratch[...] = value
    oa[...] = scratch[:half].astype(BF)
    ob[...] = scratch[half:].astype(BF)


def head_mask(width, head):
    cols = lax.broadcasted_iota(jnp.int32, (1, width), 1)
    return (cols // HEAD_DIM == head).astype(F32)


def soft(k, q, head):
    mask = (head_mask(q.shape[1], head) * HEAD_DIM ** (-0.5)).astype(BF)
    s = nt(k, q * mask)
    e = jnp.exp(s - jnp.max(s, axis=0, keepdims=True))
    return e * (1.0 / jnp.sum(e, axis=0, keepdims=True))


def attn_fwd_kernel(
    xa, xb, wq, wk, wv, wo, bq, bv, pa, pb, xc, qo, ko, vo, kto, cto, scr, *, layer
):
    x = join(xa, xb, scr, xc)
    q = (nt(x, wq[0]) + bq[layer : layer + 1, :].astype(F32)).astype(BF)
    k = nt(x, wk[0]).astype(BF)
    kto[...] = nt(wk[0], x).astype(BF)
    v32 = nt(x, wv[0]) + bv[layer : layer + 1, :].astype(F32)
    v = v32.astype(BF)
    vt = v32.T.astype(BF)
    qo[...] = q
    ko[...] = k
    vo[...] = v
    parts = []
    for h in range(q.shape[1] // HEAD_DIM):
        pt = soft(k, q, h).astype(BF)
        parts.append(nn(vt[h * HEAD_DIM : (h + 1) * HEAD_DIM], pt))
    ct = jnp.concatenate(parts, axis=0).astype(BF)
    cto[...] = ct
    split_out(tn(ct, wo[0]), scr, pa, pb)


def attn_fwd(layer, xa, xb, wq, wk, wv, wo, bq, bv):
    rows, d = 2 * xa.shape[0], xa.shape[1]
    hd = wq.shape[1]
    outs = [
        sds((rows // 2, d), BF),
        sds((rows // 2, d), BF),
        sds((rows, d), BF),
        sds((rows, hd), BF),
        sds((rows, hd), BF),
        sds((rows, hd), BF),
        sds((hd, rows), BF),
        sds((hd, rows), BF),
    ]
    return call(
        functools.partial(attn_fwd_kernel, layer=layer),
        [(xa, None), (xb, None)]
        + [(w, layer) for w in (wq, wk, wv, wo)]
        + [(bq, None), (bv, None)],
        outs,
        [pltpu.VMEM((rows, d), F32)],
        flops=2 * rows * hd * (5 * d + 2 * rows),
        name="attn_fwd",
    )


def attn_bwd_kernel(
    who, b_in, q, k, v, kt, wq, wk, wv, wo, marks, pa, pb, bc, dqt, dk, dv, sbq, sbv, smask, scr
):
    b = arrange(who, b_in, scr, bc)
    cg = nt(b, wo[0]).astype(BF)
    qv, kv, vv, ktv = q[...], k[...], v[...], kt[...]
    width = qv.shape[1]
    scale = HEAD_DIM ** (-0.5)
    dqs = []
    dk32 = jnp.zeros(qv.shape, F32)
    dv32 = jnp.zeros(qv.shape, F32)
    for h in range(width // HEAD_DIM):
        mask = head_mask(width, h)
        p = soft(kv, qv, h)
        dp = nt(vv, cg * mask.astype(BF))
        dsum = jnp.sum(p * dp, axis=0, keepdims=True)
        ds = (p * (dp - dsum)).astype(BF)
        dqs.append(nn(ktv[h * HEAD_DIM : (h + 1) * HEAD_DIM], ds))
        dk32 = dk32 + nn(ds, qv) * (mask * scale)
        dv32 = dv32 + nn(p.astype(BF), cg) * mask
    dqtv = (jnp.concatenate(dqs, axis=0) * scale).astype(BF)
    dkv = dk32.astype(BF)
    dvv = dv32.astype(BF)
    dqt[...] = dqtv
    dk[...] = dkv
    dv[...] = dvv
    sbq[...] = jnp.sum(dqtv.astype(F32).T, axis=0, keepdims=True)
    sbv[...] = jnp.sum(dvv.astype(F32), axis=0, keepdims=True)
    total = tn(dqtv, wq[0]) + nn(dkv, wk[0]) + nn(dvv, wv[0])
    smask[...] = jnp.sum(total * marks[:, :1].astype(F32), axis=0, keepdims=True)
    split_out(total, scr, pa, pb)


def attn_bwd(who, layer, b, q, k, v, kt, marks, wq, wk, wv, wo):
    rows, d = b.shape
    hd = wq.shape[1]
    outs = [
        sds((rows // 2, d), BF),
        sds((rows // 2, d), BF),
        sds((rows, d), BF),
        sds((hd, rows), BF),
        sds((rows, hd), BF),
        sds((rows, hd), BF),
        sds((1, hd), F32),
        sds((1, hd), F32),
        sds((1, d), F32),
    ]
    return call(
        attn_bwd_kernel,
        [(who, "smem"), (b, None), (q, None), (k, None), (v, None), (kt, None)]
        + [(w, layer) for w in (wq, wk, wv, wo)]
        + [(marks, None)],
        outs,
        [pltpu.VMEM((rows, d), F32)],
        flops=2 * rows * hd * (4 * d + 5 * rows),
        name="attn_bwd",
    )


def ffn_fwd_kernel(ya, yb, wu, wd, bu, pa, pb, yc, hid, slo, scr, *, layer):
    pre = nn(join(ya, yb, scr, yc), wu[0]) + bu[layer : layer + 1, :].astype(F32)
    phi = 0.5 * (1.0 + lax.erf(pre * 0.7071067811865476))
    hidden = (pre * phi).astype(BF)
    hid[...] = hidden
    slo[...] = (phi + pre * jnp.exp(-0.5 * pre * pre) * 0.3989422804014327).astype(BF)
    split_out(nn(hidden, wd[0]), scr, pa, pb)


def ffn_fwd(layer, ya, yb, wu, wd, bu):
    rows, d = 2 * ya.shape[0], ya.shape[1]
    ff = wu.shape[2]
    outs = [
        sds((rows // 2, d), BF),
        sds((rows // 2, d), BF),
        sds((rows, d), BF),
        sds((rows, ff), BF),
        sds((rows, ff), BF),
    ]
    return call(
        functools.partial(ffn_fwd_kernel, layer=layer),
        [(ya, None), (yb, None), (wu, layer), (wd, layer), (bu, None)],
        outs,
        [pltpu.VMEM((rows, d), F32)],
        flops=4 * rows * d * ff,
        name="ffn_fwd",
    )


def ffn_bwd_kernel(who, d_in, slo, wu, wd, pa, pb, dc, act_o, sbu, scr):
    act = (nt(arrange(who, d_in, scr, dc), wd[0]) * slo[...].astype(F32)).astype(BF)
    act_o[...] = act
    sbu[...] = jnp.sum(act.astype(F32), axis=0, keepdims=True)
    split_out(nt(act, wu[0]), scr, pa, pb)


def ffn_bwd(who, layer, d_in, slo, wu, wd):
    rows, d = d_in.shape
    ff = wu.shape[2]
    outs = [
        sds((rows // 2, d), BF),
        sds((rows // 2, d), BF),
        sds((rows, d), BF),
        sds((rows, ff), BF),
        sds((1, ff), F32),
    ]
    return call(
        ffn_bwd_kernel,
        [(who, "smem"), (d_in, None), (slo, None), (wu, layer), (wd, layer)],
        outs,
        [pltpu.VMEM((rows, d), F32)],
        flops=4 * rows * d * ff,
        name="ffn_bwd",
    )


def put_halves(bits, pick, scr, send, keep):
    half = keep.shape[0]
    bit = bits[pick]
    keep[...] = scr[pl.ds(pl.multiple_of(bit * half, 16), half), :]
    send[...] = scr[pl.ds(pl.multiple_of((1 - bit) * half, 16), half), :]


def pair_wgrad_kernel(bits, al, ar, bl, br, send, keep, scr, *, pick):
    scr[...] = (tn(al[...], bl[...]) + tn(ar[...], br[...])).astype(BF)
    put_halves(bits, pick, scr, send, keep)


def pair_wgrad(bits, pick, a, b, name):
    rows, m = a[0].shape
    n = b[0].shape[1]
    return call(
        functools.partial(pair_wgrad_kernel, pick=pick),
        [(bits, "smem")] + [(v, None) for v in (*a, *b)],
        [sds((m // 2, n), BF)] * 2,
        [pltpu.VMEM((m, n), BF)],
        flops=4 * rows * m * n,
        name=name,
    )


def attn_wgrad_kernel(
    bits, xl, xr, dqtl, dqtr, dkl, dkr, dvl, dvr, ctl, ctr, bl, br, send, keep, scr, *, pick
):
    hd = scr.shape[0] // 4
    scr[:hd] = (nn(dqtl[...], xl[...]) + nn(dqtr[...], xr[...])).astype(BF)
    scr[hd : 2 * hd] = (tn(dkl[...], xl[...]) + tn(dkr[...], xr[...])).astype(BF)
    scr[2 * hd : 3 * hd] = (tn(dvl[...], xl[...]) + tn(dvr[...], xr[...])).astype(BF)
    scr[3 * hd :] = (nn(ctl[...], bl[...]) + nn(ctr[...], br[...])).astype(BF)
    put_halves(bits, pick, scr, send, keep)


def attn_wgrad(bits, pick, hd, *values):
    rows, dim = values[0].shape
    return call(
        functools.partial(attn_wgrad_kernel, pick=pick),
        [(bits, "smem")] + [(v, None) for v in values],
        [sds((2 * hd, dim), BF)] * 2,
        [pltpu.VMEM((4 * hd, dim), BF)],
        flops=16 * rows * dim * hd,
        name="attn_wgrad",
    )


def attn_wgrad_two_kernel(
    bits, xl, xr, dqtl, dqtr, dkl, dkr, dvl, dvr, ctl, ctr, bl, br, sd, kd, su, ku, sc_d, sc_u
):
    hd = sc_d.shape[0] // 2
    sc_d[:hd] = (nn(dqtl[...], xl[...]) + nn(dqtr[...], xr[...])).astype(BF)
    sc_d[hd:] = (tn(dkl[...], xl[...]) + tn(dkr[...], xr[...])).astype(BF)
    put_halves(bits, 0, sc_d, sd, kd)
    sc_u[:hd] = (tn(dvl[...], xl[...]) + tn(dvr[...], xr[...])).astype(BF)
    sc_u[hd:] = (nn(ctl[...], bl[...]) + nn(ctr[...], br[...])).astype(BF)
    put_halves(bits, 1, sc_u, su, ku)


def attn_wgrad_two(bits, hd, *values):
    rows, dim = values[0].shape
    return call(
        attn_wgrad_two_kernel,
        [(bits, "smem")] + [(v, None) for v in values],
        [sds((hd, dim), BF)] * 4,
        [pltpu.VMEM((2 * hd, dim), BF)] * 2,
        flops=16 * rows * dim * hd,
        name="attn_wgrad",
    )


def place_two_kernel(bits, mine, by_low, by_high, down_far, up_far, *outs):
    size = down_far.shape[0]
    low, high = bits[0], bits[1]
    parts = [
        (low, high, mine, mine),
        (1 - low, high, by_low, by_low),
        (low, 1 - high, by_high, by_high),
        (1 - low, 1 - high, down_far, up_far),
    ]
    for l, h, ref_down, ref_up in parts:

        def put_down(spot, ref=ref_down):
            at = (spot % 2) * size
            outs[spot // 2][0, at : at + size, :] = ref[:size, :].astype(F32)

        def put_up(spot, ref=ref_up):
            at = (spot % 2) * size
            outs[2 + spot // 2][0, at : at + size, :] = ref[ref.shape[0] - size :, :].astype(F32)

        when_at(l, h, put_down)
        when_at(h, l, put_up)


def small_kernel(*refs, layers, hd):
    out = refs[-1]
    width = out.shape[1]
    zeros = jnp.zeros((8, width), F32)
    rows = []
    for l in range(layers):
        sql, sqr, svl, svr, sul, sur, own_a, own_f, sma, smb = refs[10 * l : 10 * l + 10]
        heads = [sql[...] + sqr[...], svl[...] + svr[...], zeros[:1, : width - 2 * hd]]
        mask_row = own_a[3:4] + sma[...] + smb[...] if l == 0 else zeros[:1]
        rows += [own_a[:3], own_f[:3], mask_row, zeros[:1]]
        rows += [jnp.concatenate(heads, axis=1), sul[...] + sur[...], zeros[:6]]
    out[...] = jnp.concatenate(rows, axis=0)


def small_rows(values, hd):
    layers = len(values)
    dim = values[0][6].shape[1]
    return call(
        functools.partial(small_kernel, layers=layers, hd=hd),
        [(v, None) for vs in values for v in vs],
        [sds((16 * layers, dim), F32)],
        name="small_rows",
    )[0]


def small_mp_kernel(have, got, out):
    for l in range(have.shape[0] // 16):
        out[16 * l : 16 * l + 8, :] = have[16 * l : 16 * l + 8, :] + got[16 * l : 16 * l + 8, :]
        out[16 * l + 8 : 16 * l + 16, :] = have[16 * l + 8 : 16 * l + 16, :]


def small_dp_kernel(have, got, out):
    out[...] = have[...] + got[...]


def small_add(have, got, over_mp):
    return call(
        small_mp_kernel if over_mp else small_dp_kernel,
        [(have, None), (got, None)],
        [sds(have.shape, F32)],
        name="small_add",
    )[0]


def halve_kernel(bits, have, got, send, keep, *, pick):
    half = keep.shape[0]
    bit = bits[pick]
    mine = pl.ds(pl.multiple_of(bit * half, 16), half)
    other = pl.ds(pl.multiple_of((1 - bit) * half, 16), half)
    keep[...] = (have[mine, :].astype(F32) + got[mine, :].astype(F32)).astype(BF)
    send[...] = (have[other, :].astype(F32) + got[other, :].astype(F32)).astype(BF)


def halve(bits, pick, have, got):
    rows, dim = have.shape
    return call(
        functools.partial(halve_kernel, pick=pick),
        [(bits, "smem"), (have, None), (got, None)],
        [sds((rows // 2, dim), BF)] * 2,
        name="halve",
    )


def add_kernel(a, b, o):
    o[...] = (a[...].astype(F32) + b[...].astype(F32)).astype(BF)


def add(a, b):
    return call(add_kernel, [(a, None), (b, None)], [sds(a.shape, BF)], name="add")[0]


def stacked_call(kernel, bits, parts, outs, layer, layers, old, name):
    dim = parts[0].shape[1]
    old = [] if old is None else list(old)
    shapes = [sds((layers, rows, dim), F32) for rows in outs]
    specs = [pl.BlockSpec((1, rows, dim), lambda i: (layer, 0, 0)) for rows in outs]
    n = 1 + len(parts)

    def body(*refs):
        kernel(*refs[:n], *refs[n + len(old) :])

    return ORDER.call(
        body,
        n + len(old),
        [bits, *parts, *old],
        mark=None,
        in_specs=[pl.BlockSpec(memory_space=pltpu.SMEM)]
        + [whole(q.shape) for q in parts]
        + [pl.BlockSpec(memory_space=pl.ANY)] * len(old),
        out_specs=specs,
        out_shape=shapes,
        input_output_aliases={n + i: i for i in range(len(old))},
        compiler_params=pltpu.CompilerParams(vmem_limit_bytes=VMEM_LIMIT),
        cost_estimate=pl.CostEstimate(flops=ORDER.span, bytes_accessed=1, transcendentals=0),
        name=name,
    )


def when_at(first, second, fn):
    for spot in range(4):

        @pl.when(2 * first + second == spot)
        def _(spot=spot):
            fn(spot)


def place_attn_kernel(bits, *refs, picks):
    parts, outs = refs[:4], refs[4:]
    for i, ref in enumerate(parts):
        first = bits[picks[0]] if i < 2 else 1 - bits[picks[0]]
        second = bits[picks[1]] if i % 2 == 0 else 1 - bits[picks[1]]

        def put(spot, ref=ref):
            outs[spot][0] = ref[...].astype(F32)

        when_at(first, second, put)


def place_attn(bits, picks, parts, layer, layers, old):
    return stacked_call(
        functools.partial(place_attn_kernel, picks=picks),
        bits,
        parts,
        [parts[0].shape[0]] * 4,
        layer,
        layers,
        old,
        "place_attn",
    )


def place_ffn_kernel(bits, mine, by_low, by_high, down_far, up_far, down, up):
    size = down_far.shape[0]
    low, high = bits[0], bits[1]
    parts = [
        (low, high, mine, mine),
        (1 - low, high, by_low, by_low),
        (low, 1 - high, by_high, by_high),
        (1 - low, 1 - high, down_far, up_far),
    ]
    for l, h, ref_down, ref_up in parts:

        def put_down(spot, ref=ref_down):
            down[0, spot * size : (spot + 1) * size, :] = ref[:size, :].astype(F32)

        def put_up(spot, ref=ref_up):
            up[0, spot * size : (spot + 1) * size, :] = ref[ref.shape[0] - size :, :].astype(F32)

        when_at(l, h, put_down)
        when_at(h, l, put_up)


def place_ffn(bits, parts, layer, layers, old):
    rows = 4 * parts[3].shape[0]
    return stacked_call(
        place_ffn_kernel, bits, parts, [rows] * 2, layer, layers, old, "place_ffn"
    )


def halve_two_kernel(bits, kd, gd, ku, gu, send_d, send_u, keep):
    size = send_d.shape[0]
    for have, got, send, pick, at in ((kd, gd, send_d, 1, 0), (ku, gu, send_u, 0, size)):
        bit = bits[pick]
        mine = pl.ds(pl.multiple_of(bit * size, 16), size)
        other = pl.ds(pl.multiple_of((1 - bit) * size, 16), size)
        keep[at : at + size, :] = (have[mine, :].astype(F32) + got[mine, :].astype(F32)).astype(BF)
        send[...] = (have[other, :].astype(F32) + got[other, :].astype(F32)).astype(BF)


def halve_two(bits, kd, gd, ku, gu):
    rows, dim = kd.shape
    return call(
        halve_two_kernel,
        [(bits, "smem"), (kd, None), (gd, None), (ku, None), (gu, None)],
        [sds((rows // 2, dim), BF), sds((rows // 2, dim), BF), sds((rows, dim), BF)],
        name="halve_two",
    )


def add_two_kernel(have, gd, gu, out):
    size = gd.shape[0]
    out[:size, :] = (have[:size, :].astype(F32) + gd[...].astype(F32)).astype(BF)
    out[size:, :] = (have[size:, :].astype(F32) + gu[...].astype(F32)).astype(BF)


def add_two(have, gd, gu):
    return call(
        add_two_kernel, [(have, None), (gd, None), (gu, None)], [sds(have.shape, BF)], name="add_two"
    )[0]


def cut_two_kernel(by_high, by_low, od, ou):
    size = od.shape[0]
    od[...] = by_high[:size, :]
    ou[...] = by_low[size:, :]


def cut_two(by_high, by_low):
    rows, dim = by_high.shape
    return call(
        cut_two_kernel,
        [(by_high, None), (by_low, None)],
        [sds((rows // 2, dim), BF)] * 2,
        name="cut_two",
    )


def swap_bit(v, size, pick):
    return lax.ppermute(v, "dp", [(i, i ^ (1 << pick)) for i in range(size)])


def copy_kernel(have, out):
    out[...] = have[...]


def gate(v):
    return call(copy_kernel, [(v, None)], [sds(v.shape, v.dtype)], name="gate")[0]


def merge_kernel(ffn, have, got, out):
    size = ffn.shape[0]
    out[:size, :] = ffn[...]
    out[size:, :] = (have[...].astype(F32) + got[...].astype(F32)).astype(BF)


def cut_merged_kernel(by_high, by_low, od, ou):
    size = ou.shape[0]
    od[:size, :] = by_high[:size, :]
    od[size:, :] = by_high[2 * size :, :]
    ou[...] = by_low[size : 2 * size, :]


def place_merged_kernel(bits, mine, by_low, by_high, down_far, up_far, down, up, *heads):
    size = up_far.shape[0]
    low, high = bits[0], bits[1]
    parts = [
        (low, high, mine, mine, mine, 2),
        (1 - low, high, by_low, by_low, by_low, 2),
        (low, 1 - high, by_high, by_high, by_high, 2),
        (1 - low, 1 - high, down_far, up_far, down_far, 1),
    ]
    for l, h, ref_down, ref_up, ref_head, at in parts:

        def put_down(spot, ref=ref_down, head=ref_head, at=at):
            down[0, spot * size : (spot + 1) * size, :] = ref[:size, :].astype(F32)
            heads[spot][0] = head[at * size : (at + 1) * size, :].astype(F32)

        def put_up(spot, ref=ref_up, at=at):
            up[0, spot * size : (spot + 1) * size, :] = ref[
                (at - 1) * size : at * size, :
            ].astype(F32)

        when_at(l, h, put_down)
        when_at(h, l, put_up)


class Merged:
    def __init__(self, ffn, attn):
        self.ffn, self.attn = ffn, attn

    def merge(self):
        ffn, attn = self.ffn, self.attn
        for i in range(len(attn.rest) - 1):
            attn.keep = add(attn.keep, attn.got)
            attn.got = attn.swap(attn.keep, attn.rest[i + 1])
        have, got = attn.keep, attn.got
        rows = ffn.keep.shape[0] + have.shape[0]
        self.keep = call(
            merge_kernel,
            [(ffn.keep, None), (have, None), (got, None)],
            [sds((rows, have.shape[1]), BF)],
            name="merge",
        )[0]
        self.by_high = ffn.swap(self.keep, 1)
        self.by_low = ffn.swap(self.keep, 0)

    def cut(self):
        rows, dim = self.keep.shape
        od, ou = call(
            cut_merged_kernel,
            [(self.by_high, None), (self.by_low, None)],
            [sds((2 * rows // 3, dim), BF), sds((rows // 3, dim), BF)],
            name="cut_merged",
        )
        self.down_far = self.ffn.swap(od, 0)
        self.up_far = self.ffn.swap(ou, 1)

    def place(self, bits, layer, layers):
        size = self.up_far.shape[0]
        parts = self.keep, self.by_low, self.by_high, self.down_far, self.up_far
        outs = [4 * size] * 2 + [size] * 4
        got = stacked_call(
            place_merged_kernel, bits, parts, outs, layer, layers, None, "place_merged"
        )
        return got[:2], got[2:]


class DpSum:
    def __init__(self, bits, size, picks):
        self.bits, self.size, self.picks = bits, size, picks
        self.rest = [p for p in range(size.bit_length() - 1) if p not in picks]

    def swap(self, v, pick):
        return swap_bit(v, self.size, pick)

    def start(self, fn, *values):
        send, self.keep = fn(self.bits, self.picks[0], *values)
        self.got = self.swap(send, self.picks[0])

    def halve(self):
        send, self.keep = halve(self.bits, self.picks[1], self.keep, self.got)
        self.got = self.swap(send, self.picks[1])

    def cross(self):
        self.keep = add(self.keep, self.got)
        if self.rest:
            self.got = self.swap(self.keep, self.rest[0])

    def total(self):
        for i in range(len(self.rest)):
            self.keep = add(self.keep, self.got)
            if i + 1 < len(self.rest):
                self.got = self.swap(self.keep, self.rest[i + 1])

    def hold(self):
        self.keep = gate(self.keep)

    def spread(self):
        self.near = self.swap(self.keep, self.picks[1])
        self.far = self.swap(self.keep, self.picks[0])

    def last(self):
        self.end = self.swap(self.near, self.picks[0])

    def parts(self):
        return self.keep, self.near, self.far, self.end


class FfnSum:
    def __init__(self, bits, size):
        self.bits, self.size = bits, size
        self.rest = range(2, size.bit_length() - 1)

    def swap(self, v, pick):
        return swap_bit(v, self.size, pick)

    def start(self, down, up):
        send, self.kd = pair_wgrad(self.bits, 0, down[:2], down[2:], "down_wgrad")
        self.gd = self.swap(send, 0)
        send, self.ku = pair_wgrad(self.bits, 1, up[:2], up[2:], "up_wgrad")
        self.gu = self.swap(send, 1)

    def halve(self):
        send_d, send_u, self.keep = halve_two(self.bits, self.kd, self.gd, self.ku, self.gu)
        self.gd = self.swap(send_d, 1)
        self.gu = self.swap(send_u, 0)

    def cross(self):
        self.keep = add_two(self.keep, self.gd, self.gu)
        if self.rest:
            self.got = self.swap(self.keep, self.rest[0])

    def total(self):
        for i in range(len(self.rest)):
            self.keep = add(self.keep, self.got)
            if i + 1 < len(self.rest):
                self.got = self.swap(self.keep, self.rest[i + 1])

    def hold(self):
        self.keep = gate(self.keep)

    def high(self):
        self.by_high = self.swap(self.keep, 1)

    def low(self):
        self.by_low = self.swap(self.keep, 0)

    def last(self):
        od, ou = cut_two(self.by_high, self.by_low)
        self.down_far = self.swap(od, 0)
        self.up_far = self.swap(ou, 1)

    def parts(self):
        return self.keep, self.by_low, self.by_high, self.down_far, self.up_far


class AttnSum(FfnSum):
    def start(self, fn, *values):
        sd, self.kd, su, self.ku = attn_wgrad_two(self.bits, values[0], *values[1:])
        self.gd = self.swap(sd, 0)
        self.gu = self.swap(su, 1)

    def place(self, layer, layers, old):
        parts = self.parts()
        rows = 2 * parts[3].shape[0]
        return stacked_call(
            place_two_kernel, self.bits, parts, [rows] * 4, layer, layers, old, "place_attn"
        )


def three(who, mine, pair, far):
    half = mine.shape[0]
    if pair.shape[0] == half:
        near = pair[...].astype(F32)
    else:
        near = jnp.where(who[0] == 0, pair[half:, :].astype(F32), pair[:half, :].astype(F32))
    return mine[...].astype(F32) + near + far[...].astype(F32)


def norm_fwd_kernel(near, far, res, bias, gain, shift, out, unit, inv, low, *, layer):
    row = slice(layer, layer + 1)
    r = res[...] + (near[...] + far[...].astype(F32)) + bias[row, :].astype(F32)
    mean = jnp.mean(r, axis=-1, keepdims=True)
    c = r - mean
    i = lax.rsqrt(jnp.mean(c * c, axis=-1, keepdims=True) + 1e-05)
    u = c * i
    o = u * gain[row, :].astype(F32) + shift[row, :].astype(F32)
    out[...] = o
    unit[...] = u
    inv[...] = i
    low[...] = o.astype(BF)


def norm_fwd(layer, parts, res, bias, gain, shift):
    rows, d = res.shape
    return call(
        functools.partial(norm_fwd_kernel, layer=layer),
        [(v, None) for v in (*parts, res, bias, gain, shift)],
        [sds((rows, d), F32), sds((rows, d), F32), sds((rows, 1), F32), sds((rows, d), BF)],
        name="norm_fwd",
        mark=3,
    )


def norm_bwd_core(up, unit, inv, gain, marks, resid, low, sums, layer):
    u = unit[...]
    e = up * gain[layer : layer + 1, :].astype(F32)
    r = inv[...] * (
        e - jnp.mean(e, axis=-1, keepdims=True) - u * jnp.mean(e * u, axis=-1, keepdims=True)
    )
    resid[...] = r
    lo = r.astype(BF)
    low[...] = lo
    sums[0:1, :] = jnp.sum(up * u, axis=0, keepdims=True)
    sums[1:2, :] = jnp.sum(up, axis=0, keepdims=True)
    sums[2:3, :] = jnp.sum(lo.astype(F32), axis=0, keepdims=True)
    sums[3:4, :] = jnp.sum(r * marks[...], axis=0, keepdims=True)


def norm_bwd_first_kernel(og, unit, inv, gain, marks, resid, low, sums, *, layer):
    up = og[...].astype(F32) * marks[...]
    norm_bwd_core(up, unit, inv, gain, marks, resid, low, sums, layer)


def norm_bwd_kernel(who, p0, p1, p2, res, unit, inv, gain, marks, resid, low, sums, *, layer):
    up = res[...] + three(who, p0, p1, p2)
    norm_bwd_core(up, unit, inv, gain, marks, resid, low, sums, layer)


def norm_bwd(who, layer, ins, unit, inv, gain, marks):
    rows, d = unit.shape
    first = len(ins) == 1
    return call(
        functools.partial(norm_bwd_first_kernel if first else norm_bwd_kernel, layer=layer),
        ([] if first else [(who, "smem")])
        + [(v, None) for v in (*ins, unit, inv, gain, marks)],
        [sds((rows, d), F32), sds((rows, d), BF), sds((4, d), F32)],
        name="norm_bwd",
        mark=1,
    )


def turn_kernel(near, far, res, bias, gain, shift, og, marks, hidden, resid, low, sums, *, layer):
    row = slice(layer, layer + 1)
    r = res[...] + (near[...] + far[...].astype(F32)) + bias[row, :].astype(F32)
    c = r - jnp.mean(r, axis=-1, keepdims=True)
    inv = lax.rsqrt(jnp.mean(c * c, axis=-1, keepdims=True) + 1e-05)
    unit = c * inv
    hidden[...] = (unit * gain[row, :].astype(F32) + shift[row, :].astype(F32)).astype(BF)
    up = og[...].astype(F32) * marks[...]
    norm_bwd_core(up, unit, inv, gain, marks, resid, low, sums, layer)


def norm_turn(layer, parts, res, bias, gain, shift, out_grad, marks):
    rows, d = res.shape
    return call(
        functools.partial(turn_kernel, layer=layer),
        [(v, None) for v in (*parts, res, bias, gain, shift, out_grad, marks)],
        [sds((rows, d), BF), sds((rows, d), F32), sds((rows, d), BF), sds((4, d), F32)],
        name="norm_turn",
        mark=2,
    )


def last_kernel(who, p0, p1, p2, res, marks, out):
    out[...] = (res[...] + three(who, p0, p1, p2)) * (1.0 - marks[...])


def last_rows(who, parts, res, marks):
    return call(
        last_kernel,
        [(who, "smem")] + [(v, None) for v in (*parts, res, marks)],
        [sds(res.shape, F32)],
        name="last_rows",
        mark=None,
    )[0]


FFN, ATTN, BOTH, SMALL, ROWS = range(5)
ATTN_PICKS = (0, 1)
PLAN = {
    ("ffn_far", False): [(0, FFN, "start")],
    ("attn_near", False): [(0, FFN, "halve")],
    ("attn_far", False): [(0, ATTN, "start"), (0, FFN, "cross")],
    ("ffn_near", True): [(1, ATTN, "halve")],
    ("ffn_far", True): [(0, FFN, "start"), (1, ATTN, "cross"), (1, FFN, "total")],
    ("attn_near", True): [(0, FFN, "halve"), (1, BOTH, "merge")],
    ("attn_mid", True): [(0, FFN, "cross")],
    ("attn_far", True): [(0, ATTN, "start")],
}
TAIL = [
    (0, ROWS, ""),
    (0, SMALL, ""),
    (0, ATTN, "halve"),
    (0, SMALL, ""),
    (0, FFN, "total"),
    (0, SMALL, ""),
    (0, ATTN, "cross"),
    (1, BOTH, "cut"),
    (0, FFN, "high"),
    (0, FFN, "low"),
    (0, SMALL, ""),
    (1, BOTH, "place"),
    (0, ATTN, "total"),
    (0, ATTN, "spread"),
    (0, SMALL, ""),
    (0, FFN, "last"),
    (0, SMALL, ""),
    (0, ATTN, "last"),
    (0, FFN, "place"),
    (0, ATTN, "place"),
]
CORE = [(0, 1), (1, 0), (2, 3), (3, 2)]
CHIP = [(0, 2), (2, 0), (1, 3), (3, 1)]


def core(v):
    return lax.ppermute(v, "mp", CORE)


def chip(v):
    return lax.ppermute(v, "mp", CHIP)


def both_cores(v):
    return lax.all_gather(v, "mp", axis=0, tiled=True, axis_index_groups=[[0, 1], [2, 3]])


def join_kernel(who, mine, pair, out):
    half = mine.shape[0]
    theirs = jnp.where(who[0] == 0, pair[half:, :].astype(F32), pair[:half, :].astype(F32))
    out[...] = (mine[...].astype(F32) + theirs).astype(BF)


def gather_sum(who, local, remote):
    joined = call(
        join_kernel,
        [(who, "smem"), (remote[0], None), (both_cores(remote[1]), None)],
        [sds(remote[0].shape, BF)],
        name="join",
    )[0]
    return local[0], both_cores(local[1]), chip(joined)


def prep_kernel(frames, span, vector, stream, low, marks, wide):
    m = jnp.broadcast_to(span[...].astype(F32), (8, span.shape[1])).T[:, :1]
    value = frames[...].astype(F32) * (1.0 - m) + m * vector[...].astype(F32)
    stream[...] = value
    low[...] = value.astype(BF)
    marks[...] = m
    wide[...] = jnp.broadcast_to(m, wide.shape).astype(BF)


def prep(frames, span, vector):
    rows = frames.shape[0]
    return call(
        prep_kernel,
        [(frames, None), (span, None), (vector, None)],
        [sds(frames.shape, F32), sds(frames.shape, BF), sds((rows, 1), F32), sds((rows, 128), BF)],
        name="prep",
        mark=1,
    )


def pair_kernel(a, b, out):
    both = [a[...].astype(F32), b[...].astype(F32)]
    out[...] = jnp.concatenate(both, axis=0).astype(out.dtype)


def pair_rows(a, b):
    shape = (2 * a.shape[0], a.shape[1])
    return call(pair_kernel, [(a, None), (b, None)], [sds(shape, a.dtype)], name="pair_rows")[0]


def plus_kernel(a, b, out):
    out[...] = (a[...].astype(F32) + b[...].astype(F32)).astype(out.dtype)


def plus(a, b, dtype):
    return call(plus_kernel, [(a, None), (b, None)], [sds(a.shape, dtype)], name="plus")[0]


def per_device(
    frames,
    span_mask,
    mask_vector,
    w_query,
    b_query,
    w_key,
    w_value,
    b_value,
    w_out,
    b_out,
    attn_gain,
    attn_bias,
    w_up,
    b_up,
    w_down,
    b_down,
    ffn_gain,
    ffn_bias,
    out_grad,
):
    layers = w_query.shape[0]
    dim = frames.shape[1]
    size = lax.axis_size("dp")
    place_in_dp = lax.axis_index("dp")
    who = (lax.axis_index("mp") & 1).astype(jnp.int32)[None]
    bits = jnp.stack([(place_in_dp >> k) & 1 for k in range(size.bit_length() - 1)]).astype(jnp.int32)
    wq = jnp.swapaxes(w_query, 1, 2)
    wk = jnp.swapaxes(w_key, 1, 2)
    wv = jnp.swapaxes(w_value, 1, 2)
    ORDER.last, ORDER.span, ORDER.small = None, 2 * 10**10, True
    stream, low, marks, mark_rows = prep(frames, span_mask[None], mask_vector[None])
    records = []

    def both(fn, v, extra, jobs=None, later=None, light=False):
        far = chip(v)
        near = both_cores(gate(v))
        first = fn(near, *extra[0])
        if jobs:
            jobs()
        far = both_cores(far)
        if later and light:
            ORDER.span = 0
        second = fn(far, *extra[1])
        ORDER.span = SPAN
        if later:
            later()
        return [first, second]

    def forward(fn, v, marked=None):
        far = chip(v)
        first = fn(v, core(v))
        if marked is not None:
            mark_sides.extend(pair_rows(v, core(v)) for v in (marked, chip(marked)))
        near_sum = plus(first[0], core(first[1]), F32)
        second = fn(far, core(far))
        far_sum = chip(plus(second[0], core(second[1]), BF))
        return (near_sum, far_sum), [first[2:], second[2:]]

    mark_sides = []
    for l in range(layers):
        parts, att = forward(
            lambda *v: attn_fwd(l, *v, wq, wk, wv, w_out, b_query, b_value),
            low,
            None if l else mark_rows,
        )
        normed, unit_a, inv_a, low_a = norm_fwd(l, parts, stream, b_out, attn_gain, attn_bias)
        parts, ffn = forward(lambda *v: ffn_fwd(l, *v, w_up, w_down, b_up), low_a)
        if l < layers - 1:
            stream, unit_f, inv_f, low = norm_fwd(l, parts, normed, b_down, ffn_gain, ffn_bias)
        else:
            hidden_out, *turned = norm_turn(
                l, parts, normed, b_down, ffn_gain, ffn_bias, out_grad, marks
            )
            unit_f = inv_f = None
        records.append((att, ffn, unit_a, inv_a, unit_f, inv_f))
    ORDER.span, ORDER.small = SPAN, True
    sums = [None] * layers
    smalls = [None] * layers
    ins = None
    for l in reversed(range(layers)):
        att, ffn, unit_a, inv_a, unit_f, inv_f = records[l]
        sums[l] = [FfnSum(bits, size), DpSum(bits, size, ATTN_PICKS)]
        sums[l].append(Merged(*sums[l]))
        inputs = [None, None]

        def window(name):
            for ahead, which, step in PLAN.get((name, l == 0), ()):
                if l + ahead < layers:
                    group = sums[l + ahead][which]
                    if step == "start":
                        group.start(*inputs[which])
                    else:
                        getattr(group, step)()

        if l == layers - 1:
            resid_f, low_f, sums_f = turned
        else:
            resid_f, low_f, sums_f = norm_bwd(who, l, ins, unit_f, inv_f, ffn_gain, marks)
        back = both(
            lambda v, c: ffn_bwd(who, l, v, c, w_up, w_down),
            low_f,
            [(f[2],) for f in ffn],
            lambda: window("ffn_near"),
            lambda: window("ffn_mid"),
        )
        parts = gather_sum(who, back[0][:2], back[1][:2])
        inputs[FFN] = (
            [f[1] for f in ffn] + [b[2] for b in back],
            [f[0] for f in ffn] + [b[3] for b in back],
        )
        window("ffn_far")
        s_up = [b[4] for b in back]
        resid_a, low_a, sums_a = norm_bwd(
            who, l, (*parts, resid_f), unit_a, inv_a, attn_gain, marks
        )
        back = both(
            lambda v, *c: attn_bwd(who, l, v, *c, wq, wk, wv, w_out),
            low_a,
            [(*a[1:5], m) for a, m in zip(att, mark_sides)],
            lambda: window("attn_near"),
            lambda: window("attn_mid"),
            l == 0,
        )
        parts = gather_sum(who, back[0][:2], back[1][:2])
        values = [a[0] for a in att]
        for i in (3, 4, 5):
            values += [b[i] for b in back]
        values += [a[5] for a in att]
        values += [b[2] for b in back]
        smalls[l] = [b[i] for i in (6, 7) for b in back] + s_up
        smalls[l] += [sums_a, sums_f] + [b[8] for b in back]
        inputs[ATTN] = (
            lambda bi, p, *v: attn_wgrad(bi, p, wq.shape[1], *v),
            *values,
        )
        ORDER.span = 2 * SPAN if l == 0 else SPAN
        window("attn_far")
        ins = (*parts, resid_a)
    g_att = g_ffn = None
    small = small_got = None
    small_at = 0
    for ahead, which, step in TAIL:
        if ahead >= layers:
            continue
        if which == ROWS:
            frames_grad = last_rows(who, ins[:3], ins[3], marks)
            continue
        if which == SMALL:
            if small_at == 0:
                small = small_rows(smalls, wq.shape[1])
            else:
                small = small_add(small, small_got, small_at <= 2)
            if small_at < 2:
                small_got = (core, chip)[small_at](small)
            elif small_at < size.bit_length() + 1:
                small_got = swap_bit(small, size, small_at - 2)
            small_at += 1
            continue
        group = sums[ahead][which]
        if step != "place":
            getattr(group, step)()
        elif which == BOTH:
            g_ffn, g_att = group.place(bits, ahead, layers)
        elif which == FFN:
            g_ffn = place_ffn(bits, group.parts(), ahead, layers, g_ffn)
        else:
            g_att = place_attn(bits, ATTN_PICKS, group.parts(), ahead, layers, g_att)
    while small_at < size.bit_length() + 2:
        small = small_add(small, small_got, small_at <= 2)
        if small_at < size.bit_length() + 1:
            small_got = swap_bit(small, size, small_at - 2)
        small_at += 1
    g_down, g_up = g_ffn
    small = small.reshape(layers, 16, dim)
    common = small[:, :8]
    heads = small[:, 8]
    hd = wq.shape[1]

    def swapped(i):
        return jnp.swapaxes(g_att[i], 1, 2)

    return (
        hidden_out,
        frames_grad,
        common[0, 6],
        swapped(0),
        heads[:, :hd],
        swapped(1),
        swapped(2),
        heads[:, hd : 2 * hd],
        g_att[3],
        common[:, 2],
        common[:, 0],
        common[:, 1],
        g_up,
        small[:, 9],
        g_down,
        common[:, 5],
        common[:, 3],
        common[:, 4],
    )


def solution(mesh):
    rows = P(("dp", "mp"), None)
    cols = P(None, None, "mp")
    units = P(None, "mp", None)
    vec = P(None, "mp")
    return jax.shard_map(
        per_device,
        mesh=mesh,
        in_specs=(
            rows, P(("dp", "mp")), P(), cols, vec, cols, cols, vec, units, P(), P(), P(),
            cols, vec, units, P(), P(), P(), rows,
        ),
        out_specs=(
            rows, rows, P(), cols, vec, cols, cols, vec, units, P(), P(), P(),
            cols, vec, units, P(), P(), P(),
        ),
        check_vma=False,
    )
```

```python
import functools
import math
import jax
import jax.numpy as jnp
from jax import lax
from jax.experimental import pallas as pl
from jax.experimental.pallas import tpu as pltpu
from jax.sharding import PartitionSpec as P

HEAD_DIM = 64
CLIP = 368
BF = jnp.bfloat16
F32 = jnp.float32
SPAN = 8 * 10**9
LONG = 10**12
VMEM_LIMIT = 32 * 1024 * 1024


def nn(a, b):
    return lax.dot_general(a, b, (((1,), (0,)), ((), ())), preferred_element_type=F32)


def nt(a, b):
    return lax.dot_general(a, b, (((1,), (1,)), ((), ())), preferred_element_type=F32)


def tn(a, b):
    return lax.dot_general(a, b, (((0,), (0,)), ((), ())), preferred_element_type=F32)


def whole(shape):
    zeros = (0,) * len(shape)
    return pl.BlockSpec(tuple(shape), lambda i: zeros)


def at_layer(shape, layer):
    rest = (0,) * (len(shape) - 1)
    return pl.BlockSpec((1,) + tuple(shape[1:]), lambda i: (layer,) + rest)


def sds(shape, dtype):
    return jax.ShapeDtypeStruct(shape, dtype)


def kept(shape, dtype):
    return pltpu.HBM(shape, dtype)


class Order:
    def __init__(self):
        self.last = None
        self.span = SPAN
        self.small = True

    def call(self, body, count, args, mark=0, **given):
        anywhere = pl.BlockSpec(memory_space=pl.ANY)
        given["in_specs"] = list(given["in_specs"])
        if self.last is not None:
            given["in_specs"].append(anywhere)
            args = [*args, self.last]
        extra = mark is None
        if extra:
            given["out_specs"] = [*given["out_specs"], anywhere]
            given["out_shape"] = [*given["out_shape"], sds((8, 128), F32)]
        n = len(given["out_shape"])

        def kernel(*refs):
            outs = refs[len(args) : len(args) + n - extra]
            body(*refs[:count], *outs, *refs[len(args) + n :])

        out = pl.pallas_call(kernel, grid=(1,), **given)(*args)
        self.last = out[-1 if extra else mark]
        return out[: n - extra]


ORDER = Order()


def call(kernel, ins, outs, scratch=(), flops=0, name=None, mark=0):
    specs = [
        pl.BlockSpec(memory_space=pltpu.SMEM)
        if l == "smem"
        else whole(a.shape)
        if l is None
        else at_layer(a.shape, l)
        for a, l in ins
    ]
    nbytes = sum(
        (a.size // a.shape[0] if isinstance(l, int) else a.size) * a.dtype.itemsize for a, l in ins
    ) + sum(math.prod(o.shape) * o.dtype.itemsize for o in outs)
    return ORDER.call(
        kernel,
        len(ins),
        [a for a, _ in ins],
        mark=mark,
        in_specs=specs,
        out_specs=[whole(o.shape) for o in outs],
        out_shape=outs,
        scratch_shapes=list(scratch),
        compiler_params=pltpu.CompilerParams(vmem_limit_bytes=VMEM_LIMIT),
        cost_estimate=pl.CostEstimate(
            flops=max(flops, ORDER.span), bytes_accessed=nbytes, transcendentals=0
        ),
        name=name,
    )


def join(a_ref, b_ref, scratch, joined):
    half = a_ref.shape[0]
    scratch[:half] = a_ref[...].astype(F32)
    scratch[half:] = b_ref[...].astype(F32)
    value = scratch[...].astype(BF)
    joined[...] = value
    return value


def arrange(who, pair, scratch, arranged):
    half = pair.shape[0] // 2
    scratch[...] = pair[...].astype(F32)
    at = pl.multiple_of(who[0] * half, 8)
    both = [scratch[pl.ds(at, half), :], scratch[pl.ds(half - at, half), :]]
    value = jnp.concatenate(both, axis=0).astype(BF)
    arranged[...] = value
    return value


def split_out(value, scratch, oa, ob):
    half = oa.shape[0]
    scratch[...] = value
    oa[...] = scratch[:half].astype(BF)
    ob[...] = scratch[half:].astype(BF)


def head_mask(width, head):
    cols = lax.broadcasted_iota(jnp.int32, (1, width), 1)
    return (cols // HEAD_DIM == head).astype(F32)


def soft(k, q, head):
    mask = (head_mask(q.shape[1], head) * HEAD_DIM ** (-0.5)).astype(BF)
    s = nt(k, q * mask)
    e = jnp.exp(s - jnp.max(s, axis=0, keepdims=True))
    return e * (1.0 / jnp.sum(e, axis=0, keepdims=True))


def attn_fwd_kernel(
    xa, xb, wq, wk, wv, wo, bq, bv, pa, pb, xc, qo, ko, vo, kto, cto, scr, *, layer
):
    x = join(xa, xb, scr, xc)
    q = (nt(x, wq[0]) + bq[layer : layer + 1, :].astype(F32)).astype(BF)
    k = nt(x, wk[0]).astype(BF)
    kto[...] = nt(wk[0], x).astype(BF)
    v32 = nt(x, wv[0]) + bv[layer : layer + 1, :].astype(F32)
    v = v32.astype(BF)
    vt = v32.T.astype(BF)
    qo[...] = q
    ko[...] = k
    vo[...] = v
    parts = []
    for h in range(q.shape[1] // HEAD_DIM):
        pt = soft(k, q, h).astype(BF)
        parts.append(nn(vt[h * HEAD_DIM : (h + 1) * HEAD_DIM], pt))
    ct = jnp.concatenate(parts, axis=0).astype(BF)
    cto[...] = ct
    split_out(tn(ct, wo[0]), scr, pa, pb)


def attn_fwd(layer, xa, xb, wq, wk, wv, wo, bq, bv):
    rows, d = 2 * xa.shape[0], xa.shape[1]
    hd = wq.shape[1]
    outs = [
        sds((rows // 2, d), BF),
        sds((rows // 2, d), BF),
        sds((rows, d), BF),
        sds((rows, hd), BF),
        sds((rows, hd), BF),
        sds((rows, hd), BF),
        sds((hd, rows), BF),
        sds((hd, rows), BF),
    ]
    return call(
        functools.partial(attn_fwd_kernel, layer=layer),
        [(xa, None), (xb, None)]
        + [(w, layer) for w in (wq, wk, wv, wo)]
        + [(bq, None), (bv, None)],
        outs,
        [pltpu.VMEM((rows, d), F32)],
        flops=2 * rows * hd * (5 * d + 2 * rows),
        name="attn_fwd",
    )


def attn_bwd_kernel(
    who, b_in, q, k, v, kt, wq, wk, wv, wo, marks, pa, pb, bc, dqt, dk, dv, sbq, sbv, smask, scr
):
    b = arrange(who, b_in, scr, bc)
    cg = nt(b, wo[0]).astype(BF)
    qv, kv, vv, ktv = q[...], k[...], v[...], kt[...]
    width = qv.shape[1]
    scale = HEAD_DIM ** (-0.5)
    dqs = []
    dk32 = jnp.zeros(qv.shape, F32)
    dv32 = jnp.zeros(qv.shape, F32)
    for h in range(width // HEAD_DIM):
        mask = head_mask(width, h)
        p = soft(kv, qv, h)
        dp = nt(vv, cg * mask.astype(BF))
        dsum = jnp.sum(p * dp, axis=0, keepdims=True)
        ds = (p * (dp - dsum)).astype(BF)
        dqs.append(nn(ktv[h * HEAD_DIM : (h + 1) * HEAD_DIM], ds))
        dk32 = dk32 + nn(ds, qv) * (mask * scale)
        dv32 = dv32 + nn(p.astype(BF), cg) * mask
    dqtv = (jnp.concatenate(dqs, axis=0) * scale).astype(BF)
    dkv = dk32.astype(BF)
    dvv = dv32.astype(BF)
    dqt[...] = dqtv
    dk[...] = dkv
    dv[...] = dvv
    sbq[...] = jnp.sum(dqtv.astype(F32).T, axis=0, keepdims=True)
    sbv[...] = jnp.sum(dvv.astype(F32), axis=0, keepdims=True)
    total = tn(dqtv, wq[0]) + nn(dkv, wk[0]) + nn(dvv, wv[0])
    smask[...] = jnp.sum(total * marks[:, :1].astype(F32), axis=0, keepdims=True)
    split_out(total, scr, pa, pb)


def attn_bwd(who, layer, b, q, k, v, kt, marks, wq, wk, wv, wo):
    rows, d = b.shape
    hd = wq.shape[1]
    outs = [
        sds((rows // 2, d), BF),
        sds((rows // 2, d), BF),
        sds((rows, d), BF),
        sds((hd, rows), BF),
        sds((rows, hd), BF),
        sds((rows, hd), BF),
        sds((1, hd), F32),
        sds((1, hd), F32),
        sds((1, d), F32),
    ]
    return call(
        attn_bwd_kernel,
        [(who, "smem"), (b, None), (q, None), (k, None), (v, None), (kt, None)]
        + [(w, layer) for w in (wq, wk, wv, wo)]
        + [(marks, None)],
        outs,
        [pltpu.VMEM((rows, d), F32)],
        flops=2 * rows * hd * (4 * d + 5 * rows),
        name="attn_bwd",
    )


def ffn_fwd_kernel(ya, yb, wu, wd, bu, pa, pb, yc, hid, slo, scr, *, layer):
    pre = nn(join(ya, yb, scr, yc), wu[0]) + bu[layer : layer + 1, :].astype(F32)
    phi = 0.5 * (1.0 + lax.erf(pre * 0.7071067811865476))
    hidden = (pre * phi).astype(BF)
    hid[...] = hidden
    slo[...] = (phi + pre * jnp.exp(-0.5 * pre * pre) * 0.3989422804014327).astype(BF)
    split_out(nn(hidden, wd[0]), scr, pa, pb)


def ffn_fwd(layer, ya, yb, wu, wd, bu):
    rows, d = 2 * ya.shape[0], ya.shape[1]
    ff = wu.shape[2]
    outs = [
        sds((rows // 2, d), BF),
        sds((rows // 2, d), BF),
        sds((rows, d), BF),
        sds((rows, ff), BF),
        sds((rows, ff), BF),
    ]
    return call(
        functools.partial(ffn_fwd_kernel, layer=layer),
        [(ya, None), (yb, None), (wu, layer), (wd, layer), (bu, None)],
        outs,
        [pltpu.VMEM((rows, d), F32)],
        flops=4 * rows * d * ff,
        name="ffn_fwd",
    )


def ffn_bwd_kernel(who, d_in, slo, wu, wd, pa, pb, dc, act_o, sbu, scr):
    act = (nt(arrange(who, d_in, scr, dc), wd[0]) * slo[...].astype(F32)).astype(BF)
    act_o[...] = act
    sbu[...] = jnp.sum(act.astype(F32), axis=0, keepdims=True)
    split_out(nt(act, wu[0]), scr, pa, pb)


def ffn_bwd(who, layer, d_in, slo, wu, wd):
    rows, d = d_in.shape
    ff = wu.shape[2]
    outs = [
        sds((rows // 2, d), BF),
        sds((rows // 2, d), BF),
        sds((rows, d), BF),
        sds((rows, ff), BF),
        sds((1, ff), F32),
    ]
    return call(
        ffn_bwd_kernel,
        [(who, "smem"), (d_in, None), (slo, None), (wu, layer), (wd, layer)],
        outs,
        [pltpu.VMEM((rows, d), F32)],
        flops=4 * rows * d * ff,
        name="ffn_bwd",
    )


def put_halves(bits, pick, scr, send, keep):
    half = keep.shape[0]
    bit = bits[pick]
    keep[...] = scr[pl.ds(pl.multiple_of(bit * half, 16), half), :]
    send[...] = scr[pl.ds(pl.multiple_of((1 - bit) * half, 16), half), :]


def pair_wgrad_kernel(bits, al, ar, bl, br, send, keep, scr, *, pick):
    scr[...] = (tn(al[...], bl[...]) + tn(ar[...], br[...])).astype(BF)
    put_halves(bits, pick, scr, send, keep)


def pair_wgrad(bits, pick, a, b, name):
    rows, m = a[0].shape
    n = b[0].shape[1]
    return call(
        functools.partial(pair_wgrad_kernel, pick=pick),
        [(bits, "smem")] + [(v, None) for v in (*a, *b)],
        [sds((m // 2, n), BF)] * 2,
        [pltpu.VMEM((m, n), BF)],
        flops=4 * rows * m * n,
        name=name,
    )


def attn_wgrad_kernel(
    bits, xl, xr, dqtl, dqtr, dkl, dkr, dvl, dvr, ctl, ctr, bl, br, send, keep, scr, *, pick
):
    hd = scr.shape[0] // 4
    scr[:hd] = (nn(dqtl[...], xl[...]) + nn(dqtr[...], xr[...])).astype(BF)
    scr[hd : 2 * hd] = (tn(dkl[...], xl[...]) + tn(dkr[...], xr[...])).astype(BF)
    scr[2 * hd : 3 * hd] = (tn(dvl[...], xl[...]) + tn(dvr[...], xr[...])).astype(BF)
    scr[3 * hd :] = (nn(ctl[...], bl[...]) + nn(ctr[...], br[...])).astype(BF)
    put_halves(bits, pick, scr, send, keep)


def attn_wgrad(bits, pick, hd, *values):
    rows, dim = values[0].shape
    return call(
        functools.partial(attn_wgrad_kernel, pick=pick),
        [(bits, "smem")] + [(v, None) for v in values],
        [sds((2 * hd, dim), BF)] * 2,
        [pltpu.VMEM((4 * hd, dim), BF)],
        flops=16 * rows * dim * hd,
        name="attn_wgrad",
    )


def attn_wgrad_two_kernel(
    bits, xl, xr, dqtl, dqtr, dkl, dkr, dvl, dvr, ctl, ctr, bl, br, sd, kd, su, ku, sc_d, sc_u
):
    hd = sc_d.shape[0] // 2
    sc_d[:hd] = (nn(dqtl[...], xl[...]) + nn(dqtr[...], xr[...])).astype(BF)
    sc_d[hd:] = (tn(dkl[...], xl[...]) + tn(dkr[...], xr[...])).astype(BF)
    put_halves(bits, 0, sc_d, sd, kd)
    sc_u[:hd] = (tn(dvl[...], xl[...]) + tn(dvr[...], xr[...])).astype(BF)
    sc_u[hd:] = (nn(ctl[...], bl[...]) + nn(ctr[...], br[...])).astype(BF)
    put_halves(bits, 1, sc_u, su, ku)


def attn_wgrad_two(bits, hd, *values):
    rows, dim = values[0].shape
    return call(
        attn_wgrad_two_kernel,
        [(bits, "smem")] + [(v, None) for v in values],
        [sds((hd, dim), BF)] * 4,
        [pltpu.VMEM((2 * hd, dim), BF)] * 2,
        flops=16 * rows * dim * hd,
        name="attn_wgrad",
    )


def place_two_kernel(bits, mine, by_low, by_high, down_far, up_far, *outs):
    size = down_far.shape[0]
    low, high = bits[0], bits[1]
    parts = [
        (low, high, mine, mine),
        (1 - low, high, by_low, by_low),
        (low, 1 - high, by_high, by_high),
        (1 - low, 1 - high, down_far, up_far),
    ]
    for l, h, ref_down, ref_up in parts:

        def put_down(spot, ref=ref_down):
            at = (spot % 2) * size
            outs[spot // 2][0, at : at + size, :] = ref[:size, :].astype(F32)

        def put_up(spot, ref=ref_up):
            at = (spot % 2) * size
            outs[2 + spot // 2][0, at : at + size, :] = ref[ref.shape[0] - size :, :].astype(F32)

        when_at(l, h, put_down)
        when_at(h, l, put_up)


def small_kernel(*refs, layers, hd):
    out = refs[-1]
    width = out.shape[1]
    zeros = jnp.zeros((8, width), F32)
    rows = []
    for l in range(layers):
        sql, sqr, svl, svr, sul, sur, own_a, own_f, sma, smb = refs[10 * l : 10 * l + 10]
        heads = [sql[...] + sqr[...], svl[...] + svr[...], zeros[:1, : width - 2 * hd]]
        mask_row = own_a[3:4] + sma[...] + smb[...] if l == 0 else zeros[:1]
        rows += [own_a[:3], own_f[:3], mask_row, zeros[:1]]
        rows += [jnp.concatenate(heads, axis=1), sul[...] + sur[...], zeros[:6]]
    out[...] = jnp.concatenate(rows, axis=0)


def small_rows(values, hd):
    layers = len(values)
    dim = values[0][6].shape[1]
    return call(
        functools.partial(small_kernel, layers=layers, hd=hd),
        [(v, None) for vs in values for v in vs],
        [sds((16 * layers, dim), F32)],
        name="small_rows",
    )[0]


def small_mp_kernel(have, got, out):
    for l in range(have.shape[0] // 16):
        out[16 * l : 16 * l + 8, :] = have[16 * l : 16 * l + 8, :] + got[16 * l : 16 * l + 8, :]
        out[16 * l + 8 : 16 * l + 16, :] = have[16 * l + 8 : 16 * l + 16, :]


def small_dp_kernel(have, got, out):
    out[...] = have[...] + got[...]


def small_add(have, got, over_mp):
    return call(
        small_mp_kernel if over_mp else small_dp_kernel,
        [(have, None), (got, None)],
        [sds(have.shape, F32)],
        name="small_add",
    )[0]


def halve_kernel(bits, have, got, send, keep, *, pick):
    half = keep.shape[0]
    bit = bits[pick]
    mine = pl.ds(pl.multiple_of(bit * half, 16), half)
    other = pl.ds(pl.multiple_of((1 - bit) * half, 16), half)
    keep[...] = (have[mine, :].astype(F32) + got[mine, :].astype(F32)).astype(BF)
    send[...] = (have[other, :].astype(F32) + got[other, :].astype(F32)).astype(BF)


def halve(bits, pick, have, got):
    rows, dim = have.shape
    return call(
        functools.partial(halve_kernel, pick=pick),
        [(bits, "smem"), (have, None), (got, None)],
        [sds((rows // 2, dim), BF)] * 2,
        name="halve",
    )


def add_kernel(a, b, o):
    o[...] = (a[...].astype(F32) + b[...].astype(F32)).astype(BF)


def add(a, b):
    return call(add_kernel, [(a, None), (b, None)], [sds(a.shape, BF)], name="add")[0]


def stacked_call(kernel, bits, parts, outs, layer, layers, old, name):
    dim = parts[0].shape[1]
    old = [] if old is None else list(old)
    shapes = [sds((layers, rows, dim), F32) for rows in outs]
    specs = [pl.BlockSpec((1, rows, dim), lambda i: (layer, 0, 0)) for rows in outs]
    n = 1 + len(parts)

    def body(*refs):
        kernel(*refs[:n], *refs[n + len(old) :])

    return ORDER.call(
        body,
        n + len(old),
        [bits, *parts, *old],
        mark=None,
        in_specs=[pl.BlockSpec(memory_space=pltpu.SMEM)]
        + [whole(q.shape) for q in parts]
        + [pl.BlockSpec(memory_space=pl.ANY)] * len(old),
        out_specs=specs,
        out_shape=shapes,
        input_output_aliases={n + i: i for i in range(len(old))},
        compiler_params=pltpu.CompilerParams(vmem_limit_bytes=VMEM_LIMIT),
        cost_estimate=pl.CostEstimate(flops=ORDER.span, bytes_accessed=1, transcendentals=0),
        name=name,
    )


def when_at(first, second, fn):
    for spot in range(4):

        @pl.when(2 * first + second == spot)
        def _(spot=spot):
            fn(spot)


def place_attn_kernel(bits, *refs, picks):
    parts, outs = refs[:4], refs[4:]
    for i, ref in enumerate(parts):
        first = bits[picks[0]] if i < 2 else 1 - bits[picks[0]]
        second = bits[picks[1]] if i % 2 == 0 else 1 - bits[picks[1]]

        def put(spot, ref=ref):
            outs[spot][0] = ref[...].astype(F32)

        when_at(first, second, put)


def place_attn(bits, picks, parts, layer, layers, old):
    return stacked_call(
        functools.partial(place_attn_kernel, picks=picks),
        bits,
        parts,
        [parts[0].shape[0]] * 4,
        layer,
        layers,
        old,
        "place_attn",
    )


def place_ffn_kernel(bits, mine, by_low, by_high, down_far, up_far, down, up):
    size = down_far.shape[0]
    low, high = bits[0], bits[1]
    parts = [
        (low, high, mine, mine),
        (1 - low, high, by_low, by_low),
        (low, 1 - high, by_high, by_high),
        (1 - low, 1 - high, down_far, up_far),
    ]
    for l, h, ref_down, ref_up in parts:

        def put_down(spot, ref=ref_down):
            down[0, spot * size : (spot + 1) * size, :] = ref[:size, :].astype(F32)

        def put_up(spot, ref=ref_up):
            up[0, spot * size : (spot + 1) * size, :] = ref[ref.shape[0] - size :, :].astype(F32)

        when_at(l, h, put_down)
        when_at(h, l, put_up)


def place_ffn(bits, parts, layer, layers, old):
    rows = 4 * parts[3].shape[0]
    return stacked_call(
        place_ffn_kernel, bits, parts, [rows] * 2, layer, layers, old, "place_ffn"
    )


def halve_two_kernel(bits, kd, gd, ku, gu, send_d, send_u, keep):
    size = send_d.shape[0]
    for have, got, send, pick, at in ((kd, gd, send_d, 1, 0), (ku, gu, send_u, 0, size)):
        bit = bits[pick]
        mine = pl.ds(pl.multiple_of(bit * size, 16), size)
        other = pl.ds(pl.multiple_of((1 - bit) * size, 16), size)
        keep[at : at + size, :] = (have[mine, :].astype(F32) + got[mine, :].astype(F32)).astype(BF)
        send[...] = (have[other, :].astype(F32) + got[other, :].astype(F32)).astype(BF)


def halve_two(bits, kd, gd, ku, gu):
    rows, dim = kd.shape
    return call(
        halve_two_kernel,
        [(bits, "smem"), (kd, None), (gd, None), (ku, None), (gu, None)],
        [sds((rows // 2, dim), BF), sds((rows // 2, dim), BF), sds((rows, dim), BF)],
        name="halve_two",
    )


def add_two_kernel(have, gd, gu, out):
    size = gd.shape[0]
    out[:size, :] = (have[:size, :].astype(F32) + gd[...].astype(F32)).astype(BF)
    out[size:, :] = (have[size:, :].astype(F32) + gu[...].astype(F32)).astype(BF)


def add_two(have, gd, gu):
    return call(
        add_two_kernel, [(have, None), (gd, None), (gu, None)], [sds(have.shape, BF)], name="add_two"
    )[0]


def cut_two_kernel(by_high, by_low, od, ou):
    size = od.shape[0]
    od[...] = by_high[:size, :]
    ou[...] = by_low[size:, :]


def cut_two(by_high, by_low):
    rows, dim = by_high.shape
    return call(
        cut_two_kernel,
        [(by_high, None), (by_low, None)],
        [sds((rows // 2, dim), BF)] * 2,
        name="cut_two",
    )


def swap_bit(v, size, pick):
    return lax.ppermute(v, "dp", [(i, i ^ (1 << pick)) for i in range(size)])


def copy_kernel(have, out):
    out[...] = have[...]


def gate(v):
    return call(copy_kernel, [(v, None)], [sds(v.shape, v.dtype)], name="gate")[0]


def merge_kernel(ffn, have, got, out):
    size = ffn.shape[0]
    out[:size, :] = ffn[...]
    out[size:, :] = (have[...].astype(F32) + got[...].astype(F32)).astype(BF)


def cut_merged_kernel(by_high, by_low, od, ou):
    size = ou.shape[0]
    od[:size, :] = by_high[:size, :]
    od[size:, :] = by_high[2 * size :, :]
    ou[...] = by_low[size : 2 * size, :]


def place_merged_kernel(bits, mine, by_low, by_high, down_far, up_far, down, up, *heads):
    size = up_far.shape[0]
    low, high = bits[0], bits[1]
    parts = [
        (low, high, mine, mine, mine, 2),
        (1 - low, high, by_low, by_low, by_low, 2),
        (low, 1 - high, by_high, by_high, by_high, 2),
        (1 - low, 1 - high, down_far, up_far, down_far, 1),
    ]
    for l, h, ref_down, ref_up, ref_head, at in parts:

        def put_down(spot, ref=ref_down, head=ref_head, at=at):
            down[0, spot * size : (spot + 1) * size, :] = ref[:size, :].astype(F32)
            heads[spot][0] = head[at * size : (at + 1) * size, :].astype(F32)

        def put_up(spot, ref=ref_up, at=at):
            up[0, spot * size : (spot + 1) * size, :] = ref[
                (at - 1) * size : at * size, :
            ].astype(F32)

        when_at(l, h, put_down)
        when_at(h, l, put_up)


class Merged:
    def __init__(self, ffn, attn):
        self.ffn, self.attn = ffn, attn

    def merge(self):
        ffn, attn = self.ffn, self.attn
        for i in range(len(attn.rest) - 1):
            attn.keep = add(attn.keep, attn.got)
            attn.got = attn.swap(attn.keep, attn.rest[i + 1])
        have, got = attn.keep, attn.got
        rows = ffn.keep.shape[0] + have.shape[0]
        self.keep = call(
            merge_kernel,
            [(ffn.keep, None), (have, None), (got, None)],
            [sds((rows, have.shape[1]), BF)],
            name="merge",
        )[0]
        self.by_high = ffn.swap(self.keep, 1)
        if self.whole:
            self.by_low = ffn.swap(self.keep, 0)

    whole = False

    def low(self):
        self.by_low = self.ffn.swap(gate(self.keep), 0)

    def cut(self):
        rows, dim = self.keep.shape
        od, ou = call(
            cut_merged_kernel,
            [(self.by_high, None), (self.by_low, None)],
            [sds((2 * rows // 3, dim), BF), sds((rows // 3, dim), BF)],
            name="cut_merged",
        )
        self.down_far = self.ffn.swap(od, 0)
        self.up_far = self.ffn.swap(ou, 1)

    def place(self, bits, layer, layers):
        size = self.up_far.shape[0]
        parts = self.keep, self.by_low, self.by_high, self.down_far, self.up_far
        outs = [4 * size] * 2 + [size] * 4
        got = stacked_call(
            place_merged_kernel, bits, parts, outs, layer, layers, None, "place_merged"
        )
        return got[:2], got[2:]


class DpSum:
    def __init__(self, bits, size, picks):
        self.bits, self.size, self.picks = bits, size, picks
        self.rest = [p for p in range(size.bit_length() - 1) if p not in picks]

    def swap(self, v, pick):
        return swap_bit(v, self.size, pick)

    def start(self, fn, *values):
        send, self.keep = fn(self.bits, self.picks[0], *values)
        self.got = self.swap(send, self.picks[0])

    def halve(self):
        send, self.keep = halve(self.bits, self.picks[1], self.keep, self.got)
        self.got = self.swap(send, self.picks[1])

    def cross(self):
        self.keep = add(self.keep, self.got)
        if self.rest:
            self.got = self.swap(self.keep, self.rest[0])

    def total(self):
        for i in range(len(self.rest)):
            self.keep = add(self.keep, self.got)
            if i + 1 < len(self.rest):
                self.got = self.swap(self.keep, self.rest[i + 1])

    def hold(self):
        self.keep = gate(self.keep)

    def spread(self):
        self.near = self.swap(self.keep, self.picks[1])
        self.far = self.swap(self.keep, self.picks[0])

    def last(self):
        self.end = self.swap(self.near, self.picks[0])

    def parts(self):
        return self.keep, self.near, self.far, self.end


class FfnSum:
    def __init__(self, bits, size):
        self.bits, self.size = bits, size
        self.rest = range(2, size.bit_length() - 1)

    def swap(self, v, pick):
        return swap_bit(v, self.size, pick)

    def start(self, down, up):
        send, self.kd = pair_wgrad(self.bits, 0, down[:2], down[2:], "down_wgrad")
        self.gd = self.swap(send, 0)
        send, self.ku = pair_wgrad(self.bits, 1, up[:2], up[2:], "up_wgrad")
        self.gu = self.swap(send, 1)

    def halve(self):
        send_d, send_u, self.keep = halve_two(self.bits, self.kd, self.gd, self.ku, self.gu)
        self.gd = self.swap(send_d, 1)
        self.gu = self.swap(send_u, 0)

    def cross(self):
        self.keep = add_two(self.keep, self.gd, self.gu)
        if self.rest:
            self.got = self.swap(self.keep, self.rest[0])

    def total(self):
        for i in range(len(self.rest)):
            self.keep = add(self.keep, self.got)
            if i + 1 < len(self.rest):
                self.got = self.swap(self.keep, self.rest[i + 1])

    def hold(self):
        self.keep = gate(self.keep)

    def high(self):
        self.by_high = self.swap(self.keep, 1)

    def low(self):
        self.by_low = self.swap(self.keep, 0)

    def last(self):
        od, ou = cut_two(self.by_high, self.by_low)
        self.down_far = self.swap(od, 0)
        self.up_far = self.swap(ou, 1)

    def parts(self):
        return self.keep, self.by_low, self.by_high, self.down_far, self.up_far


class AttnSum(FfnSum):
    def start(self, fn, *values):
        sd, self.kd, su, self.ku = attn_wgrad_two(self.bits, values[0], *values[1:])
        self.gd = self.swap(sd, 0)
        self.gu = self.swap(su, 1)

    def place(self, layer, layers, old):
        parts = self.parts()
        rows = 2 * parts[3].shape[0]
        return stacked_call(
            place_two_kernel, self.bits, parts, [rows] * 4, layer, layers, old, "place_attn"
        )


def three(who, mine, pair, far):
    half = mine.shape[0]
    if pair.shape[0] == half:
        near = pair[...].astype(F32)
    else:
        near = jnp.where(who[0] == 0, pair[half:, :].astype(F32), pair[:half, :].astype(F32))
    return mine[...].astype(F32) + near + far[...].astype(F32)


def norm_fwd_kernel(near, far, res, bias, gain, shift, out, unit, inv, low, *, layer):
    row = slice(layer, layer + 1)
    r = res[...] + (near[...] + far[...].astype(F32)) + bias[row, :].astype(F32)
    mean = jnp.mean(r, axis=-1, keepdims=True)
    c = r - mean
    i = lax.rsqrt(jnp.mean(c * c, axis=-1, keepdims=True) + 1e-05)
    u = c * i
    o = u * gain[row, :].astype(F32) + shift[row, :].astype(F32)
    out[...] = o
    unit[...] = u
    inv[...] = i
    low[...] = o.astype(BF)


def norm_fwd(layer, parts, res, bias, gain, shift):
    rows, d = res.shape
    return call(
        functools.partial(norm_fwd_kernel, layer=layer),
        [(v, None) for v in (*parts, res, bias, gain, shift)],
        [sds((rows, d), F32), sds((rows, d), F32), sds((rows, 1), F32), sds((rows, d), BF)],
        name="norm_fwd",
        mark=3,
    )


def norm_bwd_core(up, unit, inv, gain, marks, resid, low, sums, layer):
    u = unit[...]
    e = up * gain[layer : layer + 1, :].astype(F32)
    r = inv[...] * (
        e - jnp.mean(e, axis=-1, keepdims=True) - u * jnp.mean(e * u, axis=-1, keepdims=True)
    )
    resid[...] = r
    lo = r.astype(BF)
    low[...] = lo
    sums[0:1, :] = jnp.sum(up * u, axis=0, keepdims=True)
    sums[1:2, :] = jnp.sum(up, axis=0, keepdims=True)
    sums[2:3, :] = jnp.sum(lo.astype(F32), axis=0, keepdims=True)
    sums[3:4, :] = jnp.sum(r * marks[...], axis=0, keepdims=True)


def norm_bwd_first_kernel(og, unit, inv, gain, marks, resid, low, sums, *, layer):
    up = og[...].astype(F32) * marks[...]
    norm_bwd_core(up, unit, inv, gain, marks, resid, low, sums, layer)


def norm_bwd_kernel(who, p0, p1, p2, res, unit, inv, gain, marks, resid, low, sums, *, layer):
    up = res[...] + three(who, p0, p1, p2)
    norm_bwd_core(up, unit, inv, gain, marks, resid, low, sums, layer)


def norm_bwd(who, layer, ins, unit, inv, gain, marks):
    rows, d = unit.shape
    first = len(ins) == 1
    return call(
        functools.partial(norm_bwd_first_kernel if first else norm_bwd_kernel, layer=layer),
        ([] if first else [(who, "smem")])
        + [(v, None) for v in (*ins, unit, inv, gain, marks)],
        [sds((rows, d), F32), sds((rows, d), BF), sds((4, d), F32)],
        name="norm_bwd",
        mark=1,
    )


def turn_kernel(near, far, res, bias, gain, shift, og, marks, hidden, resid, low, sums, *, layer):
    row = slice(layer, layer + 1)
    r = res[...] + (near[...] + far[...].astype(F32)) + bias[row, :].astype(F32)
    c = r - jnp.mean(r, axis=-1, keepdims=True)
    inv = lax.rsqrt(jnp.mean(c * c, axis=-1, keepdims=True) + 1e-05)
    unit = c * inv
    hidden[...] = (unit * gain[row, :].astype(F32) + shift[row, :].astype(F32)).astype(BF)
    up = og[...].astype(F32) * marks[...]
    norm_bwd_core(up, unit, inv, gain, marks, resid, low, sums, layer)


def norm_turn(layer, parts, res, bias, gain, shift, out_grad, marks):
    rows, d = res.shape
    return call(
        functools.partial(turn_kernel, layer=layer),
        [(v, None) for v in (*parts, res, bias, gain, shift, out_grad, marks)],
        [sds((rows, d), BF), sds((rows, d), F32), sds((rows, d), BF), sds((4, d), F32)],
        name="norm_turn",
        mark=2,
    )


def last_kernel(who, p0, p1, p2, res, marks, out):
    out[...] = (res[...] + three(who, p0, p1, p2)) * (1.0 - marks[...])


def last_rows(who, parts, res, marks):
    return call(
        last_kernel,
        [(who, "smem")] + [(v, None) for v in (*parts, res, marks)],
        [sds(res.shape, F32)],
        name="last_rows",
        mark=None,
    )[0]


FFN, ATTN, BOTH, SMALL, ROWS = range(5)
ATTN_PICKS = (0, 1)
PLAN = {
    ("ffn_far", False): [(0, FFN, "start")],
    ("attn_near", False): [(0, FFN, "halve")],
    ("attn_far", False): [(0, ATTN, "start"), (0, FFN, "cross")],
    ("ffn_near", True): [(1, ATTN, "halve")],
    ("ffn_far", True): [(0, FFN, "start"), (1, ATTN, "cross"), (1, FFN, "total")],
    ("attn_near", True): [(0, FFN, "halve"), (1, BOTH, "merge")],
    ("attn_mid", True): [(0, FFN, "cross")],
    ("attn_far", True): [(0, ATTN, "start")],
}
TAIL = [
    (0, ROWS, ""),
    (0, SMALL, ""),
    (1, BOTH, "low"),
    (0, ATTN, "halve"),
    (0, SMALL, ""),
    (0, FFN, "total"),
    (0, FFN, "high"),
    (0, FFN, "low"),
    (0, ATTN, "cross"),
    (0, SMALL, ""),
    (1, BOTH, "cut"),
    (0, SMALL, ""),
    (0, ATTN, "total"),
    (0, ATTN, "spread"),
    (0, SMALL, ""),
    (0, FFN, "last"),
    (1, BOTH, "place"),
    (0, SMALL, ""),
    (0, ATTN, "last"),
    (0, FFN, "place"),
    (0, ATTN, "place"),
]
CORE = [(0, 1), (1, 0), (2, 3), (3, 2)]
CHIP = [(0, 2), (2, 0), (1, 3), (3, 1)]


def core(v):
    return lax.ppermute(v, "mp", CORE)


def chip(v):
    return lax.ppermute(v, "mp", CHIP)


def both_cores(v):
    return lax.all_gather(v, "mp", axis=0, tiled=True, axis_index_groups=[[0, 1], [2, 3]])


def join_kernel(who, mine, pair, out):
    half = mine.shape[0]
    theirs = jnp.where(who[0] == 0, pair[half:, :].astype(F32), pair[:half, :].astype(F32))
    out[...] = (mine[...].astype(F32) + theirs).astype(BF)


def gather_sum(who, local, remote):
    joined = call(
        join_kernel,
        [(who, "smem"), (remote[0], None), (both_cores(remote[1]), None)],
        [sds(remote[0].shape, BF)],
        name="join",
    )[0]
    return local[0], both_cores(local[1]), chip(joined)


def prep_kernel(frames, span, vector, stream, low, marks, wide):
    m = jnp.broadcast_to(span[...].astype(F32), (8, span.shape[1])).T[:, :1]
    value = frames[...].astype(F32) * (1.0 - m) + m * vector[...].astype(F32)
    stream[...] = value
    low[...] = value.astype(BF)
    marks[...] = m
    wide[...] = jnp.broadcast_to(m, wide.shape).astype(BF)


def prep(frames, span, vector):
    rows = frames.shape[0]
    return call(
        prep_kernel,
        [(frames, None), (span, None), (vector, None)],
        [sds(frames.shape, F32), sds(frames.shape, BF), sds((rows, 1), F32), sds((rows, 128), BF)],
        name="prep",
        mark=1,
    )


def pair_kernel(a, b, out):
    both = [a[...].astype(F32), b[...].astype(F32)]
    out[...] = jnp.concatenate(both, axis=0).astype(out.dtype)


def pair_rows(a, b):
    shape = (2 * a.shape[0], a.shape[1])
    return call(pair_kernel, [(a, None), (b, None)], [sds(shape, a.dtype)], name="pair_rows")[0]


def plus_kernel(a, b, out):
    out[...] = (a[...].astype(F32) + b[...].astype(F32)).astype(out.dtype)


def plus(a, b, dtype):
    return call(plus_kernel, [(a, None), (b, None)], [sds(a.shape, dtype)], name="plus")[0]


def per_device(
    frames,
    span_mask,
    mask_vector,
    w_query,
    b_query,
    w_key,
    w_value,
    b_value,
    w_out,
    b_out,
    attn_gain,
    attn_bias,
    w_up,
    b_up,
    w_down,
    b_down,
    ffn_gain,
    ffn_bias,
    out_grad,
):
    layers = w_query.shape[0]
    dim = frames.shape[1]
    size = lax.axis_size("dp")
    place_in_dp = lax.axis_index("dp")
    who = (lax.axis_index("mp") & 1).astype(jnp.int32)[None]
    bits = jnp.stack([(place_in_dp >> k) & 1 for k in range(size.bit_length() - 1)]).astype(jnp.int32)
    wq = jnp.swapaxes(w_query, 1, 2)
    wk = jnp.swapaxes(w_key, 1, 2)
    wv = jnp.swapaxes(w_value, 1, 2)
    ORDER.last, ORDER.span, ORDER.small = None, 2 * 10**10, True
    stream, low, marks, mark_rows = prep(frames, span_mask[None], mask_vector[None])
    records = []

    def both(fn, v, extra, jobs=None, later=None, light=False):
        far = chip(v)
        near = both_cores(gate(v))
        first = fn(near, *extra[0])
        if jobs:
            jobs()
        far = both_cores(far)
        if later and light:
            ORDER.span = 0
        second = fn(far, *extra[1])
        ORDER.span = SPAN
        if later:
            later()
        return [first, second]

    def forward(fn, v, marked=None):
        far = chip(v)
        first = fn(v, core(v))
        if marked is not None:
            mark_sides.extend(pair_rows(v, core(v)) for v in (marked, chip(marked)))
        near_sum = plus(first[0], core(first[1]), F32)
        second = fn(far, core(far))
        far_sum = chip(plus(second[0], core(second[1]), BF))
        return (near_sum, far_sum), [first[2:], second[2:]]

    mark_sides = []
    for l in range(layers):
        parts, att = forward(
            lambda *v: attn_fwd(l, *v, wq, wk, wv, w_out, b_query, b_value),
            low,
            None if l else mark_rows,
        )
        normed, unit_a, inv_a, low_a = norm_fwd(l, parts, stream, b_out, attn_gain, attn_bias)
        parts, ffn = forward(lambda *v: ffn_fwd(l, *v, w_up, w_down, b_up), low_a)
        if l < layers - 1:
            stream, unit_f, inv_f, low = norm_fwd(l, parts, normed, b_down, ffn_gain, ffn_bias)
        else:
            hidden_out, *turned = norm_turn(
                l, parts, normed, b_down, ffn_gain, ffn_bias, out_grad, marks
            )
            unit_f = inv_f = None
        records.append((att, ffn, unit_a, inv_a, unit_f, inv_f))
    ORDER.span, ORDER.small = SPAN, True
    sums = [None] * layers
    smalls = [None] * layers
    ins = None
    for l in reversed(range(layers)):
        att, ffn, unit_a, inv_a, unit_f, inv_f = records[l]
        sums[l] = [FfnSum(bits, size), DpSum(bits, size, ATTN_PICKS)]
        sums[l].append(Merged(*sums[l]))
        inputs = [None, None]

        def window(name):
            for ahead, which, step in PLAN.get((name, l == 0), ()):
                if l + ahead < layers:
                    group = sums[l + ahead][which]
                    if step == "start":
                        group.start(*inputs[which])
                    else:
                        getattr(group, step)()

        if l == layers - 1:
            resid_f, low_f, sums_f = turned
        else:
            resid_f, low_f, sums_f = norm_bwd(who, l, ins, unit_f, inv_f, ffn_gain, marks)
        back = both(
            lambda v, c: ffn_bwd(who, l, v, c, w_up, w_down),
            low_f,
            [(f[2],) for f in ffn],
            lambda: window("ffn_near"),
            lambda: window("ffn_mid"),
        )
        parts = gather_sum(who, back[0][:2], back[1][:2])
        inputs[FFN] = (
            [f[1] for f in ffn] + [b[2] for b in back],
            [f[0] for f in ffn] + [b[3] for b in back],
        )
        window("ffn_far")
        s_up = [b[4] for b in back]
        resid_a, low_a, sums_a = norm_bwd(
            who, l, (*parts, resid_f), unit_a, inv_a, attn_gain, marks
        )
        back = both(
            lambda v, *c: attn_bwd(who, l, v, *c, wq, wk, wv, w_out),
            low_a,
            [(*a[1:5], m) for a, m in zip(att, mark_sides)],
            lambda: window("attn_near"),
            lambda: window("attn_mid"),
            l == 0,
        )
        parts = gather_sum(who, back[0][:2], back[1][:2])
        values = [a[0] for a in att]
        for i in (3, 4, 5):
            values += [b[i] for b in back]
        values += [a[5] for a in att]
        values += [b[2] for b in back]
        smalls[l] = [b[i] for i in (6, 7) for b in back] + s_up
        smalls[l] += [sums_a, sums_f] + [b[8] for b in back]
        inputs[ATTN] = (
            lambda bi, p, *v: attn_wgrad(bi, p, wq.shape[1], *v),
            *values,
        )
        ORDER.span = 2 * SPAN if l == 0 else SPAN
        window("attn_far")
        ins = (*parts, resid_a)
    g_att = g_ffn = None
    small = small_got = None
    small_at = 0
    for ahead, which, step in TAIL:
        if ahead >= layers:
            continue
        if which == ROWS:
            frames_grad = last_rows(who, ins[:3], ins[3], marks)
            continue
        if which == SMALL:
            if small_at == 0:
                small = small_rows(smalls, wq.shape[1])
            else:
                small = small_add(small, small_got, small_at <= 2)
            if small_at < 2:
                small_got = (core, chip)[small_at](small)
            elif small_at < size.bit_length() + 1:
                small_got = swap_bit(small, size, small_at - 2)
            small_at += 1
            continue
        group = sums[ahead][which]
        if step != "place":
            getattr(group, step)()
        elif which == BOTH:
            g_ffn, g_att = group.place(bits, ahead, layers)
        elif which == FFN:
            g_ffn = place_ffn(bits, group.parts(), ahead, layers, g_ffn)
        else:
            g_att = place_attn(bits, ATTN_PICKS, group.parts(), ahead, layers, g_att)
    while small_at < size.bit_length() + 2:
        small = small_add(small, small_got, small_at <= 2)
        if small_at < size.bit_length() + 1:
            small_got = swap_bit(small, size, small_at - 2)
        small_at += 1
    g_down, g_up = g_ffn
    small = small.reshape(layers, 16, dim)
    common = small[:, :8]
    heads = small[:, 8]
    hd = wq.shape[1]

    def swapped(i):
        return jnp.swapaxes(g_att[i], 1, 2)

    return (
        hidden_out,
        frames_grad,
        common[0, 6],
        swapped(0),
        heads[:, :hd],
        swapped(1),
        swapped(2),
        heads[:, hd : 2 * hd],
        g_att[3],
        common[:, 2],
        common[:, 0],
        common[:, 1],
        g_up,
        small[:, 9],
        g_down,
        common[:, 5],
        common[:, 3],
        common[:, 4],
    )


def solution(mesh):
    rows = P(("dp", "mp"), None)
    cols = P(None, None, "mp")
    units = P(None, "mp", None)
    vec = P(None, "mp")
    return jax.shard_map(
        per_device,
        mesh=mesh,
        in_specs=(
            rows, P(("dp", "mp")), P(), cols, vec, cols, cols, vec, units, P(), P(), P(),
            cols, vec, units, P(), P(), P(), rows,
        ),
        out_specs=(
            rows, rows, P(), cols, vec, cols, cols, vec, units, P(), P(), P(),
            cols, vec, units, P(), P(), P(),
        ),
        check_vma=False,
    )
```

```python
import functools
import math
import jax
import jax.numpy as jnp
from jax import lax
from jax.experimental import pallas as pl
from jax.experimental.pallas import tpu as pltpu
from jax.sharding import PartitionSpec as P

HEAD_DIM = 64
CLIP = 368
BF = jnp.bfloat16
F32 = jnp.float32
SPAN = 8 * 10**9
LONG = 10**12
VMEM_LIMIT = 32 * 1024 * 1024


def nn(a, b):
    return lax.dot_general(a, b, (((1,), (0,)), ((), ())), preferred_element_type=F32)


def nt(a, b):
    return lax.dot_general(a, b, (((1,), (1,)), ((), ())), preferred_element_type=F32)


def tn(a, b):
    return lax.dot_general(a, b, (((0,), (0,)), ((), ())), preferred_element_type=F32)


def whole(shape):
    zeros = (0,) * len(shape)
    return pl.BlockSpec(tuple(shape), lambda i: zeros)


def at_layer(shape, layer):
    rest = (0,) * (len(shape) - 1)
    return pl.BlockSpec((1,) + tuple(shape[1:]), lambda i: (layer,) + rest)


def sds(shape, dtype):
    return jax.ShapeDtypeStruct(shape, dtype)


def kept(shape, dtype):
    return pltpu.HBM(shape, dtype)


class Order:
    def __init__(self):
        self.last = None
        self.span = SPAN
        self.small = True

    def call(self, body, count, args, mark=0, **given):
        anywhere = pl.BlockSpec(memory_space=pl.ANY)
        given["in_specs"] = list(given["in_specs"])
        if self.last is not None:
            given["in_specs"].append(anywhere)
            args = [*args, self.last]
        extra = mark is None
        if extra:
            given["out_specs"] = [*given["out_specs"], anywhere]
            given["out_shape"] = [*given["out_shape"], sds((8, 128), F32)]
        n = len(given["out_shape"])

        def kernel(*refs):
            outs = refs[len(args) : len(args) + n - extra]
            body(*refs[:count], *outs, *refs[len(args) + n :])

        out = pl.pallas_call(kernel, grid=(1,), **given)(*args)
        self.last = out[-1 if extra else mark]
        return out[: n - extra]


ORDER = Order()


def call(kernel, ins, outs, scratch=(), flops=0, name=None, mark=0):
    specs = [
        pl.BlockSpec(memory_space=pltpu.SMEM)
        if l == "smem"
        else whole(a.shape)
        if l is None
        else at_layer(a.shape, l)
        for a, l in ins
    ]
    nbytes = sum(
        (a.size // a.shape[0] if isinstance(l, int) else a.size) * a.dtype.itemsize for a, l in ins
    ) + sum(math.prod(o.shape) * o.dtype.itemsize for o in outs)
    return ORDER.call(
        kernel,
        len(ins),
        [a for a, _ in ins],
        mark=mark,
        in_specs=specs,
        out_specs=[whole(o.shape) for o in outs],
        out_shape=outs,
        scratch_shapes=list(scratch),
        compiler_params=pltpu.CompilerParams(vmem_limit_bytes=VMEM_LIMIT),
        cost_estimate=pl.CostEstimate(
            flops=max(flops, ORDER.span), bytes_accessed=nbytes, transcendentals=0
        ),
        name=name,
    )


def join(a_ref, b_ref, scratch, joined):
    half = a_ref.shape[0]
    scratch[:half] = a_ref[...].astype(F32)
    scratch[half:] = b_ref[...].astype(F32)
    value = scratch[...].astype(BF)
    joined[...] = value
    return value


def arrange(who, pair, scratch, arranged):
    half = pair.shape[0] // 2
    scratch[...] = pair[...].astype(F32)
    at = pl.multiple_of(who[0] * half, 8)
    both = [scratch[pl.ds(at, half), :], scratch[pl.ds(half - at, half), :]]
    value = jnp.concatenate(both, axis=0).astype(BF)
    arranged[...] = value
    return value


def split_out(value, scratch, oa, ob):
    half = oa.shape[0]
    scratch[...] = value
    oa[...] = scratch[:half].astype(BF)
    ob[...] = scratch[half:].astype(BF)


def head_mask(width, head):
    cols = lax.broadcasted_iota(jnp.int32, (1, width), 1)
    return (cols // HEAD_DIM == head).astype(F32)


def soft(k, q, head):
    mask = (head_mask(q.shape[1], head) * HEAD_DIM ** (-0.5)).astype(BF)
    s = nt(k, q * mask)
    e = jnp.exp(s - jnp.max(s, axis=0, keepdims=True))
    return e * (1.0 / jnp.sum(e, axis=0, keepdims=True))


def attn_fwd_kernel(
    xa, xb, wq, wk, wv, wo, bq, bv, pa, pb, xc, qo, ko, vo, kto, cto, scr, *, layer
):
    x = join(xa, xb, scr, xc)
    q = (nt(x, wq[0]) + bq[layer : layer + 1, :].astype(F32)).astype(BF)
    k = nt(x, wk[0]).astype(BF)
    kto[...] = nt(wk[0], x).astype(BF)
    v32 = nt(x, wv[0]) + bv[layer : layer + 1, :].astype(F32)
    v = v32.astype(BF)
    vt = v32.T.astype(BF)
    qo[...] = q
    ko[...] = k
    vo[...] = v
    parts = []
    for h in range(q.shape[1] // HEAD_DIM):
        pt = soft(k, q, h).astype(BF)
        parts.append(nn(vt[h * HEAD_DIM : (h + 1) * HEAD_DIM], pt))
    ct = jnp.concatenate(parts, axis=0).astype(BF)
    cto[...] = ct
    split_out(tn(ct, wo[0]), scr, pa, pb)


def attn_fwd(layer, xa, xb, wq, wk, wv, wo, bq, bv):
    rows, d = 2 * xa.shape[0], xa.shape[1]
    hd = wq.shape[1]
    outs = [
        sds((rows // 2, d), BF),
        sds((rows // 2, d), BF),
        sds((rows, d), BF),
        sds((rows, hd), BF),
        sds((rows, hd), BF),
        sds((rows, hd), BF),
        sds((hd, rows), BF),
        sds((hd, rows), BF),
    ]
    return call(
        functools.partial(attn_fwd_kernel, layer=layer),
        [(xa, None), (xb, None)]
        + [(w, layer) for w in (wq, wk, wv, wo)]
        + [(bq, None), (bv, None)],
        outs,
        [pltpu.VMEM((rows, d), F32)],
        flops=2 * rows * hd * (5 * d + 2 * rows),
        name="attn_fwd",
    )


def attn_bwd_kernel(
    who, b_in, q, k, v, kt, wq, wk, wv, wo, marks, pa, pb, bc, dqt, dk, dv, sbq, sbv, smask, scr
):
    b = arrange(who, b_in, scr, bc)
    cg = nt(b, wo[0]).astype(BF)
    qv, kv, vv, ktv = q[...], k[...], v[...], kt[...]
    width = qv.shape[1]
    scale = HEAD_DIM ** (-0.5)
    dqs = []
    dk32 = jnp.zeros(qv.shape, F32)
    dv32 = jnp.zeros(qv.shape, F32)
    for h in range(width // HEAD_DIM):
        mask = head_mask(width, h)
        p = soft(kv, qv, h)
        dp = nt(vv, cg * mask.astype(BF))
        dsum = jnp.sum(p * dp, axis=0, keepdims=True)
        ds = (p * (dp - dsum)).astype(BF)
        dqs.append(nn(ktv[h * HEAD_DIM : (h + 1) * HEAD_DIM], ds))
        dk32 = dk32 + nn(ds, qv) * (mask * scale)
        dv32 = dv32 + nn(p.astype(BF), cg) * mask
    dqtv = (jnp.concatenate(dqs, axis=0) * scale).astype(BF)
    dkv = dk32.astype(BF)
    dvv = dv32.astype(BF)
    dqt[...] = dqtv
    dk[...] = dkv
    dv[...] = dvv
    sbq[...] = jnp.sum(dqtv.astype(F32).T, axis=0, keepdims=True)
    sbv[...] = jnp.sum(dvv.astype(F32), axis=0, keepdims=True)
    total = tn(dqtv, wq[0]) + nn(dkv, wk[0]) + nn(dvv, wv[0])
    smask[...] = jnp.sum(total * marks[:, :1].astype(F32), axis=0, keepdims=True)
    split_out(total, scr, pa, pb)


def attn_bwd(who, layer, b, q, k, v, kt, marks, wq, wk, wv, wo):
    rows, d = b.shape
    hd = wq.shape[1]
    outs = [
        sds((rows // 2, d), BF),
        sds((rows // 2, d), BF),
        sds((rows, d), BF),
        sds((hd, rows), BF),
        sds((rows, hd), BF),
        sds((rows, hd), BF),
        sds((1, hd), F32),
        sds((1, hd), F32),
        sds((1, d), F32),
    ]
    return call(
        attn_bwd_kernel,
        [(who, "smem"), (b, None), (q, None), (k, None), (v, None), (kt, None)]
        + [(w, layer) for w in (wq, wk, wv, wo)]
        + [(marks, None)],
        outs,
        [pltpu.VMEM((rows, d), F32)],
        flops=2 * rows * hd * (4 * d + 5 * rows),
        name="attn_bwd",
    )


def ffn_fwd_kernel(ya, yb, wu, wd, bu, pa, pb, yc, hid, slo, scr, *, layer):
    pre = nn(join(ya, yb, scr, yc), wu[0]) + bu[layer : layer + 1, :].astype(F32)
    phi = 0.5 * (1.0 + lax.erf(pre * 0.7071067811865476))
    hidden = (pre * phi).astype(BF)
    hid[...] = hidden
    slo[...] = (phi + pre * jnp.exp(-0.5 * pre * pre) * 0.3989422804014327).astype(BF)
    split_out(nn(hidden, wd[0]), scr, pa, pb)


def ffn_fwd(layer, ya, yb, wu, wd, bu):
    rows, d = 2 * ya.shape[0], ya.shape[1]
    ff = wu.shape[2]
    outs = [
        sds((rows // 2, d), BF),
        sds((rows // 2, d), BF),
        sds((rows, d), BF),
        sds((rows, ff), BF),
        sds((rows, ff), BF),
    ]
    return call(
        functools.partial(ffn_fwd_kernel, layer=layer),
        [(ya, None), (yb, None), (wu, layer), (wd, layer), (bu, None)],
        outs,
        [pltpu.VMEM((rows, d), F32)],
        flops=4 * rows * d * ff,
        name="ffn_fwd",
    )


def ffn_bwd_kernel(who, d_in, slo, wu, wd, pa, pb, dc, act_o, sbu, scr):
    act = (nt(arrange(who, d_in, scr, dc), wd[0]) * slo[...].astype(F32)).astype(BF)
    act_o[...] = act
    sbu[...] = jnp.sum(act.astype(F32), axis=0, keepdims=True)
    split_out(nt(act, wu[0]), scr, pa, pb)


def ffn_bwd(who, layer, d_in, slo, wu, wd):
    rows, d = d_in.shape
    ff = wu.shape[2]
    outs = [
        sds((rows // 2, d), BF),
        sds((rows // 2, d), BF),
        sds((rows, d), BF),
        sds((rows, ff), BF),
        sds((1, ff), F32),
    ]
    return call(
        ffn_bwd_kernel,
        [(who, "smem"), (d_in, None), (slo, None), (wu, layer), (wd, layer)],
        outs,
        [pltpu.VMEM((rows, d), F32)],
        flops=4 * rows * d * ff,
        name="ffn_bwd",
    )


def put_halves(bits, pick, scr, send, keep):
    half = keep.shape[0]
    bit = bits[pick]
    keep[...] = scr[pl.ds(pl.multiple_of(bit * half, 16), half), :]
    send[...] = scr[pl.ds(pl.multiple_of((1 - bit) * half, 16), half), :]


def pair_wgrad_kernel(bits, al, ar, bl, br, send, keep, scr, *, pick):
    scr[...] = (tn(al[...], bl[...]) + tn(ar[...], br[...])).astype(BF)
    put_halves(bits, pick, scr, send, keep)


def pair_wgrad(bits, pick, a, b, name):
    rows, m = a[0].shape
    n = b[0].shape[1]
    return call(
        functools.partial(pair_wgrad_kernel, pick=pick),
        [(bits, "smem")] + [(v, None) for v in (*a, *b)],
        [sds((m // 2, n), BF)] * 2,
        [pltpu.VMEM((m, n), BF)],
        flops=4 * rows * m * n,
        name=name,
    )


def attn_wgrad_kernel(
    bits, xl, xr, dqtl, dqtr, dkl, dkr, dvl, dvr, ctl, ctr, bl, br, send, keep, scr, *, pick
):
    hd = scr.shape[0] // 4
    scr[:hd] = (nn(dqtl[...], xl[...]) + nn(dqtr[...], xr[...])).astype(BF)
    scr[hd : 2 * hd] = (tn(dkl[...], xl[...]) + tn(dkr[...], xr[...])).astype(BF)
    scr[2 * hd : 3 * hd] = (tn(dvl[...], xl[...]) + tn(dvr[...], xr[...])).astype(BF)
    scr[3 * hd :] = (nn(ctl[...], bl[...]) + nn(ctr[...], br[...])).astype(BF)
    put_halves(bits, pick, scr, send, keep)


def attn_wgrad(bits, pick, hd, *values):
    rows, dim = values[0].shape
    return call(
        functools.partial(attn_wgrad_kernel, pick=pick),
        [(bits, "smem")] + [(v, None) for v in values],
        [sds((2 * hd, dim), BF)] * 2,
        [pltpu.VMEM((4 * hd, dim), BF)],
        flops=16 * rows * dim * hd,
        name="attn_wgrad",
    )


def attn_wgrad_two_kernel(
    bits, xl, xr, dqtl, dqtr, dkl, dkr, dvl, dvr, ctl, ctr, bl, br, sd, kd, su, ku, sc_d, sc_u
):
    hd = sc_d.shape[0] // 2
    sc_d[:hd] = (nn(dqtl[...], xl[...]) + nn(dqtr[...], xr[...])).astype(BF)
    sc_d[hd:] = (tn(dkl[...], xl[...]) + tn(dkr[...], xr[...])).astype(BF)
    put_halves(bits, 0, sc_d, sd, kd)
    sc_u[:hd] = (tn(dvl[...], xl[...]) + tn(dvr[...], xr[...])).astype(BF)
    sc_u[hd:] = (nn(ctl[...], bl[...]) + nn(ctr[...], br[...])).astype(BF)
    put_halves(bits, 1, sc_u, su, ku)


def attn_wgrad_two(bits, hd, *values):
    rows, dim = values[0].shape
    return call(
        attn_wgrad_two_kernel,
        [(bits, "smem")] + [(v, None) for v in values],
        [sds((hd, dim), BF)] * 4,
        [pltpu.VMEM((2 * hd, dim), BF)] * 2,
        flops=16 * rows * dim * hd,
        name="attn_wgrad",
    )


def place_two_kernel(bits, mine, by_low, by_high, down_far, up_far, *outs):
    size = down_far.shape[0]
    low, high = bits[0], bits[1]
    parts = [
        (low, high, mine, mine),
        (1 - low, high, by_low, by_low),
        (low, 1 - high, by_high, by_high),
        (1 - low, 1 - high, down_far, up_far),
    ]
    for l, h, ref_down, ref_up in parts:

        def put_down(spot, ref=ref_down):
            at = (spot % 2) * size
            outs[spot // 2][0, at : at + size, :] = ref[:size, :].astype(F32)

        def put_up(spot, ref=ref_up):
            at = (spot % 2) * size
            outs[2 + spot // 2][0, at : at + size, :] = ref[ref.shape[0] - size :, :].astype(F32)

        when_at(l, h, put_down)
        when_at(h, l, put_up)


def small_kernel(*refs, layers, hd):
    out = refs[-1]
    width = out.shape[1]
    zeros = jnp.zeros((8, width), F32)
    rows = []
    for l in range(layers):
        sql, sqr, svl, svr, sul, sur, own_a, own_f, sma, smb = refs[10 * l : 10 * l + 10]
        heads = [sql[...] + sqr[...], svl[...] + svr[...], zeros[:1, : width - 2 * hd]]
        mask_row = own_a[3:4] + sma[...] + smb[...] if l == 0 else zeros[:1]
        rows += [own_a[:3], own_f[:3], mask_row, zeros[:1]]
        rows += [jnp.concatenate(heads, axis=1), sul[...] + sur[...], zeros[:6]]
    out[...] = jnp.concatenate(rows, axis=0)


def small_rows(values, hd):
    layers = len(values)
    dim = values[0][6].shape[1]
    return call(
        functools.partial(small_kernel, layers=layers, hd=hd),
        [(v, None) for vs in values for v in vs],
        [sds((16 * layers, dim), F32)],
        name="small_rows",
    )[0]


def small_mp_kernel(have, got, out):
    for l in range(have.shape[0] // 16):
        out[16 * l : 16 * l + 8, :] = have[16 * l : 16 * l + 8, :] + got[16 * l : 16 * l + 8, :]
        out[16 * l + 8 : 16 * l + 16, :] = have[16 * l + 8 : 16 * l + 16, :]


def small_dp_kernel(have, got, out):
    out[...] = have[...] + got[...]


def small_add(have, got, over_mp):
    return call(
        small_mp_kernel if over_mp else small_dp_kernel,
        [(have, None), (got, None)],
        [sds(have.shape, F32)],
        name="small_add",
    )[0]


def small_out_kernel(have, got, bq, bv, bo, ag, ab, bu, bd, fg, fb, mask):
    total = have[...] + got[...]
    hd = bq.shape[1]
    for l in range(bq.shape[0]):
        at = 16 * l
        for out, row in ((ag, 0), (ab, 1), (bo, 2), (fg, 3), (fb, 4), (bd, 5), (bu, 9)):
            out[l : l + 1, :] = total[at + row : at + row + 1, :]
        heads = total[at + 8 : at + 9, :]
        bq[l : l + 1, :] = heads[:, :hd]
        bv[l : l + 1, :] = heads[:, hd : 2 * hd]
    mask[...] = total[6:7, :]


def small_out(have, got, layers, hd):
    dim = have.shape[1]
    wide = sds((layers, dim), F32)
    return call(
        small_out_kernel,
        [(have, None), (got, None)],
        [sds((layers, hd), F32)] * 2 + [wide] * 7 + [sds((1, dim), F32)],
        name="small_out",
    )


def halve_kernel(bits, have, got, send, keep, *, pick):
    half = keep.shape[0]
    bit = bits[pick]
    mine = pl.ds(pl.multiple_of(bit * half, 16), half)
    other = pl.ds(pl.multiple_of((1 - bit) * half, 16), half)
    keep[...] = (have[mine, :].astype(F32) + got[mine, :].astype(F32)).astype(BF)
    send[...] = (have[other, :].astype(F32) + got[other, :].astype(F32)).astype(BF)


def halve(bits, pick, have, got):
    rows, dim = have.shape
    return call(
        functools.partial(halve_kernel, pick=pick),
        [(bits, "smem"), (have, None), (got, None)],
        [sds((rows // 2, dim), BF)] * 2,
        name="halve",
    )


def add_kernel(a, b, o):
    o[...] = (a[...].astype(F32) + b[...].astype(F32)).astype(BF)


def add(a, b):
    return call(add_kernel, [(a, None), (b, None)], [sds(a.shape, BF)], name="add")[0]


def stacked_call(kernel, bits, parts, outs, layer, layers, old, name):
    dim = parts[0].shape[1]
    old = [] if old is None else list(old)
    shapes = [sds((layers, rows, dim), F32) for rows in outs]
    specs = [pl.BlockSpec((1, rows, dim), lambda i: (layer, 0, 0)) for rows in outs]
    n = 1 + len(parts)

    def body(*refs):
        kernel(*refs[:n], *refs[n + len(old) :])

    return ORDER.call(
        body,
        n + len(old),
        [bits, *parts, *old],
        mark=None,
        in_specs=[pl.BlockSpec(memory_space=pltpu.SMEM)]
        + [whole(q.shape) for q in parts]
        + [pl.BlockSpec(memory_space=pl.ANY)] * len(old),
        out_specs=specs,
        out_shape=shapes,
        input_output_aliases={n + i: i for i in range(len(old))},
        compiler_params=pltpu.CompilerParams(vmem_limit_bytes=VMEM_LIMIT),
        cost_estimate=pl.CostEstimate(flops=ORDER.span, bytes_accessed=1, transcendentals=0),
        name=name,
    )


def when_at(first, second, fn):
    for spot in range(4):

        @pl.when(2 * first + second == spot)
        def _(spot=spot):
            fn(spot)


def place_attn_kernel(bits, *refs, picks):
    parts, outs = refs[:4], refs[4:]
    for i, ref in enumerate(parts):
        first = bits[picks[0]] if i < 2 else 1 - bits[picks[0]]
        second = bits[picks[1]] if i % 2 == 0 else 1 - bits[picks[1]]

        def put(spot, ref=ref):
            outs[spot][0] = ref[...].astype(F32)

        when_at(first, second, put)


def place_attn(bits, picks, parts, layer, layers, old):
    return stacked_call(
        functools.partial(place_attn_kernel, picks=picks),
        bits,
        parts,
        [parts[0].shape[0]] * 4,
        layer,
        layers,
        old,
        "place_attn",
    )


def place_ffn_kernel(bits, mine, by_low, by_high, down_far, up_far, down, up):
    size = down_far.shape[0]
    low, high = bits[0], bits[1]
    parts = [
        (low, high, mine, mine),
        (1 - low, high, by_low, by_low),
        (low, 1 - high, by_high, by_high),
        (1 - low, 1 - high, down_far, up_far),
    ]
    for l, h, ref_down, ref_up in parts:

        def put_down(spot, ref=ref_down):
            down[0, spot * size : (spot + 1) * size, :] = ref[:size, :].astype(F32)

        def put_up(spot, ref=ref_up):
            up[0, spot * size : (spot + 1) * size, :] = ref[ref.shape[0] - size :, :].astype(F32)

        when_at(l, h, put_down)
        when_at(h, l, put_up)


def place_ffn(bits, parts, layer, layers, old):
    rows = 4 * parts[3].shape[0]
    return stacked_call(
        place_ffn_kernel, bits, parts, [rows] * 2, layer, layers, old, "place_ffn"
    )


def halve_two_kernel(bits, kd, gd, ku, gu, send_d, send_u, keep):
    size = send_d.shape[0]
    for have, got, send, pick, at in ((kd, gd, send_d, 1, 0), (ku, gu, send_u, 0, size)):
        bit = bits[pick]
        mine = pl.ds(pl.multiple_of(bit * size, 16), size)
        other = pl.ds(pl.multiple_of((1 - bit) * size, 16), size)
        keep[at : at + size, :] = (have[mine, :].astype(F32) + got[mine, :].astype(F32)).astype(BF)
        send[...] = (have[other, :].astype(F32) + got[other, :].astype(F32)).astype(BF)


def halve_two(bits, kd, gd, ku, gu):
    rows, dim = kd.shape
    return call(
        halve_two_kernel,
        [(bits, "smem"), (kd, None), (gd, None), (ku, None), (gu, None)],
        [sds((rows // 2, dim), BF), sds((rows // 2, dim), BF), sds((rows, dim), BF)],
        name="halve_two",
    )


def add_two_kernel(have, gd, gu, out):
    size = gd.shape[0]
    out[:size, :] = (have[:size, :].astype(F32) + gd[...].astype(F32)).astype(BF)
    out[size:, :] = (have[size:, :].astype(F32) + gu[...].astype(F32)).astype(BF)


def add_two(have, gd, gu):
    return call(
        add_two_kernel, [(have, None), (gd, None), (gu, None)], [sds(have.shape, BF)], name="add_two"
    )[0]


def cut_two_kernel(by_high, by_low, od, ou):
    size = od.shape[0]
    od[...] = by_high[:size, :]
    ou[...] = by_low[size:, :]


def cut_two(by_high, by_low):
    rows, dim = by_high.shape
    return call(
        cut_two_kernel,
        [(by_high, None), (by_low, None)],
        [sds((rows // 2, dim), BF)] * 2,
        name="cut_two",
    )


def swap_bit(v, size, pick):
    return lax.ppermute(v, "dp", [(i, i ^ (1 << pick)) for i in range(size)])


def copy_kernel(have, out):
    out[...] = have[...]


def gate(v):
    return call(copy_kernel, [(v, None)], [sds(v.shape, v.dtype)], name="gate")[0]


def merge_kernel(ffn, have, got, out):
    size = ffn.shape[0]
    out[:size, :] = ffn[...]
    out[size:, :] = (have[...].astype(F32) + got[...].astype(F32)).astype(BF)


def cut_merged_kernel(by_high, by_low, od, ou):
    size = ou.shape[0]
    od[:size, :] = by_high[:size, :]
    od[size:, :] = by_high[2 * size :, :]
    ou[...] = by_low[size : 2 * size, :]


def place_merged_kernel(bits, mine, by_low, by_high, down_far, up_far, down, up, *heads):
    size = up_far.shape[0]
    low, high = bits[0], bits[1]
    parts = [
        (low, high, mine, mine, mine, 2),
        (1 - low, high, by_low, by_low, by_low, 2),
        (low, 1 - high, by_high, by_high, by_high, 2),
        (1 - low, 1 - high, down_far, up_far, down_far, 1),
    ]
    for l, h, ref_down, ref_up, ref_head, at in parts:

        def put_down(spot, ref=ref_down, head=ref_head, at=at):
            down[0, spot * size : (spot + 1) * size, :] = ref[:size, :].astype(F32)
            heads[spot][0] = head[at * size : (at + 1) * size, :].astype(F32)

        def put_up(spot, ref=ref_up, at=at):
            up[0, spot * size : (spot + 1) * size, :] = ref[
                (at - 1) * size : at * size, :
            ].astype(F32)

        when_at(l, h, put_down)
        when_at(h, l, put_up)


class Merged:
    def __init__(self, ffn, attn):
        self.ffn, self.attn = ffn, attn

    def merge(self):
        ffn, attn = self.ffn, self.attn
        for i in range(len(attn.rest) - 1):
            attn.keep = add(attn.keep, attn.got)
            attn.got = attn.swap(attn.keep, attn.rest[i + 1])
        have, got = attn.keep, attn.got
        rows = ffn.keep.shape[0] + have.shape[0]
        self.keep = call(
            merge_kernel,
            [(ffn.keep, None), (have, None), (got, None)],
            [sds((rows, have.shape[1]), BF)],
            name="merge",
        )[0]
        self.by_high = ffn.swap(self.keep, 1)
        if self.whole:
            self.by_low = ffn.swap(self.keep, 0)

    whole = False

    def low(self):
        self.by_low = self.ffn.swap(gate(self.keep), 0)

    def cut(self):
        rows, dim = self.keep.shape
        od, ou = call(
            cut_merged_kernel,
            [(self.by_high, None), (self.by_low, None)],
            [sds((2 * rows // 3, dim), BF), sds((rows // 3, dim), BF)],
            name="cut_merged",
        )
        self.down_far = self.ffn.swap(od, 0)
        self.up_far = self.ffn.swap(ou, 1)

    def place(self, bits, layer, layers):
        size = self.up_far.shape[0]
        parts = self.keep, self.by_low, self.by_high, self.down_far, self.up_far
        outs = [4 * size] * 2 + [size] * 4
        got = stacked_call(
            place_merged_kernel, bits, parts, outs, layer, layers, None, "place_merged"
        )
        return got[:2], got[2:]


class DpSum:
    def __init__(self, bits, size, picks):
        self.bits, self.size, self.picks = bits, size, picks
        self.rest = [p for p in range(size.bit_length() - 1) if p not in picks]

    def swap(self, v, pick):
        return swap_bit(v, self.size, pick)

    def start(self, fn, *values):
        send, self.keep = fn(self.bits, self.picks[0], *values)
        self.got = self.swap(send, self.picks[0])

    def halve(self):
        send, self.keep = halve(self.bits, self.picks[1], self.keep, self.got)
        self.got = self.swap(send, self.picks[1])

    def cross(self):
        self.keep = add(self.keep, self.got)
        if self.rest:
            self.got = self.swap(self.keep, self.rest[0])

    def total(self):
        for i in range(len(self.rest)):
            self.keep = add(self.keep, self.got)
            if i + 1 < len(self.rest):
                self.got = self.swap(self.keep, self.rest[i + 1])

    def hold(self):
        self.keep = gate(self.keep)

    def spread(self):
        self.near = self.swap(self.keep, self.picks[1])
        self.far = self.swap(self.keep, self.picks[0])

    def last(self):
        self.end = self.swap(gate(self.near), self.picks[0])

    def parts(self):
        return self.keep, self.near, self.far, self.end


class FfnSum:
    def __init__(self, bits, size):
        self.bits, self.size = bits, size
        self.rest = range(2, size.bit_length() - 1)

    def swap(self, v, pick):
        return swap_bit(v, self.size, pick)

    def start(self, down, up):
        send, self.kd = pair_wgrad(self.bits, 0, down[:2], down[2:], "down_wgrad")
        self.gd = self.swap(send, 0)
        send, self.ku = pair_wgrad(self.bits, 1, up[:2], up[2:], "up_wgrad")
        self.gu = self.swap(send, 1)

    def halve(self):
        send_d, send_u, self.keep = halve_two(self.bits, self.kd, self.gd, self.ku, self.gu)
        self.gd = self.swap(send_d, 1)
        self.gu = self.swap(send_u, 0)

    def cross(self):
        self.keep = add_two(self.keep, self.gd, self.gu)
        if self.rest:
            self.got = self.swap(self.keep, self.rest[0])

    def total(self):
        for i in range(len(self.rest)):
            self.keep = add(self.keep, self.got)
            if i + 1 < len(self.rest):
                self.got = self.swap(self.keep, self.rest[i + 1])

    def hold(self):
        self.keep = gate(self.keep)

    def high(self):
        self.by_high = self.swap(self.keep, 1)

    def low(self):
        self.by_low = self.swap(self.keep, 0)

    def last(self):
        od, ou = cut_two(self.by_high, self.by_low)
        self.down_far = self.swap(od, 0)
        self.up_far = self.swap(ou, 1)

    def parts(self):
        return self.keep, self.by_low, self.by_high, self.down_far, self.up_far


class AttnSum(FfnSum):
    def start(self, fn, *values):
        sd, self.kd, su, self.ku = attn_wgrad_two(self.bits, values[0], *values[1:])
        self.gd = self.swap(sd, 0)
        self.gu = self.swap(su, 1)

    def place(self, layer, layers, old):
        parts = self.parts()
        rows = 2 * parts[3].shape[0]
        return stacked_call(
            place_two_kernel, self.bits, parts, [rows] * 4, layer, layers, old, "place_attn"
        )


def three(who, mine, pair, far):
    half = mine.shape[0]
    if pair.shape[0] == half:
        near = pair[...].astype(F32)
    else:
        near = jnp.where(who[0] == 0, pair[half:, :].astype(F32), pair[:half, :].astype(F32))
    return mine[...].astype(F32) + near + far[...].astype(F32)


def norm_fwd_kernel(near, far, res, bias, gain, shift, out, unit, inv, low, *, layer):
    row = slice(layer, layer + 1)
    r = res[...] + (near[...] + far[...].astype(F32)) + bias[row, :].astype(F32)
    mean = jnp.mean(r, axis=-1, keepdims=True)
    c = r - mean
    i = lax.rsqrt(jnp.mean(c * c, axis=-1, keepdims=True) + 1e-05)
    u = c * i
    o = u * gain[row, :].astype(F32) + shift[row, :].astype(F32)
    out[...] = o
    unit[...] = u
    inv[...] = i
    low[...] = o.astype(BF)


def norm_fwd(layer, parts, res, bias, gain, shift):
    rows, d = res.shape
    return call(
        functools.partial(norm_fwd_kernel, layer=layer),
        [(v, None) for v in (*parts, res, bias, gain, shift)],
        [sds((rows, d), F32), sds((rows, d), F32), sds((rows, 1), F32), sds((rows, d), BF)],
        name="norm_fwd",
        mark=3,
    )


def norm_bwd_core(up, unit, inv, gain, marks, resid, low, sums, layer):
    u = unit[...]
    e = up * gain[layer : layer + 1, :].astype(F32)
    r = inv[...] * (
        e - jnp.mean(e, axis=-1, keepdims=True) - u * jnp.mean(e * u, axis=-1, keepdims=True)
    )
    resid[...] = r
    lo = r.astype(BF)
    low[...] = lo
    sums[0:1, :] = jnp.sum(up * u, axis=0, keepdims=True)
    sums[1:2, :] = jnp.sum(up, axis=0, keepdims=True)
    sums[2:3, :] = jnp.sum(lo.astype(F32), axis=0, keepdims=True)
    sums[3:4, :] = jnp.sum(r * marks[...], axis=0, keepdims=True)


def norm_bwd_first_kernel(og, unit, inv, gain, marks, resid, low, sums, *, layer):
    up = og[...].astype(F32) * marks[...]
    norm_bwd_core(up, unit, inv, gain, marks, resid, low, sums, layer)


def norm_bwd_kernel(who, p0, p1, p2, res, unit, inv, gain, marks, resid, low, sums, *, layer):
    up = res[...] + three(who, p0, p1, p2)
    norm_bwd_core(up, unit, inv, gain, marks, resid, low, sums, layer)


def norm_bwd(who, layer, ins, unit, inv, gain, marks):
    rows, d = unit.shape
    first = len(ins) == 1
    return call(
        functools.partial(norm_bwd_first_kernel if first else norm_bwd_kernel, layer=layer),
        ([] if first else [(who, "smem")])
        + [(v, None) for v in (*ins, unit, inv, gain, marks)],
        [sds((rows, d), F32), sds((rows, d), BF), sds((4, d), F32)],
        name="norm_bwd",
        mark=1,
    )


def turn_kernel(near, far, res, bias, gain, shift, og, marks, hidden, resid, low, sums, *, layer):
    row = slice(layer, layer + 1)
    r = res[...] + (near[...] + far[...].astype(F32)) + bias[row, :].astype(F32)
    c = r - jnp.mean(r, axis=-1, keepdims=True)
    inv = lax.rsqrt(jnp.mean(c * c, axis=-1, keepdims=True) + 1e-05)
    unit = c * inv
    hidden[...] = (unit * gain[row, :].astype(F32) + shift[row, :].astype(F32)).astype(BF)
    up = og[...].astype(F32) * marks[...]
    norm_bwd_core(up, unit, inv, gain, marks, resid, low, sums, layer)


def norm_turn(layer, parts, res, bias, gain, shift, out_grad, marks):
    rows, d = res.shape
    return call(
        functools.partial(turn_kernel, layer=layer),
        [(v, None) for v in (*parts, res, bias, gain, shift, out_grad, marks)],
        [sds((rows, d), BF), sds((rows, d), F32), sds((rows, d), BF), sds((4, d), F32)],
        name="norm_turn",
        mark=2,
    )


def last_kernel(who, p0, p1, p2, res, marks, out):
    out[...] = (res[...] + three(who, p0, p1, p2)) * (1.0 - marks[...])


def last_rows(who, parts, res, marks):
    return call(
        last_kernel,
        [(who, "smem")] + [(v, None) for v in (*parts, res, marks)],
        [sds(res.shape, F32)],
        name="last_rows",
        mark=None,
    )[0]


FFN, ATTN, BOTH, SMALL, ROWS = range(5)
ATTN_PICKS = (0, 1)
PLAN = {
    ("ffn_far", False): [(0, FFN, "start")],
    ("attn_near", False): [(0, FFN, "halve")],
    ("attn_far", False): [(0, ATTN, "start"), (0, FFN, "cross")],
    ("ffn_near", True): [(1, ATTN, "halve")],
    ("ffn_far", True): [(0, FFN, "start"), (1, ATTN, "cross"), (1, FFN, "total")],
    ("attn_near", True): [(0, FFN, "halve"), (1, BOTH, "merge")],
    ("attn_mid", True): [(0, FFN, "cross")],
    ("attn_far", True): [(0, ATTN, "start")],
}
TAIL = [
    (0, ROWS, ""),
    (0, SMALL, ""),
    (1, BOTH, "low"),
    (0, ATTN, "halve"),
    (0, SMALL, ""),
    (0, FFN, "total"),
    (0, FFN, "high"),
    (0, FFN, "low"),
    (0, ATTN, "cross"),
    (0, SMALL, ""),
    (1, BOTH, "cut"),
    (0, SMALL, ""),
    (0, ATTN, "total"),
    (0, ATTN, "spread"),
    (0, SMALL, ""),
    (0, FFN, "last"),
    (1, BOTH, "place"),
    (0, SMALL, ""),
    (0, ATTN, "last"),
    (0, FFN, "place"),
    (0, ATTN, "place"),
]
CORE = [(0, 1), (1, 0), (2, 3), (3, 2)]
CHIP = [(0, 2), (2, 0), (1, 3), (3, 1)]


def core(v):
    return lax.ppermute(v, "mp", CORE)


def chip(v):
    return lax.ppermute(v, "mp", CHIP)


def both_cores(v):
    return lax.all_gather(v, "mp", axis=0, tiled=True, axis_index_groups=[[0, 1], [2, 3]])


def join_kernel(who, mine, pair, out):
    half = mine.shape[0]
    theirs = jnp.where(who[0] == 0, pair[half:, :].astype(F32), pair[:half, :].astype(F32))
    out[...] = (mine[...].astype(F32) + theirs).astype(BF)


def gather_sum(who, local, remote):
    joined = call(
        join_kernel,
        [(who, "smem"), (remote[0], None), (both_cores(remote[1]), None)],
        [sds(remote[0].shape, BF)],
        name="join",
    )[0]
    return local[0], both_cores(local[1]), chip(joined)


def prep_kernel(frames, span, vector, stream, low, marks, wide):
    m = jnp.broadcast_to(span[...].astype(F32), (8, span.shape[1])).T[:, :1]
    value = frames[...].astype(F32) * (1.0 - m) + m * vector[...].astype(F32)
    stream[...] = value
    low[...] = value.astype(BF)
    marks[...] = m
    wide[...] = jnp.broadcast_to(m, wide.shape).astype(BF)


def prep(frames, span, vector):
    rows = frames.shape[0]
    return call(
        prep_kernel,
        [(frames, None), (span, None), (vector, None)],
        [sds(frames.shape, F32), sds(frames.shape, BF), sds((rows, 1), F32), sds((rows, 128), BF)],
        name="prep",
        mark=1,
    )


def pair_kernel(a, b, out):
    both = [a[...].astype(F32), b[...].astype(F32)]
    out[...] = jnp.concatenate(both, axis=0).astype(out.dtype)


def pair_rows(a, b):
    shape = (2 * a.shape[0], a.shape[1])
    return call(pair_kernel, [(a, None), (b, None)], [sds(shape, a.dtype)], name="pair_rows")[0]


def plus_kernel(a, b, out):
    out[...] = (a[...].astype(F32) + b[...].astype(F32)).astype(out.dtype)


def plus(a, b, dtype):
    return call(plus_kernel, [(a, None), (b, None)], [sds(a.shape, dtype)], name="plus")[0]


def per_device(
    frames,
    span_mask,
    mask_vector,
    w_query,
    b_query,
    w_key,
    w_value,
    b_value,
    w_out,
    b_out,
    attn_gain,
    attn_bias,
    w_up,
    b_up,
    w_down,
    b_down,
    ffn_gain,
    ffn_bias,
    out_grad,
):
    layers = w_query.shape[0]
    dim = frames.shape[1]
    size = lax.axis_size("dp")
    place_in_dp = lax.axis_index("dp")
    who = (lax.axis_index("mp") & 1).astype(jnp.int32)[None]
    bits = jnp.stack([(place_in_dp >> k) & 1 for k in range(size.bit_length() - 1)]).astype(jnp.int32)
    wq = jnp.swapaxes(w_query, 1, 2)
    wk = jnp.swapaxes(w_key, 1, 2)
    wv = jnp.swapaxes(w_value, 1, 2)
    ORDER.last, ORDER.span, ORDER.small = None, 2 * 10**10, True
    stream, low, marks, mark_rows = prep(frames, span_mask[None], mask_vector[None])
    records = []

    def both(fn, v, extra, jobs=None, later=None, light=False):
        far = chip(v)
        near = both_cores(gate(v))
        first = fn(near, *extra[0])
        if jobs:
            jobs()
        far = both_cores(far)
        if later and light:
            ORDER.span = 0
        second = fn(far, *extra[1])
        ORDER.span = SPAN
        if later:
            later()
        return [first, second]

    def forward(fn, v, marked=None):
        far = chip(v)
        first = fn(v, core(v))
        if marked is not None:
            mark_sides.extend(pair_rows(v, core(v)) for v in (marked, chip(marked)))
        near_sum = plus(first[0], core(first[1]), F32)
        second = fn(far, core(far))
        far_sum = chip(plus(second[0], core(second[1]), BF))
        return (near_sum, far_sum), [first[2:], second[2:]]

    mark_sides = []
    for l in range(layers):
        parts, att = forward(
            lambda *v: attn_fwd(l, *v, wq, wk, wv, w_out, b_query, b_value),
            low,
            None if l else mark_rows,
        )
        normed, unit_a, inv_a, low_a = norm_fwd(l, parts, stream, b_out, attn_gain, attn_bias)
        parts, ffn = forward(lambda *v: ffn_fwd(l, *v, w_up, w_down, b_up), low_a)
        if l < layers - 1:
            stream, unit_f, inv_f, low = norm_fwd(l, parts, normed, b_down, ffn_gain, ffn_bias)
        else:
            hidden_out, *turned = norm_turn(
                l, parts, normed, b_down, ffn_gain, ffn_bias, out_grad, marks
            )
            unit_f = inv_f = None
        records.append((att, ffn, unit_a, inv_a, unit_f, inv_f))
    ORDER.span, ORDER.small = SPAN, True
    sums = [None] * layers
    smalls = [None] * layers
    ins = None
    for l in reversed(range(layers)):
        att, ffn, unit_a, inv_a, unit_f, inv_f = records[l]
        sums[l] = [FfnSum(bits, size), DpSum(bits, size, ATTN_PICKS)]
        sums[l].append(Merged(*sums[l]))
        inputs = [None, None]

        def window(name):
            for ahead, which, step in PLAN.get((name, l == 0), ()):
                if l + ahead < layers:
                    group = sums[l + ahead][which]
                    if step == "start":
                        group.start(*inputs[which])
                    else:
                        getattr(group, step)()

        if l == layers - 1:
            resid_f, low_f, sums_f = turned
        else:
            resid_f, low_f, sums_f = norm_bwd(who, l, ins, unit_f, inv_f, ffn_gain, marks)
        back = both(
            lambda v, c: ffn_bwd(who, l, v, c, w_up, w_down),
            low_f,
            [(f[2],) for f in ffn],
            lambda: window("ffn_near"),
            lambda: window("ffn_mid"),
        )
        parts = gather_sum(who, back[0][:2], back[1][:2])
        inputs[FFN] = (
            [f[1] for f in ffn] + [b[2] for b in back],
            [f[0] for f in ffn] + [b[3] for b in back],
        )
        window("ffn_far")
        s_up = [b[4] for b in back]
        resid_a, low_a, sums_a = norm_bwd(
            who, l, (*parts, resid_f), unit_a, inv_a, attn_gain, marks
        )
        back = both(
            lambda v, *c: attn_bwd(who, l, v, *c, wq, wk, wv, w_out),
            low_a,
            [(*a[1:5], m) for a, m in zip(att, mark_sides)],
            lambda: window("attn_near"),
            lambda: window("attn_mid"),
            l == 0,
        )
        parts = gather_sum(who, back[0][:2], back[1][:2])
        values = [a[0] for a in att]
        for i in (3, 4, 5):
            values += [b[i] for b in back]
        values += [a[5] for a in att]
        values += [b[2] for b in back]
        smalls[l] = [b[i] for i in (6, 7) for b in back] + s_up
        smalls[l] += [sums_a, sums_f] + [b[8] for b in back]
        inputs[ATTN] = (
            lambda bi, p, *v: attn_wgrad(bi, p, wq.shape[1], *v),
            *values,
        )
        ORDER.span = 2 * SPAN if l == 0 else SPAN
        window("attn_far")
        ins = (*parts, resid_a)
    g_att = g_ffn = None
    hd = wq.shape[1]
    held = []
    small_steps = iter([core, chip] + [
        functools.partial(swap_bit, size=size, pick=k) for k in range(size.bit_length() - 1)
    ])

    def small_step():
        if len(held) == 3:
            return
        if not held:
            small = small_rows(smalls, hd)
        else:
            small = None
        step = next(small_steps, None)
        if step is None:
            held.append(small_out(*held, layers, hd))
            return
        if small is None:
            small = small_add(*held, held_mp[0] > 0)
            held_mp[0] -= 1
        held[:] = [small, step(small)]

    held_mp = [2]
    for ahead, which, step in TAIL:
        if ahead >= layers:
            continue
        if which == ROWS:
            frames_grad = last_rows(who, ins[:3], ins[3], marks)
            continue
        if which == SMALL:
            small_step()
            continue
        group = sums[ahead][which]
        if step != "place":
            getattr(group, step)()
        elif which == BOTH:
            g_ffn, g_att = group.place(bits, ahead, layers)
        elif which == FFN:
            g_ffn = place_ffn(bits, group.parts(), ahead, layers, g_ffn)
        else:
            g_att = place_attn(bits, ATTN_PICKS, group.parts(), ahead, layers, g_att)
    while len(held) < 3:
        small_step()
    bq, bv, bo, ag, ab, bu, bd, fg, fb, mask = held[2]
    g_down, g_up = g_ffn

    def swapped(i):
        return jnp.swapaxes(g_att[i], 1, 2)

    return (
        hidden_out,
        frames_grad,
        mask[0],
        swapped(0),
        bq,
        swapped(1),
        swapped(2),
        bv,
        g_att[3],
        bo,
        ag,
        ab,
        g_up,
        bu,
        g_down,
        bd,
        fg,
        fb,
    )


def solution(mesh):
    rows = P(("dp", "mp"), None)
    cols = P(None, None, "mp")
    units = P(None, "mp", None)
    vec = P(None, "mp")
    return jax.shard_map(
        per_device,
        mesh=mesh,
        in_specs=(
            rows, P(("dp", "mp")), P(), cols, vec, cols, cols, vec, units, P(), P(), P(),
            cols, vec, units, P(), P(), P(), rows,
        ),
        out_specs=(
            rows, rows, P(), cols, vec, cols, cols, vec, units, P(), P(), P(),
            cols, vec, units, P(), P(), P(),
        ),
        check_vma=False,
    )
```

```python
import functools
import math
import jax
import jax.numpy as jnp
from jax import lax
from jax.experimental import pallas as pl
from jax.experimental.pallas import tpu as pltpu
from jax.sharding import PartitionSpec as P

HEAD_DIM = 64
CLIP = 368
BF = jnp.bfloat16
F32 = jnp.float32
SPAN = 8 * 10**9
LONG = 10**12
VMEM_LIMIT = 32 * 1024 * 1024


def nn(a, b):
    return lax.dot_general(a, b, (((1,), (0,)), ((), ())), preferred_element_type=F32)


def nt(a, b):
    return lax.dot_general(a, b, (((1,), (1,)), ((), ())), preferred_element_type=F32)


def tn(a, b):
    return lax.dot_general(a, b, (((0,), (0,)), ((), ())), preferred_element_type=F32)


def whole(shape):
    zeros = (0,) * len(shape)
    return pl.BlockSpec(tuple(shape), lambda i: zeros)


def at_layer(shape, layer):
    rest = (0,) * (len(shape) - 1)
    return pl.BlockSpec((1,) + tuple(shape[1:]), lambda i: (layer,) + rest)


def sds(shape, dtype):
    return jax.ShapeDtypeStruct(shape, dtype)


def kept(shape, dtype):
    return pltpu.HBM(shape, dtype)


class Order:
    def __init__(self):
        self.last = None
        self.span = SPAN
        self.small = True

    def call(self, body, count, args, mark=0, **given):
        anywhere = pl.BlockSpec(memory_space=pl.ANY)
        given["in_specs"] = list(given["in_specs"])
        if self.last is not None:
            given["in_specs"].append(anywhere)
            args = [*args, self.last]
        extra = mark is None
        if extra:
            given["out_specs"] = [*given["out_specs"], anywhere]
            given["out_shape"] = [*given["out_shape"], sds((8, 128), F32)]
        n = len(given["out_shape"])

        def kernel(*refs):
            outs = refs[len(args) : len(args) + n - extra]
            body(*refs[:count], *outs, *refs[len(args) + n :])

        out = pl.pallas_call(kernel, grid=(1,), **given)(*args)
        self.last = out[-1 if extra else mark]
        return out[: n - extra]


ORDER = Order()


def call(kernel, ins, outs, scratch=(), flops=0, name=None, mark=0):
    specs = [
        pl.BlockSpec(memory_space=pltpu.SMEM)
        if l == "smem"
        else whole(a.shape)
        if l is None
        else at_layer(a.shape, l)
        for a, l in ins
    ]
    nbytes = sum(
        (a.size // a.shape[0] if isinstance(l, int) else a.size) * a.dtype.itemsize for a, l in ins
    ) + sum(math.prod(o.shape) * o.dtype.itemsize for o in outs)
    return ORDER.call(
        kernel,
        len(ins),
        [a for a, _ in ins],
        mark=mark,
        in_specs=specs,
        out_specs=[whole(o.shape) for o in outs],
        out_shape=outs,
        scratch_shapes=list(scratch),
        compiler_params=pltpu.CompilerParams(vmem_limit_bytes=VMEM_LIMIT),
        cost_estimate=pl.CostEstimate(
            flops=max(flops, ORDER.span), bytes_accessed=nbytes, transcendentals=0
        ),
        name=name,
    )


def join(a_ref, b_ref, scratch, joined):
    half = a_ref.shape[0]
    scratch[:half] = a_ref[...].astype(F32)
    scratch[half:] = b_ref[...].astype(F32)
    value = scratch[...].astype(BF)
    joined[...] = value
    return value


def arrange(who, pair, scratch, arranged):
    half = pair.shape[0] // 2
    scratch[...] = pair[...].astype(F32)
    at = pl.multiple_of(who[0] * half, 8)
    both = [scratch[pl.ds(at, half), :], scratch[pl.ds(half - at, half), :]]
    value = jnp.concatenate(both, axis=0).astype(BF)
    arranged[...] = value
    return value


def split_out(value, scratch, oa, ob):
    half = oa.shape[0]
    scratch[...] = value
    oa[...] = scratch[:half].astype(BF)
    ob[...] = scratch[half:].astype(BF)


def head_mask(width, head):
    cols = lax.broadcasted_iota(jnp.int32, (1, width), 1)
    return (cols // HEAD_DIM == head).astype(F32)


def soft(k, q, head):
    mask = (head_mask(q.shape[1], head) * HEAD_DIM ** (-0.5)).astype(BF)
    s = nt(k, q * mask)
    e = jnp.exp(s - jnp.max(s, axis=0, keepdims=True))
    return e * (1.0 / jnp.sum(e, axis=0, keepdims=True))


def attn_fwd_kernel(
    xa, xb, wq, wk, wv, wo, bq, bv, pa, pb, xc, qo, ko, vo, kto, cto, scr, *, layer
):
    x = join(xa, xb, scr, xc)
    q = (nt(x, wq[0]) + bq[layer : layer + 1, :].astype(F32)).astype(BF)
    k = nt(x, wk[0]).astype(BF)
    kto[...] = nt(wk[0], x).astype(BF)
    v32 = nt(x, wv[0]) + bv[layer : layer + 1, :].astype(F32)
    v = v32.astype(BF)
    vt = v32.T.astype(BF)
    qo[...] = q
    ko[...] = k
    vo[...] = v
    parts = []
    for h in range(q.shape[1] // HEAD_DIM):
        pt = soft(k, q, h).astype(BF)
        parts.append(nn(vt[h * HEAD_DIM : (h + 1) * HEAD_DIM], pt))
    ct = jnp.concatenate(parts, axis=0).astype(BF)
    cto[...] = ct
    split_out(tn(ct, wo[0]), scr, pa, pb)


def attn_fwd(layer, xa, xb, wq, wk, wv, wo, bq, bv):
    rows, d = 2 * xa.shape[0], xa.shape[1]
    hd = wq.shape[1]
    outs = [
        sds((rows // 2, d), BF),
        sds((rows // 2, d), BF),
        sds((rows, d), BF),
        sds((rows, hd), BF),
        sds((rows, hd), BF),
        sds((rows, hd), BF),
        sds((hd, rows), BF),
        sds((hd, rows), BF),
    ]
    return call(
        functools.partial(attn_fwd_kernel, layer=layer),
        [(xa, None), (xb, None)]
        + [(w, layer) for w in (wq, wk, wv, wo)]
        + [(bq, None), (bv, None)],
        outs,
        [pltpu.VMEM((rows, d), F32)],
        flops=2 * rows * hd * (5 * d + 2 * rows),
        name="attn_fwd",
    )


def attn_bwd_kernel(
    who, b_in, q, k, v, kt, wq, wk, wv, wo, marks, pa, pb, bc, dqt, dk, dv, sbq, sbv, smask, scr
):
    b = arrange(who, b_in, scr, bc)
    cg = nt(b, wo[0]).astype(BF)
    qv, kv, vv, ktv = q[...], k[...], v[...], kt[...]
    width = qv.shape[1]
    scale = HEAD_DIM ** (-0.5)
    dqs = []
    dk32 = jnp.zeros(qv.shape, F32)
    dv32 = jnp.zeros(qv.shape, F32)
    for h in range(width // HEAD_DIM):
        mask = head_mask(width, h)
        p = soft(kv, qv, h)
        dp = nt(vv, cg * mask.astype(BF))
        dsum = jnp.sum(p * dp, axis=0, keepdims=True)
        ds = (p * (dp - dsum)).astype(BF)
        dqs.append(nn(ktv[h * HEAD_DIM : (h + 1) * HEAD_DIM], ds))
        dk32 = dk32 + nn(ds, qv) * (mask * scale)
        dv32 = dv32 + nn(p.astype(BF), cg) * mask
    dqtv = (jnp.concatenate(dqs, axis=0) * scale).astype(BF)
    dkv = dk32.astype(BF)
    dvv = dv32.astype(BF)
    dqt[...] = dqtv
    dk[...] = dkv
    dv[...] = dvv
    sbq[...] = jnp.sum(dqtv.astype(F32).T, axis=0, keepdims=True)
    sbv[...] = jnp.sum(dvv.astype(F32), axis=0, keepdims=True)
    total = tn(dqtv, wq[0]) + nn(dkv, wk[0]) + nn(dvv, wv[0])
    smask[...] = jnp.sum(total * marks[:, :1].astype(F32), axis=0, keepdims=True)
    split_out(total, scr, pa, pb)


def attn_bwd(who, layer, b, q, k, v, kt, marks, wq, wk, wv, wo):
    rows, d = b.shape
    hd = wq.shape[1]
    outs = [
        sds((rows // 2, d), BF),
        sds((rows // 2, d), BF),
        sds((rows, d), BF),
        sds((hd, rows), BF),
        sds((rows, hd), BF),
        sds((rows, hd), BF),
        sds((1, hd), F32),
        sds((1, hd), F32),
        sds((1, d), F32),
    ]
    return call(
        attn_bwd_kernel,
        [(who, "smem"), (b, None), (q, None), (k, None), (v, None), (kt, None)]
        + [(w, layer) for w in (wq, wk, wv, wo)]
        + [(marks, None)],
        outs,
        [pltpu.VMEM((rows, d), F32)],
        flops=2 * rows * hd * (4 * d + 5 * rows),
        name="attn_bwd",
    )


def ffn_fwd_kernel(ya, yb, wu, wd, bu, pa, pb, yc, hid, slo, scr, *, layer):
    pre = nn(join(ya, yb, scr, yc), wu[0]) + bu[layer : layer + 1, :].astype(F32)
    phi = 0.5 * (1.0 + lax.erf(pre * 0.7071067811865476))
    hidden = (pre * phi).astype(BF)
    hid[...] = hidden
    slo[...] = (phi + pre * jnp.exp(-0.5 * pre * pre) * 0.3989422804014327).astype(BF)
    split_out(nn(hidden, wd[0]), scr, pa, pb)


def ffn_fwd(layer, ya, yb, wu, wd, bu):
    rows, d = 2 * ya.shape[0], ya.shape[1]
    ff = wu.shape[2]
    outs = [
        sds((rows // 2, d), BF),
        sds((rows // 2, d), BF),
        sds((rows, d), BF),
        sds((rows, ff), BF),
        sds((rows, ff), BF),
    ]
    return call(
        functools.partial(ffn_fwd_kernel, layer=layer),
        [(ya, None), (yb, None), (wu, layer), (wd, layer), (bu, None)],
        outs,
        [pltpu.VMEM((rows, d), F32)],
        flops=4 * rows * d * ff,
        name="ffn_fwd",
    )


def ffn_bwd_kernel(who, d_in, slo, wu, wd, pa, pb, dc, act_o, sbu, scr):
    act = (nt(arrange(who, d_in, scr, dc), wd[0]) * slo[...].astype(F32)).astype(BF)
    act_o[...] = act
    sbu[...] = jnp.sum(act.astype(F32), axis=0, keepdims=True)
    split_out(nt(act, wu[0]), scr, pa, pb)


def ffn_bwd(who, layer, d_in, slo, wu, wd):
    rows, d = d_in.shape
    ff = wu.shape[2]
    outs = [
        sds((rows // 2, d), BF),
        sds((rows // 2, d), BF),
        sds((rows, d), BF),
        sds((rows, ff), BF),
        sds((1, ff), F32),
    ]
    return call(
        ffn_bwd_kernel,
        [(who, "smem"), (d_in, None), (slo, None), (wu, layer), (wd, layer)],
        outs,
        [pltpu.VMEM((rows, d), F32)],
        flops=4 * rows * d * ff,
        name="ffn_bwd",
    )


def put_halves(bits, pick, scr, send, keep):
    half = keep.shape[0]
    bit = bits[pick]
    keep[...] = scr[pl.ds(pl.multiple_of(bit * half, 16), half), :]
    send[...] = scr[pl.ds(pl.multiple_of((1 - bit) * half, 16), half), :]


def pair_wgrad_kernel(bits, al, ar, bl, br, send, keep, scr, *, pick):
    scr[...] = (tn(al[...], bl[...]) + tn(ar[...], br[...])).astype(BF)
    put_halves(bits, pick, scr, send, keep)


def pair_wgrad(bits, pick, a, b, name):
    rows, m = a[0].shape
    n = b[0].shape[1]
    return call(
        functools.partial(pair_wgrad_kernel, pick=pick),
        [(bits, "smem")] + [(v, None) for v in (*a, *b)],
        [sds((m // 2, n), BF)] * 2,
        [pltpu.VMEM((m, n), BF)],
        flops=4 * rows * m * n,
        name=name,
    )


def attn_wgrad_kernel(
    bits, xl, xr, dqtl, dqtr, dkl, dkr, dvl, dvr, ctl, ctr, bl, br, send, keep, scr, *, pick
):
    hd = scr.shape[0] // 4
    scr[:hd] = (nn(dqtl[...], xl[...]) + nn(dqtr[...], xr[...])).astype(BF)
    scr[hd : 2 * hd] = (tn(dkl[...], xl[...]) + tn(dkr[...], xr[...])).astype(BF)
    scr[2 * hd : 3 * hd] = (tn(dvl[...], xl[...]) + tn(dvr[...], xr[...])).astype(BF)
    scr[3 * hd :] = (nn(ctl[...], bl[...]) + nn(ctr[...], br[...])).astype(BF)
    put_halves(bits, pick, scr, send, keep)


def attn_wgrad(bits, pick, hd, *values):
    rows, dim = values[0].shape
    return call(
        functools.partial(attn_wgrad_kernel, pick=pick),
        [(bits, "smem")] + [(v, None) for v in values],
        [sds((2 * hd, dim), BF)] * 2,
        [pltpu.VMEM((4 * hd, dim), BF)],
        flops=16 * rows * dim * hd,
        name="attn_wgrad",
    )


def attn_wgrad_two_kernel(
    bits, xl, xr, dqtl, dqtr, dkl, dkr, dvl, dvr, ctl, ctr, bl, br, sd, kd, su, ku, sc_d, sc_u
):
    hd = sc_d.shape[0] // 2
    sc_d[:hd] = (nn(dqtl[...], xl[...]) + nn(dqtr[...], xr[...])).astype(BF)
    sc_d[hd:] = (tn(dkl[...], xl[...]) + tn(dkr[...], xr[...])).astype(BF)
    put_halves(bits, 0, sc_d, sd, kd)
    sc_u[:hd] = (tn(dvl[...], xl[...]) + tn(dvr[...], xr[...])).astype(BF)
    sc_u[hd:] = (nn(ctl[...], bl[...]) + nn(ctr[...], br[...])).astype(BF)
    put_halves(bits, 1, sc_u, su, ku)


def attn_wgrad_two(bits, hd, *values):
    rows, dim = values[0].shape
    return call(
        attn_wgrad_two_kernel,
        [(bits, "smem")] + [(v, None) for v in values],
        [sds((hd, dim), BF)] * 4,
        [pltpu.VMEM((2 * hd, dim), BF)] * 2,
        flops=16 * rows * dim * hd,
        name="attn_wgrad",
    )


def place_two_kernel(bits, mine, by_low, by_high, down_far, up_far, *outs):
    size = down_far.shape[0]
    low, high = bits[0], bits[1]
    parts = [
        (low, high, mine, mine),
        (1 - low, high, by_low, by_low),
        (low, 1 - high, by_high, by_high),
        (1 - low, 1 - high, down_far, up_far),
    ]
    for l, h, ref_down, ref_up in parts:

        def put_down(spot, ref=ref_down):
            at = (spot % 2) * size
            outs[spot // 2][0, at : at + size, :] = ref[:size, :].astype(F32)

        def put_up(spot, ref=ref_up):
            at = (spot % 2) * size
            outs[2 + spot // 2][0, at : at + size, :] = ref[ref.shape[0] - size :, :].astype(F32)

        when_at(l, h, put_down)
        when_at(h, l, put_up)


def small_kernel(*refs, layers, hd):
    out = refs[-1]
    width = out.shape[1]
    zeros = jnp.zeros((8, width), F32)
    rows = []
    for l in range(layers):
        sql, sqr, svl, svr, sul, sur, own_a, own_f, sma, smb = refs[10 * l : 10 * l + 10]
        heads = [sql[...] + sqr[...], svl[...] + svr[...], zeros[:1, : width - 2 * hd]]
        mask_row = own_a[3:4] + sma[...] + smb[...] if l == 0 else zeros[:1]
        rows += [own_a[:3], own_f[:3], mask_row, zeros[:1]]
        rows += [jnp.concatenate(heads, axis=1), sul[...] + sur[...], zeros[:6]]
    out[...] = jnp.concatenate(rows, axis=0)


def small_rows(values, hd):
    layers = len(values)
    dim = values[0][6].shape[1]
    return call(
        functools.partial(small_kernel, layers=layers, hd=hd),
        [(v, None) for vs in values for v in vs],
        [sds((16 * layers, dim), F32)],
        name="small_rows",
    )[0]


def small_mp_kernel(have, got, out):
    for l in range(have.shape[0] // 16):
        out[16 * l : 16 * l + 8, :] = have[16 * l : 16 * l + 8, :] + got[16 * l : 16 * l + 8, :]
        out[16 * l + 8 : 16 * l + 16, :] = have[16 * l + 8 : 16 * l + 16, :]


def small_dp_kernel(have, got, out):
    out[...] = have[...] + got[...]


def small_add(have, got, over_mp):
    return call(
        small_mp_kernel if over_mp else small_dp_kernel,
        [(have, None), (got, None)],
        [sds(have.shape, F32)],
        name="small_add",
    )[0]


def small_out_kernel(have, got, bq, bv, bo, ag, ab, bu, bd, fg, fb, mask):
    total = have[...] + got[...]
    hd = bq.shape[1]
    for l in range(bq.shape[0]):
        at = 16 * l
        for out, row in ((ag, 0), (ab, 1), (bo, 2), (fg, 3), (fb, 4), (bd, 5), (bu, 9)):
            out[l : l + 1, :] = total[at + row : at + row + 1, :]
        heads = total[at + 8 : at + 9, :]
        bq[l : l + 1, :] = heads[:, :hd]
        bv[l : l + 1, :] = heads[:, hd : 2 * hd]
    mask[...] = total[6, :]


def small_out(have, got, layers, hd):
    dim = have.shape[1]
    wide = sds((layers, dim), F32)
    return call(
        small_out_kernel,
        [(have, None), (got, None)],
        [sds((layers, hd), F32)] * 2 + [wide] * 7 + [sds((dim,), F32)],
        name="small_out",
    )


def halve_kernel(bits, have, got, send, keep, *, pick):
    half = keep.shape[0]
    bit = bits[pick]
    mine = pl.ds(pl.multiple_of(bit * half, 16), half)
    other = pl.ds(pl.multiple_of((1 - bit) * half, 16), half)
    keep[...] = (have[mine, :].astype(F32) + got[mine, :].astype(F32)).astype(BF)
    send[...] = (have[other, :].astype(F32) + got[other, :].astype(F32)).astype(BF)


def halve(bits, pick, have, got):
    rows, dim = have.shape
    return call(
        functools.partial(halve_kernel, pick=pick),
        [(bits, "smem"), (have, None), (got, None)],
        [sds((rows // 2, dim), BF)] * 2,
        name="halve",
    )


def add_kernel(a, b, o):
    o[...] = (a[...].astype(F32) + b[...].astype(F32)).astype(BF)


def add(a, b):
    return call(add_kernel, [(a, None), (b, None)], [sds(a.shape, BF)], name="add")[0]


def stacked_call(kernel, bits, parts, outs, layer, layers, old, name):
    dim = parts[0].shape[1]
    old = [] if old is None else list(old)
    shapes = [sds((layers, rows, dim), F32) for rows in outs]
    specs = [pl.BlockSpec((1, rows, dim), lambda i: (layer, 0, 0)) for rows in outs]
    n = 1 + len(parts)

    def body(*refs):
        kernel(*refs[:n], *refs[n + len(old) :])

    return ORDER.call(
        body,
        n + len(old),
        [bits, *parts, *old],
        mark=None,
        in_specs=[pl.BlockSpec(memory_space=pltpu.SMEM)]
        + [whole(q.shape) for q in parts]
        + [pl.BlockSpec(memory_space=pl.ANY)] * len(old),
        out_specs=specs,
        out_shape=shapes,
        input_output_aliases={n + i: i for i in range(len(old))},
        compiler_params=pltpu.CompilerParams(vmem_limit_bytes=VMEM_LIMIT),
        cost_estimate=pl.CostEstimate(flops=ORDER.span, bytes_accessed=1, transcendentals=0),
        name=name,
    )


def when_at(first, second, fn):
    for spot in range(4):

        @pl.when(2 * first + second == spot)
        def _(spot=spot):
            fn(spot)


def place_attn_kernel(bits, *refs, picks):
    parts, outs = refs[:4], refs[4:]
    for i, ref in enumerate(parts):
        first = bits[picks[0]] if i < 2 else 1 - bits[picks[0]]
        second = bits[picks[1]] if i % 2 == 0 else 1 - bits[picks[1]]

        def put(spot, ref=ref):
            outs[spot][0] = ref[...].astype(F32)

        when_at(first, second, put)


def place_attn(bits, picks, parts, layer, layers, old):
    return stacked_call(
        functools.partial(place_attn_kernel, picks=picks),
        bits,
        parts,
        [parts[0].shape[0]] * 4,
        layer,
        layers,
        old,
        "place_attn",
    )


def place_ffn_kernel(bits, mine, by_low, by_high, down_far, up_far, down, up):
    size = down_far.shape[0]
    low, high = bits[0], bits[1]
    parts = [
        (low, high, mine, mine),
        (1 - low, high, by_low, by_low),
        (low, 1 - high, by_high, by_high),
        (1 - low, 1 - high, down_far, up_far),
    ]
    for l, h, ref_down, ref_up in parts:

        def put_down(spot, ref=ref_down):
            down[0, spot * size : (spot + 1) * size, :] = ref[:size, :].astype(F32)

        def put_up(spot, ref=ref_up):
            up[0, spot * size : (spot + 1) * size, :] = ref[ref.shape[0] - size :, :].astype(F32)

        when_at(l, h, put_down)
        when_at(h, l, put_up)


def place_ffn(bits, parts, layer, layers, old):
    rows = 4 * parts[3].shape[0]
    return stacked_call(
        place_ffn_kernel, bits, parts, [rows] * 2, layer, layers, old, "place_ffn"
    )


def halve_two_kernel(bits, kd, gd, ku, gu, send_d, send_u, keep):
    size = send_d.shape[0]
    for have, got, send, pick, at in ((kd, gd, send_d, 1, 0), (ku, gu, send_u, 0, size)):
        bit = bits[pick]
        mine = pl.ds(pl.multiple_of(bit * size, 16), size)
        other = pl.ds(pl.multiple_of((1 - bit) * size, 16), size)
        keep[at : at + size, :] = (have[mine, :].astype(F32) + got[mine, :].astype(F32)).astype(BF)
        send[...] = (have[other, :].astype(F32) + got[other, :].astype(F32)).astype(BF)


def halve_two(bits, kd, gd, ku, gu):
    rows, dim = kd.shape
    return call(
        halve_two_kernel,
        [(bits, "smem"), (kd, None), (gd, None), (ku, None), (gu, None)],
        [sds((rows // 2, dim), BF), sds((rows // 2, dim), BF), sds((rows, dim), BF)],
        name="halve_two",
    )


def add_two_kernel(have, gd, gu, out):
    size = gd.shape[0]
    out[:size, :] = (have[:size, :].astype(F32) + gd[...].astype(F32)).astype(BF)
    out[size:, :] = (have[size:, :].astype(F32) + gu[...].astype(F32)).astype(BF)


def add_two(have, gd, gu):
    return call(
        add_two_kernel, [(have, None), (gd, None), (gu, None)], [sds(have.shape, BF)], name="add_two"
    )[0]


def cut_two_kernel(by_high, by_low, od, ou):
    size = od.shape[0]
    od[...] = by_high[:size, :]
    ou[...] = by_low[size:, :]


def cut_two(by_high, by_low):
    rows, dim = by_high.shape
    return call(
        cut_two_kernel,
        [(by_high, None), (by_low, None)],
        [sds((rows // 2, dim), BF)] * 2,
        name="cut_two",
    )


def swap_bit(v, size, pick):
    return lax.ppermute(v, "dp", [(i, i ^ (1 << pick)) for i in range(size)])


def copy_kernel(have, out):
    out[...] = have[...]


def gate(v):
    return call(copy_kernel, [(v, None)], [sds(v.shape, v.dtype)], name="gate")[0]


def merge_kernel(ffn, have, got, out):
    size = ffn.shape[0]
    out[:size, :] = ffn[...]
    out[size:, :] = (have[...].astype(F32) + got[...].astype(F32)).astype(BF)


def cut_merged_kernel(by_high, by_low, od, ou):
    size = ou.shape[0]
    od[:size, :] = by_high[:size, :]
    od[size:, :] = by_high[2 * size :, :]
    ou[...] = by_low[size : 2 * size, :]


def place_merged_kernel(bits, mine, by_low, by_high, down_far, up_far, down, up, *heads):
    size = up_far.shape[0]
    low, high = bits[0], bits[1]
    parts = [
        (low, high, mine, mine, mine, 2),
        (1 - low, high, by_low, by_low, by_low, 2),
        (low, 1 - high, by_high, by_high, by_high, 2),
        (1 - low, 1 - high, down_far, up_far, down_far, 1),
    ]
    for l, h, ref_down, ref_up, ref_head, at in parts:

        def put_down(spot, ref=ref_down, head=ref_head, at=at):
            down[0, spot * size : (spot + 1) * size, :] = ref[:size, :].astype(F32)
            heads[spot][0] = head[at * size : (at + 1) * size, :].astype(F32)

        def put_up(spot, ref=ref_up, at=at):
            up[0, spot * size : (spot + 1) * size, :] = ref[
                (at - 1) * size : at * size, :
            ].astype(F32)

        when_at(l, h, put_down)
        when_at(h, l, put_up)


class Merged:
    def __init__(self, ffn, attn):
        self.ffn, self.attn = ffn, attn

    def merge(self):
        ffn, attn = self.ffn, self.attn
        for i in range(len(attn.rest) - 1):
            attn.keep = add(attn.keep, attn.got)
            attn.got = attn.swap(attn.keep, attn.rest[i + 1])
        have, got = attn.keep, attn.got
        rows = ffn.keep.shape[0] + have.shape[0]
        self.keep = call(
            merge_kernel,
            [(ffn.keep, None), (have, None), (got, None)],
            [sds((rows, have.shape[1]), BF)],
            name="merge",
        )[0]
        self.by_high = ffn.swap(self.keep, 1)
        if self.whole:
            self.by_low = ffn.swap(self.keep, 0)

    whole = False

    def low(self):
        self.by_low = self.ffn.swap(gate(self.keep), 0)

    def cut(self):
        rows, dim = self.keep.shape
        od, ou = call(
            cut_merged_kernel,
            [(self.by_high, None), (self.by_low, None)],
            [sds((2 * rows // 3, dim), BF), sds((rows // 3, dim), BF)],
            name="cut_merged",
        )
        self.down_far = self.ffn.swap(od, 0)
        self.up_far = self.ffn.swap(ou, 1)

    def place(self, bits, layer, layers):
        size = self.up_far.shape[0]
        parts = self.keep, self.by_low, self.by_high, self.down_far, self.up_far
        outs = [4 * size] * 2 + [size] * 4
        got = stacked_call(
            place_merged_kernel, bits, parts, outs, layer, layers, None, "place_merged"
        )
        return got[:2], got[2:]


class DpSum:
    def __init__(self, bits, size, picks):
        self.bits, self.size, self.picks = bits, size, picks
        self.rest = [p for p in range(size.bit_length() - 1) if p not in picks]

    def swap(self, v, pick):
        return swap_bit(v, self.size, pick)

    def start(self, fn, *values):
        send, self.keep = fn(self.bits, self.picks[0], *values)
        self.got = self.swap(send, self.picks[0])

    def halve(self):
        send, self.keep = halve(self.bits, self.picks[1], self.keep, self.got)
        self.got = self.swap(send, self.picks[1])

    def cross(self):
        self.keep = add(self.keep, self.got)
        if self.rest:
            self.got = self.swap(self.keep, self.rest[0])

    def total(self):
        for i in range(len(self.rest)):
            self.keep = add(self.keep, self.got)
            if i + 1 < len(self.rest):
                self.got = self.swap(self.keep, self.rest[i + 1])

    def hold(self):
        self.keep = gate(self.keep)

    def spread(self):
        self.near = self.swap(self.keep, self.picks[1])
        self.far = self.swap(self.keep, self.picks[0])

    def last(self):
        self.end = self.swap(gate(self.near), self.picks[0])

    def parts(self):
        return self.keep, self.near, self.far, self.end


class FfnSum:
    def __init__(self, bits, size):
        self.bits, self.size = bits, size
        self.rest = range(2, size.bit_length() - 1)

    def swap(self, v, pick):
        return swap_bit(v, self.size, pick)

    def start(self, down, up):
        send, self.kd = pair_wgrad(self.bits, 0, down[:2], down[2:], "down_wgrad")
        self.gd = self.swap(send, 0)
        send, self.ku = pair_wgrad(self.bits, 1, up[:2], up[2:], "up_wgrad")
        self.gu = self.swap(send, 1)

    def halve(self):
        send_d, send_u, self.keep = halve_two(self.bits, self.kd, self.gd, self.ku, self.gu)
        self.gd = self.swap(send_d, 1)
        self.gu = self.swap(send_u, 0)

    def cross(self):
        self.keep = add_two(self.keep, self.gd, self.gu)
        if self.rest:
            self.got = self.swap(self.keep, self.rest[0])

    def total(self):
        for i in range(len(self.rest)):
            self.keep = add(self.keep, self.got)
            if i + 1 < len(self.rest):
                self.got = self.swap(self.keep, self.rest[i + 1])

    def hold(self):
        self.keep = gate(self.keep)

    def high(self):
        self.by_high = self.swap(self.keep, 1)

    def low(self):
        self.by_low = self.swap(self.keep, 0)

    def last(self):
        od, ou = cut_two(self.by_high, self.by_low)
        self.down_far = self.swap(od, 0)
        self.up_far = self.swap(ou, 1)

    def parts(self):
        return self.keep, self.by_low, self.by_high, self.down_far, self.up_far


class AttnSum(FfnSum):
    def start(self, fn, *values):
        sd, self.kd, su, self.ku = attn_wgrad_two(self.bits, values[0], *values[1:])
        self.gd = self.swap(sd, 0)
        self.gu = self.swap(su, 1)

    def place(self, layer, layers, old):
        parts = self.parts()
        rows = 2 * parts[3].shape[0]
        return stacked_call(
            place_two_kernel, self.bits, parts, [rows] * 4, layer, layers, old, "place_attn"
        )


def three(who, mine, pair, far):
    half = mine.shape[0]
    if pair.shape[0] == half:
        near = pair[...].astype(F32)
    else:
        near = jnp.where(who[0] == 0, pair[half:, :].astype(F32), pair[:half, :].astype(F32))
    return mine[...].astype(F32) + near + far[...].astype(F32)


def norm_fwd_kernel(near, far, res, bias, gain, shift, out, unit, inv, low, *, layer):
    row = slice(layer, layer + 1)
    r = res[...] + (near[...] + far[...].astype(F32)) + bias[row, :].astype(F32)
    mean = jnp.mean(r, axis=-1, keepdims=True)
    c = r - mean
    i = lax.rsqrt(jnp.mean(c * c, axis=-1, keepdims=True) + 1e-05)
    u = c * i
    o = u * gain[row, :].astype(F32) + shift[row, :].astype(F32)
    out[...] = o
    unit[...] = u
    inv[...] = i
    low[...] = o.astype(BF)


def norm_fwd(layer, parts, res, bias, gain, shift):
    rows, d = res.shape
    return call(
        functools.partial(norm_fwd_kernel, layer=layer),
        [(v, None) for v in (*parts, res, bias, gain, shift)],
        [sds((rows, d), F32), sds((rows, d), F32), sds((rows, 1), F32), sds((rows, d), BF)],
        name="norm_fwd",
        mark=3,
    )


def norm_bwd_core(up, unit, inv, gain, marks, resid, low, sums, layer):
    u = unit[...]
    e = up * gain[layer : layer + 1, :].astype(F32)
    r = inv[...] * (
        e - jnp.mean(e, axis=-1, keepdims=True) - u * jnp.mean(e * u, axis=-1, keepdims=True)
    )
    resid[...] = r
    lo = r.astype(BF)
    low[...] = lo
    sums[0:1, :] = jnp.sum(up * u, axis=0, keepdims=True)
    sums[1:2, :] = jnp.sum(up, axis=0, keepdims=True)
    sums[2:3, :] = jnp.sum(lo.astype(F32), axis=0, keepdims=True)
    sums[3:4, :] = jnp.sum(r * marks[...], axis=0, keepdims=True)


def norm_bwd_first_kernel(og, unit, inv, gain, marks, resid, low, sums, *, layer):
    up = og[...].astype(F32) * marks[...]
    norm_bwd_core(up, unit, inv, gain, marks, resid, low, sums, layer)


def norm_bwd_kernel(who, p0, p1, p2, res, unit, inv, gain, marks, resid, low, sums, *, layer):
    up = res[...] + three(who, p0, p1, p2)
    norm_bwd_core(up, unit, inv, gain, marks, resid, low, sums, layer)


def norm_bwd(who, layer, ins, unit, inv, gain, marks):
    rows, d = unit.shape
    first = len(ins) == 1
    return call(
        functools.partial(norm_bwd_first_kernel if first else norm_bwd_kernel, layer=layer),
        ([] if first else [(who, "smem")])
        + [(v, None) for v in (*ins, unit, inv, gain, marks)],
        [sds((rows, d), F32), sds((rows, d), BF), sds((4, d), F32)],
        name="norm_bwd",
        mark=1,
    )


def turn_kernel(near, far, res, bias, gain, shift, og, marks, hidden, resid, low, sums, *, layer):
    row = slice(layer, layer + 1)
    r = res[...] + (near[...] + far[...].astype(F32)) + bias[row, :].astype(F32)
    c = r - jnp.mean(r, axis=-1, keepdims=True)
    inv = lax.rsqrt(jnp.mean(c * c, axis=-1, keepdims=True) + 1e-05)
    unit = c * inv
    hidden[...] = (unit * gain[row, :].astype(F32) + shift[row, :].astype(F32)).astype(BF)
    up = og[...].astype(F32) * marks[...]
    norm_bwd_core(up, unit, inv, gain, marks, resid, low, sums, layer)


def norm_turn(layer, parts, res, bias, gain, shift, out_grad, marks):
    rows, d = res.shape
    return call(
        functools.partial(turn_kernel, layer=layer),
        [(v, None) for v in (*parts, res, bias, gain, shift, out_grad, marks)],
        [sds((rows, d), BF), sds((rows, d), F32), sds((rows, d), BF), sds((4, d), F32)],
        name="norm_turn",
        mark=2,
    )


def last_kernel(who, p0, p1, p2, res, marks, out):
    out[...] = (res[...] + three(who, p0, p1, p2)) * (1.0 - marks[...])


def last_rows(who, parts, res, marks):
    return call(
        last_kernel,
        [(who, "smem")] + [(v, None) for v in (*parts, res, marks)],
        [sds(res.shape, F32)],
        name="last_rows",
        mark=None,
    )[0]


FFN, ATTN, BOTH, SMALL, ROWS = range(5)
ATTN_PICKS = (0, 1)
PLAN = {
    ("ffn_far", False): [(0, FFN, "start")],
    ("attn_near", False): [(0, FFN, "halve")],
    ("attn_far", False): [(0, ATTN, "start"), (0, FFN, "cross")],
    ("ffn_near", True): [(1, ATTN, "halve")],
    ("ffn_far", True): [(0, FFN, "start"), (1, ATTN, "cross"), (1, FFN, "total")],
    ("attn_near", True): [(0, FFN, "halve"), (1, BOTH, "merge")],
    ("attn_mid", True): [(0, FFN, "cross")],
    ("attn_far", True): [(0, ATTN, "start")],
}
TAIL = [
    (0, ROWS, ""),
    (0, SMALL, ""),
    (1, BOTH, "low"),
    (0, ATTN, "halve"),
    (0, SMALL, ""),
    (0, FFN, "total"),
    (0, FFN, "high"),
    (0, FFN, "low"),
    (0, ATTN, "cross"),
    (0, SMALL, ""),
    (1, BOTH, "cut"),
    (0, SMALL, ""),
    (0, ATTN, "total"),
    (0, ATTN, "spread"),
    (0, SMALL, ""),
    (0, FFN, "last"),
    (1, BOTH, "place"),
    (0, SMALL, ""),
    (0, ATTN, "last"),
    (0, FFN, "place"),
    (0, ATTN, "place"),
]
CORE = [(0, 1), (1, 0), (2, 3), (3, 2)]
CHIP = [(0, 2), (2, 0), (1, 3), (3, 1)]


def core(v):
    return lax.ppermute(v, "mp", CORE)


def chip(v):
    return lax.ppermute(v, "mp", CHIP)


def both_cores(v):
    return lax.all_gather(v, "mp", axis=0, tiled=True, axis_index_groups=[[0, 1], [2, 3]])


def join_kernel(who, mine, pair, out):
    half = mine.shape[0]
    theirs = jnp.where(who[0] == 0, pair[half:, :].astype(F32), pair[:half, :].astype(F32))
    out[...] = (mine[...].astype(F32) + theirs).astype(BF)


def gather_sum(who, local, remote):
    joined = call(
        join_kernel,
        [(who, "smem"), (remote[0], None), (both_cores(remote[1]), None)],
        [sds(remote[0].shape, BF)],
        name="join",
    )[0]
    return local[0], both_cores(local[1]), chip(joined)


def prep_kernel(frames, span, vector, stream, low, marks, wide):
    m = jnp.broadcast_to(span[...].astype(F32), (8, span.shape[1])).T[:, :1]
    value = frames[...].astype(F32) * (1.0 - m) + m * vector[...].astype(F32)
    stream[...] = value
    low[...] = value.astype(BF)
    marks[...] = m
    wide[...] = jnp.broadcast_to(m, wide.shape).astype(BF)


def prep(frames, span, vector):
    rows = frames.shape[0]
    return call(
        prep_kernel,
        [(frames, None), (span, None), (vector, None)],
        [sds(frames.shape, F32), sds(frames.shape, BF), sds((rows, 1), F32), sds((rows, 128), BF)],
        name="prep",
        mark=1,
    )


def pair_kernel(a, b, out):
    both = [a[...].astype(F32), b[...].astype(F32)]
    out[...] = jnp.concatenate(both, axis=0).astype(out.dtype)


def pair_rows(a, b):
    shape = (2 * a.shape[0], a.shape[1])
    return call(pair_kernel, [(a, None), (b, None)], [sds(shape, a.dtype)], name="pair_rows")[0]


def plus_kernel(a, b, out):
    out[...] = (a[...].astype(F32) + b[...].astype(F32)).astype(out.dtype)


def plus(a, b, dtype):
    return call(plus_kernel, [(a, None), (b, None)], [sds(a.shape, dtype)], name="plus")[0]


def per_device(
    frames,
    span_mask,
    mask_vector,
    w_query,
    b_query,
    w_key,
    w_value,
    b_value,
    w_out,
    b_out,
    attn_gain,
    attn_bias,
    w_up,
    b_up,
    w_down,
    b_down,
    ffn_gain,
    ffn_bias,
    out_grad,
):
    layers = w_query.shape[0]
    dim = frames.shape[1]
    size = lax.axis_size("dp")
    place_in_dp = lax.axis_index("dp")
    who = (lax.axis_index("mp") & 1).astype(jnp.int32)[None]
    bits = jnp.stack([(place_in_dp >> k) & 1 for k in range(size.bit_length() - 1)]).astype(jnp.int32)
    wq = jnp.swapaxes(w_query, 1, 2)
    wk = jnp.swapaxes(w_key, 1, 2)
    wv = jnp.swapaxes(w_value, 1, 2)
    ORDER.last, ORDER.span, ORDER.small = None, 2 * 10**10, True
    stream, low, marks, mark_rows = prep(frames, span_mask[None], mask_vector[None])
    records = []

    def both(fn, v, extra, jobs=None, later=None, light=False):
        far = chip(v)
        near = both_cores(gate(v))
        first = fn(near, *extra[0])
        if jobs:
            jobs()
        far = both_cores(far)
        if later and light:
            ORDER.span = 0
        second = fn(far, *extra[1])
        ORDER.span = SPAN
        if later:
            later()
        return [first, second]

    def forward(fn, v, marked=None):
        far = chip(v)
        first = fn(v, core(v))
        if marked is not None:
            mark_sides.extend(pair_rows(v, core(v)) for v in (marked, chip(marked)))
        near_sum = plus(first[0], core(first[1]), F32)
        second = fn(far, core(far))
        far_sum = chip(plus(second[0], core(second[1]), BF))
        return (near_sum, far_sum), [first[2:], second[2:]]

    mark_sides = []
    for l in range(layers):
        parts, att = forward(
            lambda *v: attn_fwd(l, *v, wq, wk, wv, w_out, b_query, b_value),
            low,
            None if l else mark_rows,
        )
        normed, unit_a, inv_a, low_a = norm_fwd(l, parts, stream, b_out, attn_gain, attn_bias)
        parts, ffn = forward(lambda *v: ffn_fwd(l, *v, w_up, w_down, b_up), low_a)
        if l < layers - 1:
            stream, unit_f, inv_f, low = norm_fwd(l, parts, normed, b_down, ffn_gain, ffn_bias)
        else:
            hidden_out, *turned = norm_turn(
                l, parts, normed, b_down, ffn_gain, ffn_bias, out_grad, marks
            )
            unit_f = inv_f = None
        records.append((att, ffn, unit_a, inv_a, unit_f, inv_f))
    ORDER.span, ORDER.small = SPAN, True
    sums = [None] * layers
    smalls = [None] * layers
    ins = None
    for l in reversed(range(layers)):
        att, ffn, unit_a, inv_a, unit_f, inv_f = records[l]
        sums[l] = [FfnSum(bits, size), DpSum(bits, size, ATTN_PICKS)]
        sums[l].append(Merged(*sums[l]))
        inputs = [None, None]

        def window(name):
            for ahead, which, step in PLAN.get((name, l == 0), ()):
                if l + ahead < layers:
                    group = sums[l + ahead][which]
                    if step == "start":
                        group.start(*inputs[which])
                    else:
                        getattr(group, step)()

        if l == layers - 1:
            resid_f, low_f, sums_f = turned
        else:
            resid_f, low_f, sums_f = norm_bwd(who, l, ins, unit_f, inv_f, ffn_gain, marks)
        back = both(
            lambda v, c: ffn_bwd(who, l, v, c, w_up, w_down),
            low_f,
            [(f[2],) for f in ffn],
            lambda: window("ffn_near"),
            lambda: window("ffn_mid"),
        )
        parts = gather_sum(who, back[0][:2], back[1][:2])
        inputs[FFN] = (
            [f[1] for f in ffn] + [b[2] for b in back],
            [f[0] for f in ffn] + [b[3] for b in back],
        )
        window("ffn_far")
        s_up = [b[4] for b in back]
        resid_a, low_a, sums_a = norm_bwd(
            who, l, (*parts, resid_f), unit_a, inv_a, attn_gain, marks
        )
        back = both(
            lambda v, *c: attn_bwd(who, l, v, *c, wq, wk, wv, w_out),
            low_a,
            [(*a[1:5], m) for a, m in zip(att, mark_sides)],
            lambda: window("attn_near"),
            lambda: window("attn_mid"),
            l == 0,
        )
        parts = gather_sum(who, back[0][:2], back[1][:2])
        values = [a[0] for a in att]
        for i in (3, 4, 5):
            values += [b[i] for b in back]
        values += [a[5] for a in att]
        values += [b[2] for b in back]
        smalls[l] = [b[i] for i in (6, 7) for b in back] + s_up
        smalls[l] += [sums_a, sums_f] + [b[8] for b in back]
        inputs[ATTN] = (
            lambda bi, p, *v: attn_wgrad(bi, p, wq.shape[1], *v),
            *values,
        )
        ORDER.span = 2 * SPAN if l == 0 else SPAN
        window("attn_far")
        ins = (*parts, resid_a)
    g_att = g_ffn = None
    hd = wq.shape[1]
    held = []
    small_steps = iter([core, chip] + [
        functools.partial(swap_bit, size=size, pick=k) for k in range(size.bit_length() - 1)
    ])

    def small_step():
        if len(held) == 3:
            return
        if not held:
            small = small_rows(smalls, hd)
        else:
            small = None
        step = next(small_steps, None)
        if step is None:
            held.append(small_out(*held, layers, hd))
            return
        if small is None:
            small = small_add(*held, held_mp[0] > 0)
            held_mp[0] -= 1
        held[:] = [small, step(small)]

    held_mp = [2]
    for ahead, which, step in TAIL:
        if ahead >= layers:
            continue
        if which == ROWS:
            frames_grad = last_rows(who, ins[:3], ins[3], marks)
            continue
        if which == SMALL:
            small_step()
            continue
        group = sums[ahead][which]
        if step != "place":
            getattr(group, step)()
        elif which == BOTH:
            g_ffn, g_att = group.place(bits, ahead, layers)
        elif which == FFN:
            g_ffn = place_ffn(bits, group.parts(), ahead, layers, g_ffn)
        else:
            g_att = place_attn(bits, ATTN_PICKS, group.parts(), ahead, layers, g_att)
    while len(held) < 3:
        small_step()
    bq, bv, bo, ag, ab, bu, bd, fg, fb, mask = held[2]
    g_down, g_up = g_ffn

    def swapped(i):
        return jnp.swapaxes(g_att[i], 1, 2)

    return (
        hidden_out,
        frames_grad,
        mask,
        swapped(0),
        bq,
        swapped(1),
        swapped(2),
        bv,
        g_att[3],
        bo,
        ag,
        ab,
        g_up,
        bu,
        g_down,
        bd,
        fg,
        fb,
    )


def solution(mesh):
    rows = P(("dp", "mp"), None)
    cols = P(None, None, "mp")
    units = P(None, "mp", None)
    vec = P(None, "mp")
    return jax.shard_map(
        per_device,
        mesh=mesh,
        in_specs=(
            rows, P(("dp", "mp")), P(), cols, vec, cols, cols, vec, units, P(), P(), P(),
            cols, vec, units, P(), P(), P(), rows,
        ),
        out_specs=(
            rows, rows, P(), cols, vec, cols, cols, vec, units, P(), P(), P(),
            cols, vec, units, P(), P(), P(),
        ),
        check_vma=False,
    )
```
